256 devices in a mesh: seq: 64 (over x, z_lo, y), rep: 4 (over z_hi, core).
Axes of the slice: x: 4, y: 4, z: 8 (z_hi: 2, z_lo: 4; z = z_hi * 4 + z_lo), core: 2. Of those that a mesh axis runs over, the one named last changes fastest.
Arguments:
- query: bfloat16 [65536, 1024], P('seq', 'rep'), parts along dimension 1
- keys: bfloat16 [65536, 1024], P('seq', 'rep'), parts along dimension 1
- values: bfloat16 [65536, 1024], P('seq', 'rep'), parts along dimension 1, may hold values from -6 to 6
- grad_out: bfloat16 [65536, 1024], P('seq', 'rep'), parts along dimension 1, may hold values from -48 to 48
- offsets: int32 [3, 8], P(None, 'rep'), parts along dimension 1, may hold values from 0 to 127, as said below
Outputs:
- attended: float32 [65536, 1024], P('seq', 'rep'), parts along dimension 1
- grad_query: float32 [65536, 1024], P('seq', 'rep'), parts along dimension 1
- grad_keys: float32 [65536, 1024], P('seq', 'rep'), parts along dimension 1
- grad_values: float32 [65536, 1024], P('seq', 'rep'), parts along dimension 1
The draws below stay inside these ranges and needn't reach their ends.
There are 4 independent parts, one for each index of `rep`. The reference program is written for one: setup_inputs(seed, part) draws one part's arguments, and reference() takes and returns one part's arrays. A program takes and returns all parts, laid end to end along the dimension named above; each array names one. Nothing has to cross between parts.
Inputs may be any that keep to these rules, and one draw needn't show every extreme that they name: offsets[l, h] lies in 0 to r - 1 for the dilation r of level l + 1 (8, 32, 128); at level 3 some head has offset 128 - 1, and at level 1 some head has offset 0.
All inputs are finite; a program needn't handle non-finite values.
Results may differ from the reference program's by a relative error of at most 0.0062.
The reference program's roundings to bfloat16 on the way (of `weights`, `grad_low` and `probs_low`) count: a program that leaves them out, or rounds other values in their place, can miss the bound.
Values may be sent and summed in bfloat16 or wider, within the bound.
A program may use at most 128 MiB of HBM per device.

```python
import jax
import jax.numpy as jnp
from jax import lax

HEADS = 2
HEAD_DIM = 128
KEYS = 512
SEQ = 65536
RATE1 = 8
RATE2 = 32
RATE3 = 128


def draw_query(key, part):
    key = jax.random.fold_in(key, 1)
    drawn = jnp.clip(1.4 * jax.random.normal(key, (SEQ, HEADS * HEAD_DIM), jnp.float32), -8.0, 8.0)
    return drawn.astype(jnp.bfloat16)


def draw_keys(key, part):
    key = jax.random.fold_in(key, 2)
    drawn = jnp.clip(1.4 * jax.random.normal(key, (SEQ, HEADS * HEAD_DIM), jnp.float32), -8.0, 8.0)
    return drawn.astype(jnp.bfloat16)


def draw_offsets(key, part):
    key = jax.random.fold_in(key, 3)
    rows_list = []
    for level_number, dilation in enumerate((RATE1, RATE2, RATE3)):
        level_key = jax.random.fold_in(key, level_number)
        drawn = jax.random.randint(level_key, (HEADS,), 0, dilation, jnp.int32)
        chosen = jax.random.randint(jax.random.fold_in(level_key, 11), (), 0, HEADS, jnp.int32)
        marked = jnp.arange(HEADS, dtype=jnp.int32) == chosen
        if level_number == 0:
            drawn = jnp.where(marked, jnp.zeros((HEADS,), jnp.int32), drawn)
        if level_number == 2:
            drawn = jnp.where(marked, jnp.full((HEADS,), dilation - 1, jnp.int32), drawn)
        rows_list.append(drawn)
    return jnp.stack(rows_list).astype(jnp.int32)


def levels(stream_key, shape, shards, least, top_value):
    def one(dim, parts):
        steps = jax.random.uniform(jax.random.fold_in(jax.random.fold_in(stream_key, 6), dim), (parts,), jnp.float32, least / len(shards), top_value / len(shards))
        return jnp.repeat(jnp.exp(steps), shape[dim] // parts).reshape((-1,) + (1,) * (len(shape) - dim - 1))

    level = one(*shards[0])
    for cut in shards[1:]:
        level = level * one(*cut)
    return level


def gaussian(rng, dims, deviation, most, cuts=(), held_as=jnp.bfloat16):
    level = levels(rng, dims, cuts, -0.22, 0.18) if cuts else 1.0
    entries = jax.random.normal(rng, dims, jnp.float32) * deviation * level
    return jnp.minimum(jnp.maximum(entries, -most), most).astype(held_as)


def setup_inputs(seed: int = 0, part: int = 0) -> dict:
    seeds = jax.random.split(jax.random.key(seed), 6)
    part_splits = jax.random.split(jax.random.fold_in(seeds[5], part), 6)
    query = draw_query(jax.random.fold_in(jax.random.fold_in(seeds[5], part), 71), part)
    keys = draw_keys(jax.random.fold_in(jax.random.fold_in(seeds[5], part), 71), part)
    values = gaussian(part_splits[2], (SEQ, HEADS * HEAD_DIM), 1.0, 6.0, ((0, 64),))
    grad_out = gaussian(part_splits[3], (SEQ, HEADS * HEAD_DIM), 8.0, 48.0, ((0, 64),))
    offsets = draw_offsets(jax.random.fold_in(jax.random.fold_in(seeds[5], part), 71), part)
    return dict(query=query, keys=keys, values=values, grad_out=grad_out, offsets=offsets)


def dilate(source, dilation, offsets_row):
    row_count = source.shape[0] // dilation
    folded = source.reshape((row_count, dilation) + source.shape[1:])
    columns = [lax.dynamic_index_in_dim(folded[:, :, head], offsets_row[head], 1, keepdims=False) for head in range(source.shape[1])]
    return jnp.stack(columns, 1)


def spread(dilated, dilation, offsets_row):
    row_count, head_count = dilated.shape[0], dilated.shape[1]
    selector = (jnp.arange(dilation, dtype=jnp.int32)[:, None] == offsets_row[None, :]).astype(dilated.dtype)
    selector = selector.reshape((1, dilation, head_count) + (1,) * (dilated.ndim - 2))
    return (dilated[:, None] * selector).reshape((row_count * dilation,) + dilated.shape[1:])


def spread_max(row_max, dilation, offsets_row):
    row_count, head_count = row_max.shape
    member_mask = jnp.arange(dilation, dtype=jnp.int32)[:, None] == offsets_row[None, :]
    member_mask = jnp.broadcast_to(member_mask[None], (row_count, dilation, head_count)).reshape(row_count * dilation, head_count)
    broad = jnp.broadcast_to(row_max[:, None], (row_count, dilation, head_count)).reshape(row_count * dilation, head_count)
    return jnp.where(member_mask, broad, -jnp.inf)


def attend_block(query_rows, key_rows, value_rows):
    factor = HEAD_DIM ** -0.5
    scores = jnp.einsum('qhd,khd->hqk', query_rows.astype(jnp.float32), key_rows.astype(jnp.float32)) * factor
    row_max = jnp.max(scores, -1)
    powers = jnp.exp(scores - row_max[..., None])
    total = jnp.sum(powers, -1)
    weights = lax.optimization_barrier(powers.astype(jnp.bfloat16)).astype(jnp.float32)
    weighted = jnp.einsum('hqk,khd->qhd', weights, value_rows.astype(jnp.float32))
    return row_max.T, total.T, weighted


def grad_block(query_rows, key_rows, value_rows, dout_rows, log_rows, delta_rows):
    factor = HEAD_DIM ** -0.5
    scores = jnp.einsum('qhd,khd->hqk', query_rows.astype(jnp.float32), key_rows.astype(jnp.float32)) * factor
    probs = jnp.exp(scores - log_rows.T[:, :, None])
    grad_probs = jnp.einsum('qhd,khd->hqk', dout_rows.astype(jnp.float32), value_rows.astype(jnp.float32))
    grad_scores = probs * (grad_probs - delta_rows.T[:, :, None])
    grad_low = lax.optimization_barrier(grad_scores.astype(jnp.bfloat16)).astype(jnp.float32)
    probs_low = lax.optimization_barrier(probs.astype(jnp.bfloat16)).astype(jnp.float32)
    grad_q = factor * jnp.einsum('hqk,khd->qhd', grad_low, key_rows.astype(jnp.float32))
    grad_k = factor * jnp.einsum('hqk,qhd->khd', grad_low, query_rows.astype(jnp.float32))
    grad_v = jnp.einsum('hqk,qhd->khd', probs_low, dout_rows.astype(jnp.float32))
    return grad_q, grad_k, grad_v


def by_segments(function, arrays):
    blocked = tuple(item.reshape((-1, KEYS) + item.shape[1:]) for item in arrays)
    results = lax.map(lambda blocks: function(*blocks), blocked)
    return tuple(item.reshape((-1,) + item.shape[2:]) for item in results)


def reference(query, keys, values, grad_out, offsets):
    shape3 = (SEQ, HEADS, HEAD_DIM)
    query3 = query.reshape(shape3)
    keys3 = keys.reshape(shape3)
    values3 = values.reshape(shape3)
    dout3 = grad_out.reshape(shape3)
    plans = [(1, jnp.zeros((HEADS,), jnp.int32)), (RATE1, offsets[0]), (RATE2, offsets[1]), (RATE3, offsets[2])]
    maxima = []
    totals = []
    weighted_list = []
    for dilation, offsets_row in plans:
        row_max, total, weighted = by_segments(attend_block, (dilate(query3, dilation, offsets_row), dilate(keys3, dilation, offsets_row), dilate(values3, dilation, offsets_row)))
        maxima.append(spread_max(row_max, dilation, offsets_row))
        totals.append(spread(total, dilation, offsets_row))
        weighted_list.append(spread(weighted, dilation, offsets_row))
    peak = maxima[0]
    for item in maxima[1:]:
        peak = jnp.maximum(peak, item)
    factors = [jnp.exp(item - peak) for item in maxima]
    denominator = factors[0] * totals[0]
    numerator = factors[0][..., None] * weighted_list[0]
    for level in range(1, 4):
        denominator = denominator + factors[level] * totals[level]
        numerator = numerator + factors[level][..., None] * weighted_list[level]
    attended = numerator / denominator[..., None]
    log_total = peak + jnp.log(denominator)
    delta = jnp.sum(dout3.astype(jnp.float32) * attended, -1)
    grad_q = jnp.zeros(shape3, jnp.float32)
    grad_k = jnp.zeros(shape3, jnp.float32)
    grad_v = jnp.zeros(shape3, jnp.float32)
    for dilation, offsets_row in plans:
        pieces = by_segments(grad_block, (dilate(query3, dilation, offsets_row), dilate(keys3, dilation, offsets_row), dilate(values3, dilation, offsets_row), dilate(dout3, dilation, offsets_row), dilate(log_total, dilation, offsets_row), dilate(delta, dilation, offsets_row)))
        grad_q = grad_q + spread(pieces[0], dilation, offsets_row)
        grad_k = grad_k + spread(pieces[1], dilation, offsets_row)
        grad_v = grad_v + spread(pieces[2], dilation, offsets_row)
    flat = (SEQ, HEADS * HEAD_DIM)
    return attended.reshape(flat), grad_q.reshape(flat), grad_k.reshape(flat), grad_v.reshape(flat)
```

```python
import jax
import jax.numpy as jnp
from jax import lax
from jax.experimental import pallas as pl
from jax.experimental.pallas import tpu as pltpu
from jax.sharding import PartitionSpec as P

HEADS = 2
KEYS = 512
DIM = 128
TOKENS = 1024
BLOCK = 128
RATES = (8, 32, 128)
FACTOR = DIM**-0.5
MESH = pl.DeviceIdType.MESH
F32 = jnp.float32
BF16 = jnp.bfloat16

WORKER3 = (5, 11)


def dot(a, b, dims):
    return lax.dot_general(a, b, (dims, ((), ())), preferred_element_type=F32)


def nn(a, b):
    return dot(a, b, ((1,), (0,)))


def nt(a, b):
    return dot(a, b, ((1,), (1,)))


def tn(a, b):
    return dot(a, b, ((0,), (0,)))


def split3(a):
    high = a.astype(BF16)
    rest = a - high.astype(F32)
    middle = rest.astype(BF16)
    low = (rest - middle.astype(F32)).astype(BF16)
    return jnp.concatenate([high.astype(F32), middle.astype(F32), low.astype(F32)], 0).astype(BF16)


def join3(a):
    rows = a.shape[0] // 3
    return a[:rows] + a[rows : 2 * rows] + a[2 * rows :]


def select_rows(stats, chooser):
    return join3(nn(split3(stats), chooser))


def select_rows_nt(stats, chooser):
    return join3(nt(split3(stats), chooser))


def iota(shape, dim):
    return lax.broadcasted_iota(jnp.int32, shape, dim)


def kernel(
    offsets, query, keys, values, dout,
    att_out, dq_out, dk_out, dv_out,
    sel, spread, sel2, sel3, dout_t, powers0, weighted0, stat0, logs,
    pack1, pack2, pack3, in1, work, in3, power_item, stat_item, weighted1,
    send2, send3, back2, back3, grad_send2, grad_send3, grad1, grad2, grad3,
    tiles, tiles1, tiles2, tiles3,
    send_in, send_back, send_stat, send_grad,
    recv_in, recv_back, recv_stat, recv_grad,
):
    me = lax.axis_index("seq")
    y = lax.rem(me, 4)
    z = lax.rem(lax.div(me, 4), 4)
    x = lax.div(me, 16)
    place = lax.rem(me, 16)
    plane = me - place
    group = me - y
    is2 = lax.rem(y, 2) == 0
    is3 = (place == WORKER3[0]) | (place == WORKER3[1])
    one2 = jnp.where(is2, 1, 0)
    one3 = jnp.where(is3, 1, 0)

    barrier = pltpu.get_barrier_semaphore()

    def greet(device):
        pl.semaphore_signal(barrier, inc=1, device_id={"seq": device}, device_id_type=MESH)

    @pl.when(is3)
    def _():
        def step(i, carry):
            greet(lax.rem(me + i, 64))
            return carry

        lax.fori_loop(1, 64, step, 0)

    @pl.when(is2)
    def _():
        def step(i, carry):
            greet(plane + lax.rem(place + i, 16))
            return carry

        lax.fori_loop(1, 16, step, 0)

    for spot in WORKER3:
        @pl.when(place != spot)
        def _(spot=spot):
            greet(plane + spot)

    for i in range(1, 4):
        greet(group + lax.rem(y + i, 4))

    bases = (0, 32 * y, 8 * place)
    for head in range(HEADS):
        off = [offsets[level, head] for level in range(3)]
        row = iota((256, 1), 0)
        target = jnp.where(
            row < 128,
            row * RATES[0] + off[0],
            jnp.where(row < 160, (row - 128) * RATES[1] + off[1], (row - 160) * RATES[2] + off[2]),
        )
        sel[head] = jnp.where(iota((256, TOKENS), 1) == target, 1.0, 0.0).astype(BF16)
        column = iota((1, 256), 1)
        target = jnp.where(
            column < 128,
            column * RATES[0] + off[0],
            jnp.where(
                column < 160, (column - 128) * RATES[1] + off[1], (column - 160) * RATES[2] + off[2]
            ),
        )
        spread[head] = jnp.where(iota((TOKENS, 256), 0) == target, 1.0, 0.0).astype(BF16)
        row = iota((128, 1), 0)
        for ref, level in ((sel2, 1), (sel3, 2)):
            target = (row - bases[level]) * RATES[level] + off[level]
            ref[head] = jnp.where(iota((128, TOKENS), 1) == target, 1.0, 0.0).astype(BF16)

        lanes = slice(DIM * head, DIM * head + DIM)
        chooser = sel[head, 0:176]
        pair_qk = nn(chooser, jnp.concatenate([query[:, lanes], keys[:, lanes]], 1))
        pair_vd = nn(chooser, jnp.concatenate([values[:, lanes], dout[:, lanes]], 1))
        pack1[:, 512 * head : 512 * head + 256] = pair_qk[:128].astype(BF16)
        pack1[:, 512 * head + 256 : 512 * head + 512] = pair_vd[:128].astype(BF16)
        pack2[head, :, 0:256] = pair_qk[128:160].astype(BF16)
        pack2[head, :, 256:512] = pair_vd[128:160].astype(BF16)
        pack3[head] = jnp.concatenate([pair_qk[160:168], pair_vd[160:168]], 0).astype(BF16)

    pl.semaphore_wait(barrier, 3 + (8 - one2) + (8 - one3) + 15 * one3)

    def remote(src, dst, send_sem, recv_sem, device):
        return pltpu.make_async_remote_copy(
            src_ref=src, dst_ref=dst, send_sem=send_sem, recv_sem=recv_sem,
            device_id={"seq": device}, device_id_type=MESH,
        )

    pending = []

    def send(src, dst, send_sem, recv_sem, device):
        copy = remote(src, dst, send_sem, recv_sem, device)
        pending.append((device, copy))

        @pl.when(device != me)
        def _():
            copy.start()

    def arrived(ref, sem):
        pltpu.make_async_copy(ref, ref, sem).wait()

    for block in range(4):
        for head in range(HEADS):
            send(pack3.at[head], in3.at[me], send_in.at[2 * block + head], recv_in.at[2],
                 16 * block + WORKER3[head])
    for block in range(4):
        for head in range(HEADS):
            send(pack2.at[head], work.at[pl.ds(pl.multiple_of(32 * place, 32), 32)],
                 send_in.at[8 + 2 * block + head], recv_in.at[1], plane + 4 * block + 2 * head)
    for i in range(1, 4):
        send(pack1, in1.at[pl.ds(pl.multiple_of(128 * y, 128), 128)], send_in.at[15 + i],
             recv_in.at[0], group + lax.rem(y + i, 4))

    in1[pl.ds(pl.multiple_of(128 * y, 128), 128)] = pack1[...]
    for head in range(HEADS):
        @pl.when(place == WORKER3[head])
        def _(head=head):
            in3[me] = pack3[head]

        @pl.when(y == 2 * head)
        def _(head=head):
            work[pl.ds(pl.multiple_of(32 * place, 32), 32)] = pack2[head]

    def unit_refs(unit):
        head = lax.div(unit, 2)
        segment = lax.rem(unit, 2)
        return head, segment, pl.ds(pl.multiple_of(DIM * head, DIM), DIM)

    def forward0(unit, carry):
        head, segment, lanes = unit_refs(unit)
        rows = pl.ds(pl.multiple_of(KEYS * segment, KEYS), KEYS)
        key, value = keys[rows, lanes], values[rows, lanes]
        for chunk in range(2):
            start = pl.multiple_of(KEYS * segment + 256 * chunk, 256)
            part = pl.ds(start, 256)
            scores = nt(key, query[part, lanes]) * FACTOR
            row_max = jnp.max(scores, 0, keepdims=True)
            powers = jnp.exp(scores - row_max)
            powers0[unit, :, 256 * chunk : 256 * chunk + 256] = powers
            weighted0[head, :, part] = tn(value, powers.astype(BF16))
            stat0[head, 0:1, part] = row_max
            stat0[head, 1:2, part] = jnp.sum(powers, 0, keepdims=True)
        return carry

    lax.fori_loop(0, 4, forward0, 0)
    for head in range(HEADS):
        dout_t[head] = dout[:, DIM * head : DIM * head + DIM].astype(F32).T

    def item_forward(ref, first, block, slot):
        rows = pl.ds(pl.multiple_of(BLOCK * block, BLOCK), BLOCK)
        scores = nt(ref[:, first + 128 : first + 256], ref[rows, first : first + 128]) * FACTOR
        row_max = jnp.max(scores, 0, keepdims=True)
        powers = jnp.exp(scores - row_max)
        total = jnp.sum(powers, 0, keepdims=True)
        power_item[slot] = powers
        stat_item[slot] = jnp.concatenate([row_max, total, jnp.zeros((6, BLOCK), F32)], 0)
        return tn(powers.astype(BF16), ref[:, first + 256 : first + 384])

    def item_backward(ref, first, block, slot, log_all, delta_all, log_own, delta_own):
        rows = pl.ds(pl.multiple_of(BLOCK * block, BLOCK), BLOCK)
        q_all, k_all = ref[:, first : first + 128], ref[:, first + 128 : first + 256]
        v_all, d_all = ref[:, first + 256 : first + 384], ref[:, first + 384 : first + 512]
        k_own, v_own = ref[rows, first + 128 : first + 256], ref[rows, first + 256 : first + 384]
        d_own = ref[rows, first + 384 : first + 512]
        probs = power_item[slot] * jnp.exp(stat_item[slot, 0:1] - log_own)
        low = (probs * (nt(v_all, d_own) - delta_own)).astype(BF16)
        grad_q = FACTOR * tn(low, k_all)
        probs = jnp.exp(nt(k_own, q_all) * FACTOR - log_all)
        low = (probs * (nt(v_own, d_all) - delta_all)).astype(BF16)
        grad_k = FACTOR * nn(low, q_all)
        grad_v = nn(probs.astype(BF16), d_all)
        return jnp.concatenate([grad_q, grad_k, grad_v], 1)

    worker_block = jnp.where(is2, z, x)
    worker_head = jnp.where(is2, lax.div(y, 2), jnp.where(place == WORKER3[0], 0, 1))

    @pl.when(is2)
    def _():
        arrived(work.at[pl.ds(0, 480)], recv_in.at[1])

    @pl.when(is3)
    def _():
        arrived(in3.at[pl.ds(0, 63)], recv_in.at[2])
        both = in3[...].astype(F32)
        work[:, 0:256] = both[:, 0:8].reshape(KEYS, 256).astype(BF16)
        work[:, 256:512] = both[:, 8:16].reshape(KEYS, 256).astype(BF16)

    @pl.when(is2 | is3)
    def _():
        weighted = item_forward(work, 0, worker_block, 2)
        stats = stat_item[2]

        @pl.when(is2)
        def _():
            for i in range(4):
                send2[i] = jnp.concatenate([weighted[32 * i : 32 * i + 32], stats], 0)

        @pl.when(is3)
        def _():
            for i in range(16):
                send3[i] = jnp.concatenate([weighted[8 * i : 8 * i + 8], stats], 0)

    def returns(src2, dst2, src3, dst3, sems, recv, wait):
        def each(src, dst, sem, recv_sem, device):
            copy = remote(src, dst, sem, recv_sem, device)
            if wait:
                copy.wait_send()
            else:
                copy.start()

        @pl.when(is2)
        def _():
            for i in range(1, 4):
                other = lax.rem(y + i, 4)
                each(src2.at[other], dst2.at[worker_head], sems.at[i], recv.at[worker_head], group + other)
            if not wait:
                dst2[worker_head] = src2[y]

        @pl.when(is3)
        def _():
            def step(i, carry):
                other = lax.rem(place + i, 16)
                each(src3.at[other], dst3.at[worker_head], sems.at[i], recv.at[2 + worker_head], plane + other)
                return carry

            lax.fori_loop(1, 16, step, 0)
            if not wait:
                dst3[worker_head] = src3[place]

    def returned(dst2, dst3, recv):
        for head in range(HEADS):
            @pl.when(y != 2 * head)
            def _(head=head):
                arrived(dst2.at[head], recv.at[head])

            @pl.when(place != WORKER3[head])
            def _(head=head):
                arrived(dst3.at[head], recv.at[2 + head])

    returns(send2, back2, send3, back3, send_back, recv_back, False)

    arrived(in1.at[pl.ds(0, 384)], recv_in.at[0])
    for head in range(HEADS):
        weighted1[head] = item_forward(in1, 512 * head, y, head)

    returned(back2, back3, recv_back)
    position = iota((1, TOKENS), 1)
    for head in range(HEADS):
        found = (
            select_rows(stat_item[head], sel[head, 0:128]),
            select_rows(back2[head, 32:40], sel2[head]),
            select_rows(back3[head, 8:16], sel3[head]),
        )
        maxima = [stat0[head, 0:1]]
        for level in range(3):
            member = lax.rem(position, RATES[level]) == offsets[level, head]
            maxima.append(jnp.where(member, found[level][0:1], -jnp.inf))
        peak = jnp.maximum(jnp.maximum(maxima[0], maxima[1]), jnp.maximum(maxima[2], maxima[3]))
        factors = [jnp.exp(item - peak) for item in maxima]
        denominator = factors[0] * stat0[head, 1:2]
        for level in range(3):
            denominator += factors[level + 1] * found[level][1:2]
        log_total = peak + jnp.log(denominator)
        shares = [item / denominator for item in factors]
        lane_shares = select_rows_nt(
            jnp.concatenate(shares[1:] + [jnp.zeros((5, TOKENS), F32)], 0), sel[head]
        )
        lane = iota((1, 256), 1)
        share = jnp.where(lane < 128, lane_shares[0:1], jnp.where(lane < 160, lane_shares[1:2], lane_shares[2:3]))
        stacked = jnp.concatenate(
            [weighted1[head], back2[head, 0:32], back3[head, 0:8], jnp.zeros((88, DIM), F32)], 0
        ).T * share
        high = stacked.astype(BF16)
        low = (stacked - high.astype(F32)).astype(BF16)
        attended = shares[0] * weighted0[head] + nn(high, sel[head]) + nn(low, sel[head])
        delta = jnp.sum(dout_t[head] * attended, 0, keepdims=True)
        att_out[:, DIM * head : DIM * head + DIM] = attended.T
        rows = jnp.concatenate([log_total, delta, jnp.zeros((6, TOKENS), F32)], 0)
        logs[head] = rows
        tiles[0, 2 * head : 2 * head + 2] = select_rows_nt(rows, sel[head, 0:128])[0:2]
        tiles[1, 2 * head : 2 * head + 2] = select_rows_nt(rows, sel2[head])[0:2]
        tiles[2, 2 * head : 2 * head + 2] = select_rows_nt(rows, sel3[head])[0:2]
    for level in range(3):
        tiles[level, 4:8] = jnp.zeros((4, BLOCK), F32)

    for block in range(4):
        for head in range(HEADS):
            send(tiles.at[2], tiles3.at[me], send_stat.at[2 * block + head], recv_stat.at[2],
                 16 * block + WORKER3[head])
    for block in range(4):
        for head in range(HEADS):
            send(tiles.at[1], tiles2.at[place], send_stat.at[8 + 2 * block + head], recv_stat.at[1],
                 plane + 4 * block + 2 * head)
    for i in range(1, 4):
        send(tiles.at[0], tiles1.at[y], send_stat.at[15 + i], recv_stat.at[0], group + lax.rem(y + i, 4))
    tiles1[y] = tiles[0]

    @pl.when(is2)
    def _():
        tiles2[place] = tiles[1]

    @pl.when(is3)
    def _():
        tiles3[me] = tiles[2]

    def backward0(unit, carry):
        head, segment, lanes = unit_refs(unit)
        rows = pl.ds(pl.multiple_of(KEYS * segment, KEYS), KEYS)
        key, value = keys[rows, lanes], values[rows, lanes]
        grad_k = jnp.zeros((KEYS, DIM), F32)
        grad_v = jnp.zeros((KEYS, DIM), F32)
        for chunk in range(2):
            part = pl.ds(pl.multiple_of(KEYS * segment + 256 * chunk, 256), 256)
            rescale = jnp.exp(stat0[head, 0:1, part] - logs[head, 0:1, part])
            probs = powers0[unit, :, 256 * chunk : 256 * chunk + 256] * rescale
            grad_rows = dout[part, lanes]
            low = (probs * (nt(value, grad_rows) - logs[head, 1:2, part])).astype(BF16)
            grad_k += nn(low, query[part, lanes])
            grad_v += nn(probs.astype(BF16), grad_rows)
            dq_out[part, lanes] = (FACTOR * tn(key, low)).T
        dk_out[rows, lanes] = FACTOR * grad_k
        dv_out[rows, lanes] = grad_v
        return carry

    lax.fori_loop(0, 4, backward0, 0)

    def row_blocks(blocks):
        first = worker_head == 0
        logs_all = [jnp.where(first, blocks[i, 0:1], blocks[i, 2:3]) for i in range(4)]
        deltas_all = [jnp.where(first, blocks[i, 1:2], blocks[i, 3:4]) for i in range(4)]
        return logs_all, deltas_all

    def pick(rows, block):
        chosen = rows[0]
        for i in range(1, 4):
            chosen = jnp.where(block == i, rows[i], chosen)
        return chosen

    @pl.when(is2)
    def _():
        arrived(tiles2.at[pl.ds(0, 15)], recv_stat.at[1])
        stat_item[3] = jnp.sum(tiles2[0:4], 0)
        for i in range(1, 4):
            stat_item[3 + i] = jnp.sum(tiles2[4 * i : 4 * i + 4], 0)

    @pl.when(is3)
    def _():
        arrived(tiles3.at[pl.ds(0, 63)], recv_stat.at[2])
        for i in range(4):
            stat_item[3 + i] = jnp.sum(tiles3[16 * i : 16 * i + 16], 0)

    @pl.when(is2 | is3)
    def _():
        log_rows, delta_rows = row_blocks(stat_item[3:7])
        grads = item_backward(
            work, 0, worker_block, 2,
            jnp.concatenate(log_rows, 1), jnp.concatenate(delta_rows, 1),
            pick(log_rows, worker_block), pick(delta_rows, worker_block),
        )

        @pl.when(is2)
        def _():
            for i in range(4):
                grad_send2[i] = grads[32 * i : 32 * i + 32]

        @pl.when(is3)
        def _():
            for i in range(16):
                grad_send3[i] = grads[8 * i : 8 * i + 8]

    returns(grad_send2, grad2, grad_send3, grad3, send_grad, recv_grad, False)

    arrived(tiles1.at[pl.ds(0, 3)], recv_stat.at[0])
    for head in range(HEADS):
        log_rows = [tiles1[i, 2 * head : 2 * head + 1] for i in range(4)]
        delta_rows = [tiles1[i, 2 * head + 1 : 2 * head + 2] for i in range(4)]
        grad1[head] = item_backward(
            in1, 512 * head, y, head,
            jnp.concatenate(log_rows, 1), jnp.concatenate(delta_rows, 1),
            tiles[0, 2 * head : 2 * head + 1], tiles[0, 2 * head + 1 : 2 * head + 2],
        )

    returned(grad2, grad3, recv_grad)
    for head in range(HEADS):
        lanes = slice(DIM * head, DIM * head + DIM)
        stacked = jnp.concatenate(
            [grad1[head], grad2[head], grad3[head], jnp.zeros((88, 3 * DIM), F32)], 0
        ).astype(BF16)
        added = nn(spread[head], stacked)
        dq_out[:, lanes] += added[:, 0:128]
        dk_out[:, lanes] += added[:, 128:256]
        dv_out[:, lanes] += added[:, 256:384]

    for device, copy in pending:
        @pl.when(device != me)
        def _(copy=copy):
            copy.wait_send()
    returns(send2, back2, send3, back3, send_back, recv_back, True)
    returns(grad_send2, grad2, grad_send3, grad3, send_grad, recv_grad, True)


def body(query, keys, values, grad_out, offsets):
    vmem = pl.BlockSpec(memory_space=pltpu.VMEM)
    smem = pl.BlockSpec(memory_space=pltpu.SMEM)
    out = jax.ShapeDtypeStruct((TOKENS, HEADS * DIM), F32)
    dma = pltpu.SemaphoreType.DMA
    return pl.pallas_call(
        kernel,
        out_shape=(out, out, out, out),
        in_specs=[smem, vmem, vmem, vmem, vmem],
        out_specs=(vmem, vmem, vmem, vmem),
        scratch_shapes=[
            pltpu.VMEM((2, 256, TOKENS), BF16),
            pltpu.VMEM((2, TOKENS, 256), BF16),
            pltpu.VMEM((2, 128, TOKENS), BF16),
            pltpu.VMEM((2, 128, TOKENS), BF16),
            pltpu.VMEM((2, DIM, TOKENS), F32),
            pltpu.VMEM((4, KEYS, KEYS), F32),
            pltpu.VMEM((2, DIM, TOKENS), F32),
            pltpu.VMEM((2, 8, TOKENS), F32),
            pltpu.VMEM((2, 8, TOKENS), F32),
            pltpu.VMEM((128, 1024), BF16),
            pltpu.VMEM((2, 32, 512), BF16),
            pltpu.VMEM((2, 16, 256), BF16),
            pltpu.VMEM((512, 1024), BF16),
            pltpu.VMEM((512, 512), BF16),
            pltpu.VMEM((64, 16, 256), BF16),
            pltpu.VMEM((3, 512, 128), F32),
            pltpu.VMEM((7, 8, 128), F32),
            pltpu.VMEM((2, 128, 128), F32),
            pltpu.VMEM((4, 40, 128), F32),
            pltpu.VMEM((16, 16, 128), F32),
            pltpu.VMEM((2, 40, 128), F32),
            pltpu.VMEM((2, 16, 128), F32),
            pltpu.VMEM((4, 32, 384), F32),
            pltpu.VMEM((16, 8, 384), F32),
            pltpu.VMEM((2, 128, 384), F32),
            pltpu.VMEM((2, 32, 384), F32),
            pltpu.VMEM((2, 8, 384), F32),
            pltpu.VMEM((3, 8, 128), F32),
            pltpu.VMEM((4, 8, 128), F32),
            pltpu.VMEM((16, 8, 128), F32),
            pltpu.VMEM((64, 8, 128), F32),
            dma((19,)),
            dma((16,)),
            dma((19,)),
            dma((16,)),
            dma((3,)),
            dma((4,)),
            dma((3,)),
            dma((4,)),
        ],
        compiler_params=pltpu.CompilerParams(
            collective_id=0, has_side_effects=True, vmem_limit_bytes=48 * 2**20
        ),
    )(offsets, query, keys, values, grad_out)


def solution(mesh):
    spec = P("seq", "rep")
    return jax.shard_map(
        body,
        mesh=mesh,
        in_specs=(spec, spec, spec, spec, P(None, "rep")),
        out_specs=(spec, spec, spec, spec),
        check_vma=False,
    )
```

```python
import jax
import jax.numpy as jnp
from jax import lax
from jax.experimental import pallas as pl
from jax.experimental.pallas import tpu as pltpu
from jax.sharding import PartitionSpec as P

HEADS = 2
KEYS = 512
DIM = 128
TOKENS = 1024
BLOCK = 128
RATES = (8, 32, 128)
FACTOR = DIM**-0.5
MESH = pl.DeviceIdType.MESH
F32 = jnp.float32
BF16 = jnp.bfloat16

WORKER3 = (5, 11)


def dot(a, b, dims):
    return lax.dot_general(a, b, (dims, ((), ())), preferred_element_type=F32)


def nn(a, b):
    return dot(a, b, ((1,), (0,)))


def nt(a, b):
    return dot(a, b, ((1,), (1,)))


def tn(a, b):
    return dot(a, b, ((0,), (0,)))


def split3(a):
    high = a.astype(BF16)
    rest = a - high.astype(F32)
    middle = rest.astype(BF16)
    low = (rest - middle.astype(F32)).astype(BF16)
    return jnp.concatenate([high.astype(F32), middle.astype(F32), low.astype(F32)], 0).astype(BF16)


def join3(a):
    rows = a.shape[0] // 3
    return a[:rows] + a[rows : 2 * rows] + a[2 * rows :]


def select_rows(stats, chooser):
    return join3(nn(split3(stats), chooser))


def select_rows_nt(stats, chooser):
    return join3(nt(split3(stats), chooser))


def iota(shape, dim):
    return lax.broadcasted_iota(jnp.int32, shape, dim)


def worker2(half, head):
    return 4 * (1 + half) + 2 * head


def kernel(
    offsets, query_hbm, keys_hbm, values_hbm, dout_hbm,
    att_out, dq_out, dk_out, dv_out, spread, stack_out,
    query, keys, values, dout,
    sel, sel2, sel3, dout_t, powers0, weighted0, stat0, logs,
    pack1, pack2, pack3, in1, work, in3, power1, power_work, stat1, stat_own,
    send1, send2, send3, back1, back2, back3, grad_send1, grad_send2, grad_send3, stack,
    tiles, tiles1, tiles2, tiles3,
    load_sem, send_in, send_back, send_stat, send_grad,
    recv_in, recv_back, recv_stat, recv_grad,
):
    me = lax.axis_index("seq")
    y = lax.rem(me, 4)
    z = lax.rem(lax.div(me, 4), 4)
    x = lax.div(me, 16)
    place = lax.rem(me, 16)
    plane = me - place
    group = me - y
    side = lax.rem(y, 2)
    pair = lax.div(y, 2)
    partner = group + 2 * pair + 1 - side
    half = lax.div(z, 2)
    is2 = (side == 0) & ((z == 1) | (z == 2))
    head2 = pair
    is3 = (place == WORKER3[0]) | (place == WORKER3[1])
    head3 = jnp.where(place == WORKER3[0], 0, 1)
    one2 = jnp.where(is2, 1, 0)
    one3 = jnp.where(is3, 1, 0)

    loads = []
    for i, (source, held) in enumerate(
        ((query_hbm, query), (keys_hbm, keys), (values_hbm, values), (dout_hbm, dout))
    ):
        loads.append(pltpu.make_async_copy(source, held, load_sem.at[i]))
        loads[-1].start()

    barrier = pltpu.get_barrier_semaphore()

    def greet(device):
        pl.semaphore_signal(barrier, inc=1, device_id={"seq": device}, device_id_type=MESH)

    @pl.when(is3)
    def _():
        def step(i, carry):
            greet(lax.rem(me + i, 64))
            return carry

        lax.fori_loop(1, 64, step, 0)

    @pl.when(is2)
    def _():
        def step(i, carry):
            greet(plane + lax.rem(place + i, 16))
            return carry

        lax.fori_loop(1, 16, step, 0)

    for spot in WORKER3:
        @pl.when(place != spot)
        def _(spot=spot):
            greet(plane + spot)
    for head in range(HEADS):
        spot = worker2(half, head)

        @pl.when(place != spot)
        def _(spot=spot):
            greet(plane + spot)

    for i in range(1, 4):
        greet(group + lax.rem(y + i, 4))

    bases = (0, 32 * y, 8 * place)
    for head in range(HEADS):
        off = [offsets[head, level] for level in range(3)]

        def target(index, off=off):
            return jnp.where(
                index < 128,
                index * RATES[0] + off[0],
                jnp.where(
                    index < 160, (index - 128) * RATES[1] + off[1], (index - 160) * RATES[2] + off[2]
                ),
            )

        sel[head] = jnp.where(
            iota((256, TOKENS), 1) == target(iota((256, 1), 0)), 1.0, 0.0
        ).astype(BF16)
    for load in loads:
        load.wait()
    for head in range(HEADS):
        lanes = slice(DIM * head, DIM * head + DIM)
        chooser = sel[head, 0:176]
        first = nn(chooser, jnp.concatenate([keys[:, lanes], values[:, lanes]], 1))
        second = nn(chooser, jnp.concatenate([query[:, lanes], dout[:, lanes]], 1))
        pack1[head, :, 0:256] = first[:128].astype(BF16)
        pack1[head, :, 256:512] = second[:128].astype(BF16)
        pack2[head, :, 0:256] = first[128:160].astype(BF16)
        pack2[head, :, 256:512] = second[128:160].astype(BF16)
        pack3[head] = jnp.concatenate([first[160:168], second[160:168]], 0).astype(BF16)

    pl.semaphore_wait(barrier, 3 + (4 - one2) + (8 - one3) + 15 * one3 + 7 * one2)

    def remote(src, dst, send_sem, recv_sem, device):
        return pltpu.make_async_remote_copy(
            src_ref=src, dst_ref=dst, send_sem=send_sem, recv_sem=recv_sem,
            device_id={"seq": device}, device_id_type=MESH,
        )

    pending = []

    def send(src, dst, send_sem, recv_sem, device):
        copy = remote(src, dst, send_sem, recv_sem, device)
        pending.append((device, copy))

        @pl.when(device != me)
        def _():
            copy.start()

    def arrived(ref, sem):
        pltpu.make_async_copy(ref, ref, sem).wait()

    mine1 = pl.ds(pl.multiple_of(128 * y, 128), 128)
    mine2 = pl.ds(pl.multiple_of(32 * place, 32), 32)
    for block in range(4):
        for head in range(HEADS):
            send(pack3.at[head], in3.at[me], send_in.at[2 * block + head], recv_in.at[4],
                 16 * block + WORKER3[head])
    for part in range(2):
        for i in range(4):
            lanes = (slice(0, 384), slice(384, 512))[part]
            send(pack2.at[i % 2, :, lanes], work.at[mine2, lanes], send_in.at[8 + 4 * part + i],
                 recv_in.at[2 + part], plane + worker2(i // 2, i % 2))
        for i in range(3):
            wide = 384 if i == 0 else 256
            lanes = (slice(0, wide), slice(wide, 512))[part]
            other = (partner, group + 2 * (1 - pair), group + 2 * (1 - pair) + 1)[i]
            head = (1 - side, 0, 1)[i]
            send(pack1.at[head, :, lanes], in1.at[mine1, lanes], send_in.at[16 + 3 * part + i],
                 recv_in.at[part], other)

    in1[mine1] = pack1[side]
    for head in range(HEADS):
        @pl.when(place == WORKER3[head])
        def _(head=head):
            in3[me] = pack3[head]

    @pl.when(is2)
    def _():
        work[mine2] = pack2[head2]

    def unit_refs(unit):
        head = lax.div(unit, 2)
        segment = lax.rem(unit, 2)
        return head, segment, pl.ds(pl.multiple_of(DIM * head, DIM), DIM)

    def forward0(unit, carry):
        head, segment, lanes = unit_refs(unit)
        rows = pl.ds(pl.multiple_of(KEYS * segment, KEYS), KEYS)
        key, value = keys[rows, lanes], values[rows, lanes]
        for chunk in range(2):
            start = pl.multiple_of(KEYS * segment + 256 * chunk, 256)
            part = pl.ds(start, 256)
            scores = nt(key, query[part, lanes]) * FACTOR
            row_max = jnp.max(scores, 0, keepdims=True)
            powers = jnp.exp(scores - row_max)
            powers0[unit, :, 256 * chunk : 256 * chunk + 256] = powers
            weighted0[head, :, part] = tn(value, powers.astype(BF16))
            stat0[head, 0:1, part] = row_max
            stat0[head, 1:2, part] = jnp.sum(powers, 0, keepdims=True)
        return carry

    lax.fori_loop(0, 4, forward0, 0)
    for head in range(HEADS):
        dout_t[head] = dout[:, DIM * head : DIM * head + DIM].astype(F32).T

    for head in range(HEADS):
        off = [offsets[head, level] for level in range(3)]
        column = iota((1, 256), 1)
        target = jnp.where(
            column < 128,
            column * RATES[0] + off[0],
            jnp.where(
                column < 160, (column - 128) * RATES[1] + off[1], (column - 160) * RATES[2] + off[2]
            ),
        )
        spread[head] = jnp.where(iota((TOKENS, 256), 0) == target, 1.0, 0.0).astype(BF16)
        row = iota((128, 1), 0)
        for ref, level in ((sel2, 1), (sel3, 2)):
            target = (row - bases[level]) * RATES[level] + off[level]
            ref[head] = jnp.where(iota((128, TOKENS), 1) == target, 1.0, 0.0).astype(BF16)

    def item_forward(ref, rows, powers_ref):
        scores = nt(ref[:, 0:128], ref[rows, 256:384]) * FACTOR
        row_max = jnp.max(scores, 0, keepdims=True)
        powers = jnp.exp(scores - row_max)
        powers_ref[...] = powers
        total = jnp.sum(powers, 0, keepdims=True)
        stats = jnp.concatenate([row_max, total, jnp.zeros((6, total.shape[1]), F32)], 0)
        return tn(powers.astype(BF16), ref[:, 128:256]), stats

    def item_backward(ref, rows, powers_ref, log_all, delta_all, row_max, log_own, delta_own):
        k_all, v_all, q_all, d_all = (ref[:, 128 * i : 128 * i + 128] for i in range(4))
        k_own, v_own, d_own = ref[rows, 0:128], ref[rows, 128:256], ref[rows, 384:512]
        probs = powers_ref[...] * jnp.exp(row_max - log_own)
        low = (probs * (nt(v_all, d_own) - delta_own)).astype(BF16)
        grad_q = FACTOR * tn(low, k_all)
        probs = jnp.exp(nt(k_own, q_all) * FACTOR - log_all)
        low = (probs * (nt(v_own, d_all) - delta_all)).astype(BF16)
        grad_k = FACTOR * nn(low, q_all)
        grad_v = nn(probs.astype(BF16), d_all)
        return jnp.concatenate([grad_q, grad_k, grad_v], 1)

    rows1 = pl.ds(pl.multiple_of(256 * pair, 256), 256)
    rows2 = pl.ds(pl.multiple_of(256 * half, 256), 256)
    rows3 = pl.ds(pl.multiple_of(128 * x, 128), 128)
    power3 = power_work.at[:, 0:128]

    @pl.when(is2)
    def _():
        arrived(work.at[pl.ds(0, 480), pl.ds(0, 384)], recv_in.at[2])
        weighted, stats = item_forward(work, rows2, power_work)
        stat_own[:, 0:256] = stats
        for i in range(8):
            tile = stats[:, 128 * (i // 4) : 128 * (i // 4) + 128]
            send2[i] = jnp.concatenate([weighted[32 * i : 32 * i + 32], tile], 0)

    @pl.when(is3)
    def _():
        arrived(in3.at[pl.ds(0, 63)], recv_in.at[4])
        both = in3[...].astype(F32)
        work[:, 0:256] = both[:, 0:8].reshape(KEYS, 256).astype(BF16)
        work[:, 256:512] = both[:, 8:16].reshape(KEYS, 256).astype(BF16)
        weighted, stats = item_forward(work, rows3, power3)
        stat_own[:, 0:128] = stats
        for i in range(16):
            send3[i] = jnp.concatenate([weighted[8 * i : 8 * i + 8], stats], 0)

    def returns(src2, dst2, src3, dst3, sems, recv, wait):
        def each(src, dst, sem, recv_sem, device):
            copy = remote(src, dst, sem, recv_sem, device)
            if wait:
                copy.wait_send()
            else:
                copy.start()

        @pl.when(is2)
        def _():
            here = place - 8 * half

            def step(i, carry):
                other = lax.rem(here + i, 8)
                each(src2.at[other], dst2.at[head2], sems.at[i], recv.at[head2], plane + 8 * half + other)
                return carry

            lax.fori_loop(1, 8, step, 0)
            if not wait:
                dst2[head2] = src2[here]

        @pl.when(is3)
        def _():
            def step(i, carry):
                other = lax.rem(place + i, 16)
                each(src3.at[other], dst3.at[head3], sems.at[i], recv.at[2 + head3], plane + other)
                return carry

            lax.fori_loop(1, 16, step, 0)
            if not wait:
                dst3[head3] = src3[place]

    def returned(dst1, dst2, dst3, recv):
        arrived(dst1.at[1 - side], recv.at[4])
        for head in range(HEADS):
            @pl.when(place != worker2(half, head))
            def _(head=head):
                arrived(dst2.at[head], recv.at[head])

            @pl.when(place != WORKER3[head])
            def _(head=head):
                arrived(dst3.at[head], recv.at[2 + head])

    returns(send2, back2, send3, back3, send_back, recv_back, False)

    arrived(in1.at[pl.ds(0, 448), pl.ds(0, 256)], recv_in.at[0])
    weighted, stats = item_forward(in1, rows1, power1)
    stat1[...] = stats
    for i in range(2):
        send1[i] = jnp.concatenate(
            [weighted[128 * i : 128 * i + 128], stats[:, 128 * i : 128 * i + 128]], 0
        )
    send(send1.at[1 - side], back1.at[side], send_back.at[16], recv_back.at[4], partner)
    back1[side] = send1[side]

    returned(back1, back2, back3, recv_back)
    position = iota((1, TOKENS), 1)
    for head in range(HEADS):
        found = (
            select_rows(back1[head, 128:136], sel[head, 0:128]),
            select_rows(back2[head, 32:40], sel2[head]),
            select_rows(back3[head, 8:16], sel3[head]),
        )
        maxima = [stat0[head, 0:1]]
        for level in range(3):
            member = lax.rem(position, RATES[level]) == offsets[head, level]
            maxima.append(jnp.where(member, found[level][0:1], -jnp.inf))
        peak = jnp.maximum(jnp.maximum(maxima[0], maxima[1]), jnp.maximum(maxima[2], maxima[3]))
        factors = [jnp.exp(item - peak) for item in maxima]
        denominator = factors[0] * stat0[head, 1:2]
        for level in range(3):
            denominator += factors[level + 1] * found[level][1:2]
        log_total = peak + jnp.log(denominator)
        shares = [item / denominator for item in factors]
        lane_shares = select_rows_nt(
            jnp.concatenate(shares[1:] + [jnp.zeros((5, TOKENS), F32)], 0), sel[head]
        )
        lane = iota((1, 256), 1)
        share = jnp.where(lane < 128, lane_shares[0:1], jnp.where(lane < 160, lane_shares[1:2], lane_shares[2:3]))
        stacked = jnp.concatenate(
            [back1[head, 0:128], back2[head, 0:32], back3[head, 0:8], jnp.zeros((88, DIM), F32)], 0
        ).T * share
        high = stacked.astype(BF16)
        low = (stacked - high.astype(F32)).astype(BF16)
        attended = shares[0] * weighted0[head] + nn(high, sel[head]) + nn(low, sel[head])
        delta = jnp.sum(dout_t[head] * attended, 0, keepdims=True)
        att_out[:, DIM * head : DIM * head + DIM] = attended.T
        rows = jnp.concatenate([log_total, delta, jnp.zeros((6, TOKENS), F32)], 0)
        logs[head] = rows
        tiles[0, 2 * head : 2 * head + 2] = select_rows_nt(rows, sel[head, 0:128])[0:2]
        tiles[1, 2 * head : 2 * head + 2] = select_rows_nt(rows, sel2[head])[0:2]
        tiles[2, 2 * head : 2 * head + 2] = select_rows_nt(rows, sel3[head])[0:2]
    for level in range(3):
        tiles[level, 4:8] = jnp.zeros((4, BLOCK), F32)

    for block in range(4):
        for head in range(HEADS):
            send(tiles.at[2], tiles3.at[me], send_stat.at[2 * block + head], recv_stat.at[2],
                 16 * block + WORKER3[head])
    for i in range(4):
        send(tiles.at[1], tiles2.at[place], send_stat.at[8 + i], recv_stat.at[1],
             plane + worker2(i // 2, i % 2))
    for i in range(1, 4):
        send(tiles.at[0], tiles1.at[y], send_stat.at[11 + i], recv_stat.at[0], group + lax.rem(y + i, 4))
    tiles1[y] = tiles[0]

    @pl.when(is2)
    def _():
        tiles2[place] = tiles[1]

    @pl.when(is3)
    def _():
        tiles3[me] = tiles[2]

    def backward0(unit, carry):
        head, segment, lanes = unit_refs(unit)
        rows = pl.ds(pl.multiple_of(KEYS * segment, KEYS), KEYS)
        key, value = keys[rows, lanes], values[rows, lanes]
        grad_k = jnp.zeros((KEYS, DIM), F32)
        grad_v = jnp.zeros((KEYS, DIM), F32)
        for chunk in range(2):
            part = pl.ds(pl.multiple_of(KEYS * segment + 256 * chunk, 256), 256)
            rescale = jnp.exp(stat0[head, 0:1, part] - logs[head, 0:1, part])
            probs = powers0[unit, :, 256 * chunk : 256 * chunk + 256] * rescale
            grad_rows = dout[part, lanes]
            low = (probs * (nt(value, grad_rows) - logs[head, 1:2, part])).astype(BF16)
            grad_k += nn(low, query[part, lanes])
            grad_v += nn(probs.astype(BF16), grad_rows)
            dq_out[part, lanes] = (FACTOR * tn(key, low)).T
        dk_out[rows, lanes] = FACTOR * grad_k
        dv_out[rows, lanes] = grad_v
        return carry

    lax.fori_loop(0, 4, backward0, 0)

    def row_blocks(blocks, head):
        first = head == 0
        return (
            [jnp.where(first, tile[0:1], tile[2:3]) for tile in blocks],
            [jnp.where(first, tile[1:2], tile[3:4]) for tile in blocks],
        )

    def pick(rows, block):
        chosen = rows[0]
        for i in range(1, len(rows)):
            chosen = jnp.where(block == i, rows[i], chosen)
        return chosen

    def pairs(rows):
        return [jnp.concatenate(rows[0:2], 1), jnp.concatenate(rows[2:4], 1)]

    @pl.when(is2)
    def _():
        arrived(work.at[pl.ds(0, 480), pl.ds(0, 128)], recv_in.at[3])
        arrived(tiles2.at[pl.ds(0, 15)], recv_stat.at[1])
        blocks = [jnp.sum(tiles2[4 * i : 4 * i + 4], 0) for i in range(4)]
        log_rows, delta_rows = row_blocks(blocks, head2)
        grads = item_backward(
            work, rows2, power_work, jnp.concatenate(log_rows, 1), jnp.concatenate(delta_rows, 1),
            stat_own[0:1], pick(pairs(log_rows), half), pick(pairs(delta_rows), half),
        ).astype(BF16)
        for i in range(8):
            grad_send2[i] = grads[32 * i : 32 * i + 32]

    @pl.when(is3)
    def _():
        arrived(tiles3.at[pl.ds(0, 63)], recv_stat.at[2])
        blocks = [jnp.sum(tiles3[16 * i : 16 * i + 16], 0) for i in range(4)]
        log_rows, delta_rows = row_blocks(blocks, head3)
        grads = item_backward(
            work, rows3, power3, jnp.concatenate(log_rows, 1), jnp.concatenate(delta_rows, 1),
            stat_own[0:1, 0:128], pick(log_rows, x), pick(delta_rows, x),
        )
        for i in range(16):
            tile = jnp.concatenate([grads[8 * i : 8 * i + 8], jnp.zeros((8, 3 * DIM), F32)], 0)
            grad_send3[i] = tile.astype(BF16)

    stack1 = stack.at[:, 0:128]
    stack2 = stack.at[:, 128:160]
    stack3 = stack.at[:, 160:176]
    returns(grad_send2, stack2, grad_send3, stack3, send_grad, recv_grad, False)

    arrived(in1.at[pl.ds(0, 320), pl.ds(0, 256)], recv_in.at[1])
    arrived(tiles1.at[pl.ds(0, 3)], recv_stat.at[0])
    log_rows, delta_rows = row_blocks([tiles1[i] for i in range(4)], side)
    grads = item_backward(
        in1, rows1, power1, jnp.concatenate(log_rows, 1), jnp.concatenate(delta_rows, 1),
        stat1[0:1], pick(pairs(log_rows), pair), pick(pairs(delta_rows), pair),
    ).astype(BF16)
    for i in range(2):
        grad_send1[i] = grads[128 * i : 128 * i + 128]
    send(grad_send1.at[1 - side], stack1.at[side], send_grad.at[16], recv_grad.at[4], partner)
    stack1[side] = grad_send1[side]

    stack_out[:, 176:256] = jnp.zeros((2, 80, 3 * DIM), BF16)
    returned(stack1, stack2, stack3, recv_grad)
    stack_out[:, 0:176] = stack[...]

    for device, copy in pending:
        @pl.when(device != me)
        def _(copy=copy):
            copy.wait_send()
    returns(send2, back2, send3, back3, send_back, recv_back, True)
    returns(grad_send2, stack2, grad_send3, stack3, send_grad, recv_grad, True)


def finish(att, dq, dk, dv, spread, stack, att_out, dq_out, dk_out, dv_out, full, sems):
    first = pltpu.make_async_copy(att, att_out, sems.at[12])
    first.start()
    copies = [first]
    for part in range(4):
        rows = slice(256 * part, 256 * part + 256)
        for head in range(HEADS):
            lanes = slice(DIM * head, DIM * head + DIM)
            added = nn(spread[head, rows], stack[head])
            for i, ref in enumerate((dq, dk, dv)):
                full[i, rows, lanes] = ref[rows, lanes] + added[:, DIM * i : DIM * i + DIM]
        for i, out in enumerate((dq_out, dk_out, dv_out)):
            copies.append(
                pltpu.make_async_copy(full.at[i, rows], out.at[rows], sems.at[3 * part + i])
            )
            copies[-1].start()
    for copy in copies:
        copy.wait()


def body(query, keys, values, grad_out, offsets):
    vmem = pl.BlockSpec(memory_space=pltpu.VMEM)
    hbm = pl.BlockSpec(memory_space=pltpu.HBM)
    smem = pl.BlockSpec(memory_space=pltpu.SMEM)
    out = jax.ShapeDtypeStruct((TOKENS, HEADS * DIM), F32)
    dma = pltpu.SemaphoreType.DMA
    held = pltpu.VMEM((TOKENS, HEADS * DIM), BF16)
    parts = pl.pallas_call(
        kernel,
        out_shape=(
            out, out, out, out,
            jax.ShapeDtypeStruct((2, TOKENS, 256), BF16),
            jax.ShapeDtypeStruct((2, 256, 3 * DIM), BF16),
        ),
        in_specs=[smem, hbm, hbm, hbm, hbm],
        out_specs=(vmem,) * 6,
        scratch_shapes=[
            held, held, held, held,
            pltpu.VMEM((2, 256, TOKENS), BF16),
            pltpu.VMEM((2, 128, TOKENS), BF16),
            pltpu.VMEM((2, 128, TOKENS), BF16),
            pltpu.VMEM((2, DIM, TOKENS), F32),
            pltpu.VMEM((4, KEYS, KEYS), F32),
            pltpu.VMEM((2, DIM, TOKENS), F32),
            pltpu.VMEM((2, 8, TOKENS), F32),
            pltpu.VMEM((2, 8, TOKENS), F32),
            pltpu.VMEM((2, 128, 512), BF16),
            pltpu.VMEM((2, 32, 512), BF16),
            pltpu.VMEM((2, 16, 256), BF16),
            pltpu.VMEM((512, 512), BF16),
            pltpu.VMEM((512, 512), BF16),
            pltpu.VMEM((64, 16, 256), BF16),
            pltpu.VMEM((512, 256), F32),
            pltpu.VMEM((512, 256), F32),
            pltpu.VMEM((8, 256), F32),
            pltpu.VMEM((8, 256), F32),
            pltpu.VMEM((2, 136, 128), F32),
            pltpu.VMEM((8, 40, 128), F32),
            pltpu.VMEM((16, 16, 128), F32),
            pltpu.VMEM((2, 136, 128), F32),
            pltpu.VMEM((2, 40, 128), F32),
            pltpu.VMEM((2, 16, 128), F32),
            pltpu.VMEM((2, 128, 384), BF16),
            pltpu.VMEM((8, 32, 384), BF16),
            pltpu.VMEM((16, 16, 384), BF16),
            pltpu.VMEM((2, 176, 384), BF16),
            pltpu.VMEM((3, 8, 128), F32),
            pltpu.VMEM((4, 8, 128), F32),
            pltpu.VMEM((16, 8, 128), F32),
            pltpu.VMEM((64, 8, 128), F32),
            dma((4,)),
            dma((22,)),
            dma((17,)),
            dma((15,)),
            dma((17,)),
            dma((5,)),
            dma((5,)),
            dma((3,)),
            dma((5,)),
        ],
        compiler_params=pltpu.CompilerParams(
            collective_id=0, has_side_effects=True, vmem_limit_bytes=32 * 2**20
        ),
    )(offsets.T, query, keys, values, grad_out)
    return pl.pallas_call(
        finish,
        out_shape=(out, out, out, out),
        in_specs=[vmem] * 6,
        out_specs=(hbm,) * 4,
        scratch_shapes=[pltpu.VMEM((3, TOKENS, HEADS * DIM), F32), dma((13,))],
        compiler_params=pltpu.CompilerParams(vmem_limit_bytes=16 * 2**20),
    )(*parts)


def solution(mesh):
    spec = P("seq", "rep")
    return jax.shard_map(
        body,
        mesh=mesh,
        in_specs=(spec, spec, spec, spec, P(None, "rep")),
        out_specs=(spec, spec, spec, spec),
        check_vma=False,
    )
```

```python
import jax
import jax.numpy as jnp
from jax import lax
from jax.experimental import pallas as pl
from jax.experimental.pallas import tpu as pltpu
from jax.sharding import PartitionSpec as P

HEADS = 2
KEYS = 512
DIM = 128
TOKENS = 1024
BLOCK = 128
RATES = (8, 32, 128)
FACTOR = DIM**-0.5
MESH = pl.DeviceIdType.MESH
F32 = jnp.float32
BF16 = jnp.bfloat16

WORKER3 = (5, 11)


def dot(a, b, dims):
    return lax.dot_general(a, b, (dims, ((), ())), preferred_element_type=F32)


def nn(a, b):
    return dot(a, b, ((1,), (0,)))


def nt(a, b):
    return dot(a, b, ((1,), (1,)))


def tn(a, b):
    return dot(a, b, ((0,), (0,)))


def split3(a):
    high = a.astype(BF16)
    rest = a - high.astype(F32)
    middle = rest.astype(BF16)
    low = (rest - middle.astype(F32)).astype(BF16)
    return jnp.concatenate([high.astype(F32), middle.astype(F32), low.astype(F32)], 0).astype(BF16)


def join3(a):
    rows = a.shape[0] // 3
    return a[:rows] + a[rows : 2 * rows] + a[2 * rows :]


def select_rows(stats, chooser):
    return join3(nn(split3(stats), chooser))


def select_rows_nt(stats, chooser):
    return join3(nt(split3(stats), chooser))


def iota(shape, dim):
    return lax.broadcasted_iota(jnp.int32, shape, dim)


def worker2(half, head):
    return 4 * (1 + half) + 2 * head


def kernel(
    offsets_hbm, query_hbm, keys_hbm, values_hbm, dout_hbm,
    att_out, dq_out, dk_out, dv_out, spread, stack_out,
    offsets, query, keys, values, dout,
    sel, sel2, sel3, powers0, products0, shares, weighted0, stat0, logs,
    pack1, pack2, pack3, in1, work, in3, power1, power_work, product1, product_work, stat1, stat_own,
    send1, send2, send3, back1, back2, back3, grad_send1, grad_send2, grad_send3, stack,
    tiles, tiles1, tiles2, tiles3,
    load_sem, send_in, send_back, send_stat, send_grad,
    recv_in, recv_back, recv_stat, recv_grad,
):
    me = lax.axis_index("seq")
    y = lax.rem(me, 4)
    z = lax.rem(lax.div(me, 4), 4)
    x = lax.div(me, 16)
    place = lax.rem(me, 16)
    plane = me - place
    group = me - y
    side = lax.rem(y, 2)
    pair = lax.div(y, 2)
    partner = group + 2 * pair + 1 - side
    half = lax.div(z, 2)
    is2 = (side == 0) & ((z == 1) | (z == 2))
    head2 = pair
    is3 = (place == WORKER3[0]) | (place == WORKER3[1])
    head3 = jnp.where(place == WORKER3[0], 0, 1)
    one2 = jnp.where(is2, 1, 0)
    one3 = jnp.where(is3, 1, 0)

    load_offsets = pltpu.make_async_copy(offsets_hbm, offsets, load_sem.at[4])
    load_offsets.start()
    loads = []
    for i, (source, held) in enumerate(
        ((query_hbm, query), (keys_hbm, keys), (values_hbm, values), (dout_hbm, dout))
    ):
        loads.append(pltpu.make_async_copy(source, held, load_sem.at[i]))
        loads[-1].start()

    barrier = pltpu.get_barrier_semaphore()

    def greet(device):
        pl.semaphore_signal(barrier, inc=1, device_id={"seq": device}, device_id_type=MESH)

    @pl.when(is3)
    def _():
        def step(i, carry):
            greet(lax.rem(me + i, 64))
            return carry

        lax.fori_loop(1, 64, step, 0)

    @pl.when(is2)
    def _():
        def step(i, carry):
            greet(plane + lax.rem(place + i, 16))
            return carry

        lax.fori_loop(1, 16, step, 0)

    for spot in WORKER3:
        @pl.when(place != spot)
        def _(spot=spot):
            greet(plane + spot)
    for head in range(HEADS):
        spot = worker2(half, head)

        @pl.when(place != spot)
        def _(spot=spot):
            greet(plane + spot)

    for i in range(1, 4):
        greet(group + lax.rem(y + i, 4))

    bases = (0, 32 * y, 8 * place)
    load_offsets.wait()
    for head in range(HEADS):
        off = [offsets[head, level] for level in range(3)]

        def target(index, off=off):
            return jnp.where(
                index < 128,
                index * RATES[0] + off[0],
                jnp.where(
                    index < 160, (index - 128) * RATES[1] + off[1], (index - 160) * RATES[2] + off[2]
                ),
            )

        sel[head] = jnp.where(
            iota((256, TOKENS), 1) == target(iota((256, 1), 0)), 1.0, 0.0
        ).astype(BF16)
    for load in loads:
        load.wait()
    for head in range(HEADS):
        lanes = slice(DIM * head, DIM * head + DIM)
        chooser = sel[head, 0:176]
        first = nn(chooser, jnp.concatenate([keys[:, lanes], values[:, lanes]], 1))
        second = nn(chooser, jnp.concatenate([query[:, lanes], dout[:, lanes]], 1))
        pack1[head, :, 0:256] = first[:128].astype(BF16)
        pack1[head, :, 256:512] = second[:128].astype(BF16)
        pack2[head, :, 0:256] = first[128:160].astype(BF16)
        pack2[head, :, 256:512] = second[128:160].astype(BF16)
        pack3[head] = jnp.concatenate([first[160:168], second[160:168]], 0).astype(BF16)

    pl.semaphore_wait(barrier, 3 + (4 - one2) + (8 - one3) + 15 * one3 + 7 * one2)

    def remote(src, dst, send_sem, recv_sem, device):
        return pltpu.make_async_remote_copy(
            src_ref=src, dst_ref=dst, send_sem=send_sem, recv_sem=recv_sem,
            device_id={"seq": device}, device_id_type=MESH,
        )

    pending = []

    def send(src, dst, send_sem, recv_sem, device):
        copy = remote(src, dst, send_sem, recv_sem, device)
        pending.append((device, copy))

        @pl.when(device != me)
        def _():
            copy.start()

    def arrived(ref, sem):
        pltpu.make_async_copy(ref, ref, sem).wait()

    mine1 = pl.ds(pl.multiple_of(128 * y, 128), 128)
    mine2 = pl.ds(pl.multiple_of(32 * place, 32), 32)
    for block in range(4):
        for head in range(HEADS):
            send(pack3.at[head], in3.at[me], send_in.at[2 * block + head], recv_in.at[4],
                 16 * block + WORKER3[head])
    for head in range(HEADS):
        send(pack2.at[head], work.at[mine2], send_in.at[8 + head], recv_in.at[2],
             plane + worker2(half, head))
    send(pack1.at[1 - side], in1.at[mine1], send_in.at[10], recv_in.at[0], partner)
    other_pair = group + 2 * (1 - pair)
    for part in range(2):
        lanes = (slice(0, 256), slice(256, 512))[part]
        for head in range(HEADS):
            send(pack2.at[head, :, lanes], work.at[mine2, lanes], send_in.at[11 + 4 * part + head],
                 recv_in.at[2 + part], plane + worker2(1 - half, head))
            send(pack1.at[head, :, lanes], in1.at[mine1, lanes], send_in.at[13 + 4 * part + head],
                 recv_in.at[part], other_pair + head)

    in1[mine1] = pack1[side]
    for head in range(HEADS):
        @pl.when(place == WORKER3[head])
        def _(head=head):
            in3[me] = pack3[head]

    @pl.when(is2)
    def _():
        work[mine2] = pack2[head2]

    def unit_refs(unit):
        head = lax.div(unit, 2)
        segment = lax.rem(unit, 2)
        return head, segment, pl.ds(pl.multiple_of(DIM * head, DIM), DIM)

    def forward0(unit, carry):
        head, segment, lanes = unit_refs(unit)
        rows = pl.ds(pl.multiple_of(KEYS * segment, KEYS), KEYS)
        key, value = keys[rows, lanes], values[rows, lanes]
        for chunk in range(2):
            start = pl.multiple_of(KEYS * segment + 256 * chunk, 256)
            part = pl.ds(start, 256)
            scores = nt(key, query[part, lanes]) * FACTOR
            row_max = jnp.max(scores, 0, keepdims=True)
            powers = jnp.exp(scores - row_max)
            powers0[unit, :, 256 * chunk : 256 * chunk + 256] = powers
            weights = powers.astype(BF16)
            weighted0[head, :, part] = tn(value, weights)
            products = nt(value, dout[part, lanes])
            products0[unit, :, 256 * chunk : 256 * chunk + 256] = products
            stat0[head, 0:1, part] = row_max
            stat0[head, 1:2, part] = jnp.sum(powers, 0, keepdims=True)
            stat0[head, 2:3, part] = jnp.sum(weights.astype(F32) * products, 0, keepdims=True)
        return carry

    lax.fori_loop(0, 4, forward0, 0)
    for head in range(HEADS):
        off = [offsets[head, level] for level in range(3)]
        column = iota((1, 256), 1)
        target = jnp.where(
            column < 128,
            column * RATES[0] + off[0],
            jnp.where(
                column < 160, (column - 128) * RATES[1] + off[1], (column - 160) * RATES[2] + off[2]
            ),
        )
        spread[head] = jnp.where(iota((TOKENS, 256), 0) == target, 1.0, 0.0).astype(BF16)
        row = iota((128, 1), 0)
        for ref, level in ((sel2, 1), (sel3, 2)):
            target = (row - bases[level]) * RATES[level] + off[level]
            ref[head] = jnp.where(iota((128, TOKENS), 1) == target, 1.0, 0.0).astype(BF16)

    def item_forward(ref, rows, powers_ref, products_ref):
        scores = nt(ref[:, 0:128], ref[rows, 256:384]) * FACTOR
        row_max = jnp.max(scores, 0, keepdims=True)
        powers = jnp.exp(scores - row_max)
        powers_ref[...] = powers
        weights = powers.astype(BF16)
        products = nt(ref[:, 128:256], ref[rows, 384:512])
        products_ref[...] = products
        stats = jnp.concatenate(
            [
                row_max,
                jnp.sum(powers, 0, keepdims=True),
                jnp.sum(weights.astype(F32) * products, 0, keepdims=True),
                jnp.zeros((5, row_max.shape[1]), F32),
            ],
            0,
        )
        return tn(weights, ref[:, 128:256]), stats

    def item_backward(
        ref, rows, powers_ref, products_ref, log_all, delta_all, row_max, log_own, delta_own
    ):
        k_all, q_all, d_all = ref[:, 0:128], ref[:, 256:384], ref[:, 384:512]
        k_own, v_own = ref[rows, 0:128], ref[rows, 128:256]
        probs = powers_ref[...] * jnp.exp(row_max - log_own)
        low = (probs * (products_ref[...] - delta_own)).astype(BF16)
        grad_q = FACTOR * tn(low, k_all)
        probs = jnp.exp(nt(k_own, q_all) * FACTOR - log_all)
        low = (probs * (nt(v_own, d_all) - delta_all)).astype(BF16)
        grad_k = FACTOR * nn(low, q_all)
        grad_v = nn(probs.astype(BF16), d_all)
        return jnp.concatenate([grad_q, grad_k, grad_v], 1)

    rows1 = pl.ds(pl.multiple_of(256 * pair, 256), 256)
    rows2 = pl.ds(pl.multiple_of(256 * half, 256), 256)
    rows3 = pl.ds(pl.multiple_of(128 * x, 128), 128)
    power3 = power_work.at[:, 0:128]
    product3 = product_work.at[:, 0:128]

    @pl.when(is2)
    def _():
        arrived(work.at[pl.ds(0, 352)], recv_in.at[2])
        weighted, stats = item_forward(work, rows2, power_work, product_work)
        stat_own[:, 0:256] = stats
        for i in range(8):
            tile = stats[:, 128 * (i // 4) : 128 * (i // 4) + 128]
            send2[i] = jnp.concatenate([weighted[32 * i : 32 * i + 32], tile], 0)

    @pl.when(is3)
    def _():
        arrived(in3.at[pl.ds(0, 63)], recv_in.at[4])
        both = in3[...].astype(F32)
        work[:, 0:256] = both[:, 0:8].reshape(KEYS, 256).astype(BF16)
        work[:, 256:512] = both[:, 8:16].reshape(KEYS, 256).astype(BF16)
        weighted, stats = item_forward(work, rows3, power3, product3)
        stat_own[:, 0:128] = stats
        for i in range(16):
            send3[i] = jnp.concatenate([weighted[8 * i : 8 * i + 8], stats], 0)

    def returns(src2, dst2, src3, dst3, sems, recv, wait):
        def each(src, dst, sem, recv_sem, device):
            copy = remote(src, dst, sem, recv_sem, device)
            if wait:
                copy.wait_send()
            else:
                copy.start()

        @pl.when(is2)
        def _():
            here = place - 8 * half

            def step(i, carry):
                other = lax.rem(here + i, 8)
                each(src2.at[other], dst2.at[head2], sems.at[i], recv.at[head2], plane + 8 * half + other)
                return carry

            lax.fori_loop(1, 8, step, 0)
            if not wait:
                dst2[head2] = src2[here]

        @pl.when(is3)
        def _():
            def step(i, carry):
                other = lax.rem(place + i, 16)
                each(src3.at[other], dst3.at[head3], sems.at[i], recv.at[2 + head3], plane + other)
                return carry

            lax.fori_loop(1, 16, step, 0)
            if not wait:
                dst3[head3] = src3[place]

    def returned(dst1, dst2, dst3, recv):
        arrived(dst1.at[1 - side], recv.at[4])
        for head in range(HEADS):
            @pl.when(place != worker2(half, head))
            def _(head=head):
                arrived(dst2.at[head], recv.at[head])

            @pl.when(place != WORKER3[head])
            def _(head=head):
                arrived(dst3.at[head], recv.at[2 + head])

    returns(send2, back2, send3, back3, send_back, recv_back, False)

    arrived(in1.at[:, pl.ds(0, 256)], recv_in.at[0])
    weighted, stats = item_forward(in1, rows1, power1, product1)
    stat1[...] = stats
    for i in range(2):
        send1[i] = jnp.concatenate(
            [weighted[128 * i : 128 * i + 128], stats[:, 128 * i : 128 * i + 128]], 0
        )
    send(send1.at[1 - side], back1.at[side], send_back.at[16], recv_back.at[4], partner)
    back1[side] = send1[side]

    returned(back1, back2, back3, recv_back)
    position = iota((1, TOKENS), 1)
    for head in range(HEADS):
        found = (
            select_rows(back1[head, 128:136], sel[head, 0:128]),
            select_rows(back2[head, 32:40], sel2[head]),
            select_rows(back3[head, 8:16], sel3[head]),
        )
        maxima = [stat0[head, 0:1]]
        for level in range(3):
            member = lax.rem(position, RATES[level]) == offsets[head, level]
            maxima.append(jnp.where(member, found[level][0:1], -jnp.inf))
        peak = jnp.maximum(jnp.maximum(maxima[0], maxima[1]), jnp.maximum(maxima[2], maxima[3]))
        factors = [jnp.exp(item - peak) for item in maxima]
        denominator = factors[0] * stat0[head, 1:2]
        for level in range(3):
            denominator += factors[level + 1] * found[level][1:2]
        product = factors[0] * stat0[head, 2:3]
        for level in range(3):
            product += factors[level + 1] * found[level][2:3]
        log_total = peak + jnp.log(denominator)
        inverse = 1.0 / denominator
        rows = jnp.concatenate([log_total, product * inverse, jnp.zeros((6, TOKENS), F32)], 0)
        logs[head] = rows
        shares[head] = jnp.concatenate(
            [item * inverse for item in factors] + [jnp.zeros((4, TOKENS), F32)], 0
        )
        for level, chooser in enumerate((sel[head, 0:128], sel2[head], sel3[head])):
            tiles[level, 2 * head : 2 * head + 2] = select_rows_nt(rows, chooser)[0:2]
    for level in range(3):
        tiles[level, 4:8] = jnp.zeros((4, BLOCK), F32)

    for block in range(4):
        for head in range(HEADS):
            send(tiles.at[2], tiles3.at[me], send_stat.at[2 * block + head], recv_stat.at[2],
                 16 * block + WORKER3[head])
    for i in range(4):
        send(tiles.at[1], tiles2.at[place], send_stat.at[8 + i], recv_stat.at[1],
             plane + worker2(i // 2, i % 2))
    for i in range(1, 4):
        send(tiles.at[0], tiles1.at[y], send_stat.at[11 + i], recv_stat.at[0], group + lax.rem(y + i, 4))
    tiles1[y] = tiles[0]

    @pl.when(is2)
    def _():
        tiles2[place] = tiles[1]

    @pl.when(is3)
    def _():
        tiles3[me] = tiles[2]

    def backward0(unit, carry):
        head, segment, lanes = unit_refs(unit)
        rows = pl.ds(pl.multiple_of(KEYS * segment, KEYS), KEYS)
        key = keys[rows, lanes]
        grad_k = jnp.zeros((KEYS, DIM), F32)
        grad_v = jnp.zeros((KEYS, DIM), F32)
        for chunk in range(2):
            part = pl.ds(pl.multiple_of(KEYS * segment + 256 * chunk, 256), 256)
            rescale = jnp.exp(stat0[head, 0:1, part] - logs[head, 0:1, part])
            probs = powers0[unit, :, 256 * chunk : 256 * chunk + 256] * rescale
            grad_rows = dout[part, lanes]
            products = products0[unit, :, 256 * chunk : 256 * chunk + 256]
            low = (probs * (products - logs[head, 1:2, part])).astype(BF16)
            grad_k += nn(low, query[part, lanes])
            grad_v += nn(probs.astype(BF16), grad_rows)
            dq_out[part, lanes] = (FACTOR * tn(key, low)).T
        dk_out[rows, lanes] = FACTOR * grad_k
        dv_out[rows, lanes] = grad_v
        return carry

    lax.fori_loop(0, 3, backward0, 0)

    def row_blocks(blocks, head):
        first = head == 0
        return (
            [jnp.where(first, tile[0:1], tile[2:3]) for tile in blocks],
            [jnp.where(first, tile[1:2], tile[3:4]) for tile in blocks],
        )

    def pick(rows, block):
        chosen = rows[0]
        for i in range(1, len(rows)):
            chosen = jnp.where(block == i, rows[i], chosen)
        return chosen

    def pairs(rows):
        return [jnp.concatenate(rows[0:2], 1), jnp.concatenate(rows[2:4], 1)]

    @pl.when(is2)
    def _():
        arrived(work.at[pl.ds(0, 128)], recv_in.at[3])
        arrived(tiles2.at[pl.ds(0, 15)], recv_stat.at[1])
        blocks = [jnp.sum(tiles2[4 * i : 4 * i + 4], 0) for i in range(4)]
        log_rows, delta_rows = row_blocks(blocks, head2)
        grads = item_backward(
            work, rows2, power_work, product_work, jnp.concatenate(log_rows, 1), jnp.concatenate(delta_rows, 1),
            stat_own[0:1], pick(pairs(log_rows), half), pick(pairs(delta_rows), half),
        ).astype(BF16)
        for i in range(8):
            grad_send2[i] = grads[32 * i : 32 * i + 32]

    @pl.when(is3)
    def _():
        arrived(tiles3.at[pl.ds(0, 63)], recv_stat.at[2])
        blocks = [jnp.sum(tiles3[16 * i : 16 * i + 16], 0) for i in range(4)]
        log_rows, delta_rows = row_blocks(blocks, head3)
        grads = item_backward(
            work, rows3, power3, product3, jnp.concatenate(log_rows, 1), jnp.concatenate(delta_rows, 1),
            stat_own[0:1, 0:128], pick(log_rows, x), pick(delta_rows, x),
        )
        for i in range(16):
            tile = jnp.concatenate([grads[8 * i : 8 * i + 8], jnp.zeros((8, 3 * DIM), F32)], 0)
            grad_send3[i] = tile.astype(BF16)

    stack1 = stack.at[:, 0:128]
    stack2 = stack.at[:, 128:160]
    stack3 = stack.at[:, 160:176]
    returns(grad_send2, stack2, grad_send3, stack3, send_grad, recv_grad, False)

    arrived(in1.at[pl.ds(0, 256), pl.ds(0, 256)], recv_in.at[1])
    arrived(tiles1.at[pl.ds(0, 3)], recv_stat.at[0])
    log_rows, delta_rows = row_blocks([tiles1[i] for i in range(4)], side)
    grads = item_backward(
        in1, rows1, power1, product1,
        jnp.concatenate(log_rows, 1), jnp.concatenate(delta_rows, 1),
        stat1[0:1], pick(pairs(log_rows), pair), pick(pairs(delta_rows), pair),
    ).astype(BF16)
    for i in range(2):
        grad_send1[i] = grads[128 * i : 128 * i + 128]
    send(grad_send1.at[1 - side], stack1.at[side], send_grad.at[16], recv_grad.at[4], partner)
    stack1[side] = grad_send1[side]

    lax.fori_loop(3, 4, backward0, 0)
    for head in range(HEADS):
        lane_shares = select_rows_nt(shares[head], sel[head])
        lane = iota((1, 256), 1)
        share = jnp.where(
            lane < 128, lane_shares[1:2], jnp.where(lane < 160, lane_shares[2:3], lane_shares[3:4])
        )
        stacked = jnp.concatenate(
            [back1[head, 0:128], back2[head, 0:32], back3[head, 0:8], jnp.zeros((88, DIM), F32)], 0
        ).T * share
        high = stacked.astype(BF16)
        low = (stacked - high.astype(F32)).astype(BF16)
        attended = shares[head, 0:1] * weighted0[head] + nn(high, sel[head]) + nn(low, sel[head])
        att_out[:, DIM * head : DIM * head + DIM] = attended.T

    stack_out[:, 176:256] = jnp.zeros((2, 80, 3 * DIM), BF16)
    returned(stack1, stack2, stack3, recv_grad)
    stack_out[:, 0:176] = stack[...]

    for device, copy in pending:
        @pl.when(device != me)
        def _(copy=copy):
            copy.wait_send()
    returns(send2, back2, send3, back3, send_back, recv_back, True)
    returns(grad_send2, stack2, grad_send3, stack3, send_grad, recv_grad, True)


def finish(att, dq, dk, dv, spread, stack, att_out, dq_out, dk_out, dv_out, full, sems):
    first = pltpu.make_async_copy(att, att_out, sems.at[12])
    first.start()
    copies = [first]
    for part in range(4):
        rows = slice(256 * part, 256 * part + 256)
        for head in range(HEADS):
            lanes = slice(DIM * head, DIM * head + DIM)
            added = nn(spread[head, rows], stack[head])
            for i, ref in enumerate((dq, dk, dv)):
                full[i, rows, lanes] = ref[rows, lanes] + added[:, DIM * i : DIM * i + DIM]
        for i, out in enumerate((dq_out, dk_out, dv_out)):
            copies.append(
                pltpu.make_async_copy(full.at[i, rows], out.at[rows], sems.at[3 * part + i])
            )
            copies[-1].start()
    for copy in copies:
        copy.wait()


def body(query, keys, values, grad_out, offsets):
    vmem = pl.BlockSpec(memory_space=pltpu.VMEM)
    hbm = pl.BlockSpec(memory_space=pltpu.HBM)
    out = jax.ShapeDtypeStruct((TOKENS, HEADS * DIM), F32)
    dma = pltpu.SemaphoreType.DMA
    held = pltpu.VMEM((TOKENS, HEADS * DIM), BF16)
    pinned = [
        pltpu.with_memory_space_constraint(item, pltpu.HBM)
        for item in (offsets.T, query, keys, values, grad_out)
    ]
    parts = pl.pallas_call(
        kernel,
        out_shape=(
            out, out, out, out,
            jax.ShapeDtypeStruct((2, TOKENS, 256), BF16),
            jax.ShapeDtypeStruct((2, 256, 3 * DIM), BF16),
        ),
        in_specs=[hbm] * 5,
        out_specs=(vmem,) * 6,
        scratch_shapes=[
            pltpu.SMEM((HEADS, 3), jnp.int32),
            held, held, held, held,
            pltpu.VMEM((2, 256, TOKENS), BF16),
            pltpu.VMEM((2, 128, TOKENS), BF16),
            pltpu.VMEM((2, 128, TOKENS), BF16),
            pltpu.VMEM((4, KEYS, KEYS), F32),
            pltpu.VMEM((4, KEYS, KEYS), F32),
            pltpu.VMEM((2, 8, TOKENS), F32),
            pltpu.VMEM((2, DIM, TOKENS), F32),
            pltpu.VMEM((2, 8, TOKENS), F32),
            pltpu.VMEM((2, 8, TOKENS), F32),
            pltpu.VMEM((2, 128, 512), BF16),
            pltpu.VMEM((2, 32, 512), BF16),
            pltpu.VMEM((2, 16, 256), BF16),
            pltpu.VMEM((512, 512), BF16),
            pltpu.VMEM((512, 512), BF16),
            pltpu.VMEM((64, 16, 256), BF16),
            pltpu.VMEM((512, 256), F32),
            pltpu.VMEM((512, 256), F32),
            pltpu.VMEM((512, 256), F32),
            pltpu.VMEM((512, 256), F32),
            pltpu.VMEM((8, 256), F32),
            pltpu.VMEM((8, 256), F32),
            pltpu.VMEM((2, 136, 128), F32),
            pltpu.VMEM((8, 40, 128), F32),
            pltpu.VMEM((16, 16, 128), F32),
            pltpu.VMEM((2, 136, 128), F32),
            pltpu.VMEM((2, 40, 128), F32),
            pltpu.VMEM((2, 16, 128), F32),
            pltpu.VMEM((2, 128, 384), BF16),
            pltpu.VMEM((8, 32, 384), BF16),
            pltpu.VMEM((16, 16, 384), BF16),
            pltpu.VMEM((2, 176, 384), BF16),
            pltpu.VMEM((3, 8, 128), F32),
            pltpu.VMEM((4, 8, 128), F32),
            pltpu.VMEM((16, 8, 128), F32),
            pltpu.VMEM((64, 8, 128), F32),
            dma((5,)),
            dma((19,)),
            dma((17,)),
            dma((15,)),
            dma((17,)),
            dma((5,)),
            dma((5,)),
            dma((3,)),
            dma((5,)),
        ],
        compiler_params=pltpu.CompilerParams(
            collective_id=0, has_side_effects=True, vmem_limit_bytes=32 * 2**20
        ),
    )(*pinned)
    return pl.pallas_call(
        finish,
        out_shape=(out, out, out, out),
        in_specs=[vmem] * 6,
        out_specs=(hbm,) * 4,
        scratch_shapes=[pltpu.VMEM((3, TOKENS, HEADS * DIM), F32), dma((13,))],
        compiler_params=pltpu.CompilerParams(vmem_limit_bytes=16 * 2**20),
    )(*parts)


def solution(mesh):
    spec = P("seq", "rep")
    return jax.shard_map(
        body,
        mesh=mesh,
        in_specs=(spec, spec, spec, spec, P(None, "rep")),
        out_specs=(spec, spec, spec, spec),
        check_vma=False,
    )
```

```python
import jax
import jax.numpy as jnp
from jax import lax
from jax.experimental import pallas as pl
from jax.experimental.pallas import tpu as pltpu
from jax.sharding import PartitionSpec as P

HEADS = 2
KEYS = 512
DIM = 128
TOKENS = 1024
BLOCK = 128
RATES = (8, 32, 128)
FACTOR = DIM**-0.5
MESH = pl.DeviceIdType.MESH
F32 = jnp.float32
BF16 = jnp.bfloat16


def dot(a, b, dims):
    return lax.dot_general(a, b, (dims, ((), ())), preferred_element_type=F32)


def nn(a, b):
    return dot(a, b, ((1,), (0,)))


def nt(a, b):
    return dot(a, b, ((1,), (1,)))


def tn(a, b):
    return dot(a, b, ((0,), (0,)))


def split3(a):
    high = a.astype(BF16)
    rest = a - high.astype(F32)
    middle = rest.astype(BF16)
    low = (rest - middle.astype(F32)).astype(BF16)
    return jnp.concatenate([high.astype(F32), middle.astype(F32), low.astype(F32)], 0).astype(BF16)


def join3(a):
    rows = a.shape[0] // 3
    return a[:rows] + a[rows : 2 * rows] + a[2 * rows :]


def select_rows(stats, chooser):
    return join3(nn(split3(stats), chooser))


def select_rows_nt(stats, chooser):
    return join3(nt(split3(stats), chooser))


def iota(shape, dim):
    return lax.broadcasted_iota(jnp.int32, shape, dim)


def kernel(
    offsets_hbm, query_hbm, keys_hbm, values_hbm, dout_hbm,
    att_out, dq_out, dk_out, dv_out, spread, stack_out,
    offsets, query, keys, values, dout,
    sel, sel2, sel3, powers0, products0, shares, weighted0, stat0, logs,
    pack1, pack2, pack3, work, in3, power_work, product_work, stat_work, weighted_work,
    stat_send, send2, send3, back_stat1, back_rows1, back2, back3, grad_work, grad_send3, stack,
    tiles, tiles1, tiles2, tiles3,
    load_sem, send_in, send_back, send_back1, send_rows1, send_stat, send_grad, send_grad1,
    recv_in, recv_back, recv_back1, recv_rows1, recv_stat, recv_grad, recv_grad1,
):
    me = lax.axis_index("seq")
    y = lax.rem(me, 4)
    z = lax.rem(lax.div(me, 4), 4)
    x = lax.div(me, 16)
    place = lax.rem(me, 16)
    plane = me - place
    group = me - y
    core = lax.rem(lax.axis_index("rep"), 2)
    worker1 = (core, 2 + core)
    worker2 = (5 + core, 9 + core)
    worker3 = (7 - 3 * core, 11 - 3 * core)
    is1 = (y == worker1[0]) | (y == worker1[1])
    is2 = (place == worker2[0]) | (place == worker2[1])
    is3 = (place == worker3[0]) | (place == worker3[1])
    head12 = jnp.where((is1 & (y == worker1[0])) | (is2 & (place == worker2[0])), 0, 1)
    head3 = jnp.where(place == worker3[0], 0, 1)
    one2 = jnp.where(is2, 1, 0)
    one3 = jnp.where(is3, 1, 0)

    load_offsets = pltpu.make_async_copy(offsets_hbm, offsets, load_sem.at[4])
    load_offsets.start()
    loads = []
    for i, (source, held) in enumerate(
        ((query_hbm, query), (keys_hbm, keys), (values_hbm, values), (dout_hbm, dout))
    ):
        loads.append(pltpu.make_async_copy(source, held, load_sem.at[i]))
        loads[-1].start()

    barrier = pltpu.get_barrier_semaphore()

    def greet(device):
        pl.semaphore_signal(barrier, inc=1, device_id={"seq": device}, device_id_type=MESH)

    @pl.when(is3)
    def _():
        def step(i, carry):
            greet(lax.rem(me + i, 64))
            return carry

        lax.fori_loop(1, 64, step, 0)

    @pl.when(is2)
    def _():
        def step(i, carry):
            greet(plane + lax.rem(place + i, 16))
            return carry

        lax.fori_loop(1, 16, step, 0)

    for spot in worker2 + worker3:
        @pl.when(place != spot)
        def _(spot=spot):
            greet(plane + spot)

    for i in range(1, 4):
        greet(group + lax.rem(y + i, 4))

    bases = (0, 32 * y, 8 * place)
    load_offsets.wait()
    for head in range(HEADS):
        off = [offsets[head, level] for level in range(3)]

        def target(index, off=off):
            return jnp.where(
                index < 128,
                index * RATES[0] + off[0],
                jnp.where(
                    index < 160, (index - 128) * RATES[1] + off[1], (index - 160) * RATES[2] + off[2]
                ),
            )

        sel[head] = jnp.where(
            iota((256, TOKENS), 1) == target(iota((256, 1), 0)), 1.0, 0.0
        ).astype(BF16)
    for load in loads:
        load.wait()
    for head in range(HEADS):
        lanes = slice(DIM * head, DIM * head + DIM)
        chooser = sel[head, 0:176]
        first = nn(chooser, jnp.concatenate([keys[:, lanes], values[:, lanes]], 1))
        second = nn(chooser, jnp.concatenate([query[:, lanes], dout[:, lanes]], 1))
        pack1[head, :, 0:256] = first[:128].astype(BF16)
        pack1[head, :, 256:512] = second[:128].astype(BF16)
        pack2[head, :, 0:256] = first[128:160].astype(BF16)
        pack2[head, :, 256:512] = second[128:160].astype(BF16)
        pack3[head] = jnp.concatenate([first[160:168], second[160:168]], 0).astype(BF16)

    pl.semaphore_wait(barrier, 3 + (2 - one2) + (8 - one3) + 15 * one3 + 15 * one2)

    def remote(src, dst, send_sem, recv_sem, device):
        return pltpu.make_async_remote_copy(
            src_ref=src, dst_ref=dst, send_sem=send_sem, recv_sem=recv_sem,
            device_id={"seq": device}, device_id_type=MESH,
        )

    pending = []

    def send(src, dst, send_sem, recv_sem, device):
        copy = remote(src, dst, send_sem, recv_sem, device)
        pending.append((device, copy))

        @pl.when(device != me)
        def _():
            copy.start()

    def arrived(ref, sem):
        pltpu.make_async_copy(ref, ref, sem).wait()

    mine1 = pl.ds(pl.multiple_of(128 * y, 128), 128)
    mine2 = pl.ds(pl.multiple_of(32 * place, 32), 32)
    for block in range(4):
        for head in range(HEADS):
            send(pack3.at[head], in3.at[me], send_in.at[2 * block + head], recv_in.at[2],
                 16 * block + worker3[head])
    for head in range(HEADS):
        send(pack2.at[head], work.at[mine2], send_in.at[8 + head], recv_in.at[1],
             plane + worker2[head])
    for head in range(HEADS):
        send(pack1.at[head], work.at[mine1], send_in.at[10 + head], recv_in.at[0],
             group + worker1[head])

    @pl.when(is1)
    def _():
        work[mine1] = pack1[head12]

    @pl.when(is2)
    def _():
        work[mine2] = pack2[head12]

    @pl.when(is3)
    def _():
        in3[me] = pack3[head3]

    def unit_refs(unit):
        head = lax.div(unit, 2)
        segment = lax.rem(unit, 2)
        return head, segment, pl.ds(pl.multiple_of(DIM * head, DIM), DIM)

    def forward0(unit, carry):
        head, segment, lanes = unit_refs(unit)
        rows = pl.ds(pl.multiple_of(KEYS * segment, KEYS), KEYS)
        key, value = keys[rows, lanes], values[rows, lanes]
        for chunk in range(2):
            start = pl.multiple_of(KEYS * segment + 256 * chunk, 256)
            part = pl.ds(start, 256)
            scores = nt(key, query[part, lanes]) * FACTOR
            row_max = jnp.max(scores, 0, keepdims=True)
            powers = jnp.exp(scores - row_max)
            powers0[unit, :, 256 * chunk : 256 * chunk + 256] = powers
            weights = powers.astype(BF16)
            weighted0[head, :, part] = tn(value, weights)
            products = nt(value, dout[part, lanes])
            products0[unit, :, 256 * chunk : 256 * chunk + 256] = products
            stat0[head, 0:1, part] = row_max
            stat0[head, 1:2, part] = jnp.sum(powers, 0, keepdims=True)
            stat0[head, 2:3, part] = jnp.sum(weights.astype(F32) * products, 0, keepdims=True)
        return carry

    lax.fori_loop(0, 4, forward0, 0)
    for head in range(HEADS):
        off = [offsets[head, level] for level in range(3)]
        column = iota((1, 256), 1)
        target = jnp.where(
            column < 128,
            column * RATES[0] + off[0],
            jnp.where(
                column < 160, (column - 128) * RATES[1] + off[1], (column - 160) * RATES[2] + off[2]
            ),
        )
        spread[head] = jnp.where(iota((TOKENS, 256), 0) == target, 1.0, 0.0).astype(BF16)
        row = iota((128, 1), 0)
        for ref, level in ((sel2, 1), (sel3, 2)):
            target = (row - bases[level]) * RATES[level] + off[level]
            ref[head] = jnp.where(iota((128, TOKENS), 1) == target, 1.0, 0.0).astype(BF16)

    def whole_forward():
        for chunk in range(2):
            part = slice(256 * chunk, 256 * chunk + 256)
            scores = nt(work[:, 0:128], work[part, 256:384]) * FACTOR
            row_max = jnp.max(scores, 0, keepdims=True)
            powers = jnp.exp(scores - row_max)
            weights = powers.astype(BF16)
            products = nt(work[:, 128:256], work[part, 384:512])
            power_work[:, part] = powers
            product_work[:, part] = products
            stat_work[:, part] = jnp.concatenate(
                [
                    row_max,
                    jnp.sum(powers, 0, keepdims=True),
                    jnp.sum(weights.astype(F32) * products, 0, keepdims=True),
                    jnp.zeros((5, 256), F32),
                ],
                0,
            )
            weighted_work[part] = tn(weights, work[:, 128:256])

    def whole_backward(log_row, delta_row):
        grad_k = jnp.zeros((KEYS, DIM), F32)
        grad_v = jnp.zeros((KEYS, DIM), F32)
        for chunk in range(2):
            part = slice(256 * chunk, 256 * chunk + 256)
            log_part, delta_part = log_row[:, part], delta_row[:, part]
            probs = power_work[:, part] * jnp.exp(stat_work[0:1, part] - log_part)
            low = (probs * (product_work[:, part] - delta_part)).astype(BF16)
            grad_work[part, 0:128] = (FACTOR * tn(low, work[:, 0:128])).astype(BF16)
            grad_k += nn(low, work[part, 256:384])
            grad_v += nn(probs.astype(BF16), work[part, 384:512])
        grad_work[:, 128:256] = (FACTOR * grad_k).astype(BF16)
        grad_work[:, 256:384] = grad_v.astype(BF16)

    rows3 = pl.ds(pl.multiple_of(128 * x, 128), 128)

    def block_forward():
        scores = nt(work[:, 0:128], work[rows3, 256:384]) * FACTOR
        row_max = jnp.max(scores, 0, keepdims=True)
        powers = jnp.exp(scores - row_max)
        weights = powers.astype(BF16)
        products = nt(work[:, 128:256], work[rows3, 384:512])
        power_work[:, 0:128] = powers
        product_work[:, 0:128] = products
        stats = jnp.concatenate(
            [
                row_max,
                jnp.sum(powers, 0, keepdims=True),
                jnp.sum(weights.astype(F32) * products, 0, keepdims=True),
                jnp.zeros((5, BLOCK), F32),
            ],
            0,
        )
        stat_work[:, 0:128] = stats
        return tn(weights, work[:, 128:256]), stats

    def block_backward(log_all, delta_all, log_own, delta_own):
        k_all, q_all, d_all = work[:, 0:128], work[:, 256:384], work[:, 384:512]
        k_own, v_own = work[rows3, 0:128], work[rows3, 128:256]
        probs = power_work[:, 0:128] * jnp.exp(stat_work[0:1, 0:128] - log_own)
        low = (probs * (product_work[:, 0:128] - delta_own)).astype(BF16)
        grad_q = FACTOR * tn(low, k_all)
        probs = jnp.exp(nt(k_own, q_all) * FACTOR - log_all)
        low = (probs * (nt(v_own, d_all) - delta_all)).astype(BF16)
        grad_k = FACTOR * nn(low, q_all)
        grad_v = nn(probs.astype(BF16), d_all)
        return jnp.concatenate([grad_q, grad_k, grad_v], 1)

    def rows_of(ref, index, count):
        return ref.at[pl.ds(pl.multiple_of(count * index, count), count)]

    def returns(wait, src1, dst1, sem1, recv1, src2, dst2, src3, dst3, sems, recv):
        def each(src, dst, sem, recv_sem, device):
            copy = remote(src, dst, sem, recv_sem, device)
            if wait:
                copy.wait_send()
            else:
                copy.start()

        if src1 is not None:
            @pl.when(is1)
            def _():
                for i in range(1, 4):
                    other = lax.rem(y + i, 4)
                    each(src1(other), dst1(head12), sem1.at[i], recv1.at[head12], group + other)

        if src2 is not None:
            @pl.when(is2)
            def _():
                def step(i, carry):
                    other = lax.rem(place + i, 16)
                    each(src2(other), dst2(head12), sems.at[i], recv.at[head12], plane + other)
                    return carry

                lax.fori_loop(1, 16, step, 0)

            @pl.when(is3)
            def _():
                def step(i, carry):
                    other = lax.rem(place + i, 16)
                    each(src3(other), dst3(head3), sems.at[i], recv.at[2 + head3], plane + other)
                    return carry

                lax.fori_loop(1, 16, step, 0)

    def back(wait):
        returns(
            wait,
            lambda i: stat_send.at[i], lambda h: back_stat1.at[h], send_back1, recv_back1,
            lambda i: send2.at[i], lambda h: back2.at[h],
            lambda i: send3.at[i], lambda h: back3.at[h], send_back, recv_back,
        )
        returns(
            wait,
            lambda i: rows_of(weighted_work, i, 128), lambda h: back_rows1.at[h], send_rows1, recv_rows1,
            None, None, None, None, None, None,
        )

    def grads_back(wait):
        returns(
            wait,
            lambda i: rows_of(grad_work, i, 128), lambda h: stack.at[h, pl.ds(0, 128)], send_grad1, recv_grad1,
            lambda i: rows_of(grad_work, i, 32), lambda h: stack.at[h, pl.ds(128, 32)],
            lambda i: grad_send3.at[i], lambda h: stack.at[h, pl.ds(160, 16)], send_grad, recv_grad,
        )

    def returned1(dst, recv):
        for head in range(HEADS):
            @pl.when(y != worker1[head])
            def _(head=head):
                arrived(dst(head), recv.at[head])

    def returned23(dst2, dst3, recv):
        for head in range(HEADS):
            @pl.when(place != worker2[head])
            def _(head=head):
                arrived(dst2(head), recv.at[head])

            @pl.when(place != worker3[head])
            def _(head=head):
                arrived(dst3(head), recv.at[2 + head])

    @pl.when(is1)
    def _():
        arrived(work.at[pl.ds(0, 384)], recv_in.at[0])

    @pl.when(is2)
    def _():
        arrived(work.at[pl.ds(0, 480)], recv_in.at[1])

    @pl.when(is3)
    def _():
        arrived(in3.at[pl.ds(0, 63)], recv_in.at[2])
        both = in3[...].astype(F32)
        work[:, 0:256] = both[:, 0:8].reshape(KEYS, 256).astype(BF16)
        work[:, 256:512] = both[:, 8:16].reshape(KEYS, 256).astype(BF16)
        weighted, stats = block_forward()
        for i in range(16):
            send3[i] = jnp.concatenate([weighted[8 * i : 8 * i + 8], stats], 0)
        back3[head3] = send3[place]

    @pl.when(is1 | is2)
    def _():
        whole_forward()
        for i in range(4):
            stat_send[i] = stat_work[:, 128 * i : 128 * i + 128]

        @pl.when(is2)
        def _():
            for i in range(16):
                send2[i, 0:32] = weighted_work[32 * i : 32 * i + 32]
                send2[i, 32:40] = stat_send[i // 4]
            back2[head12] = send2[place]

        @pl.when(is1)
        def _():
            back_stat1[head12] = stat_send[y]
            back_rows1[head12] = weighted_work[mine1]

    back(False)

    returned1(lambda h: back_stat1.at[h], recv_back1)
    returned23(lambda h: back2.at[h], lambda h: back3.at[h], recv_back)
    position = iota((1, TOKENS), 1)
    for head in range(HEADS):
        found = (
            select_rows(back_stat1[head], sel[head, 0:128]),
            select_rows(back2[head, 32:40], sel2[head]),
            select_rows(back3[head, 8:16], sel3[head]),
        )
        maxima = [stat0[head, 0:1]]
        for level in range(3):
            member = lax.rem(position, RATES[level]) == offsets[head, level]
            maxima.append(jnp.where(member, found[level][0:1], -jnp.inf))
        peak = jnp.maximum(jnp.maximum(maxima[0], maxima[1]), jnp.maximum(maxima[2], maxima[3]))
        factors = [jnp.exp(item - peak) for item in maxima]
        denominator = factors[0] * stat0[head, 1:2]
        for level in range(3):
            denominator += factors[level + 1] * found[level][1:2]
        product = factors[0] * stat0[head, 2:3]
        for level in range(3):
            product += factors[level + 1] * found[level][2:3]
        log_total = peak + jnp.log(denominator)
        inverse = 1.0 / denominator
        rows = jnp.concatenate([log_total, product * inverse, jnp.zeros((6, TOKENS), F32)], 0)
        logs[head] = rows
        shares[head] = jnp.concatenate(
            [item * inverse for item in factors] + [jnp.zeros((4, TOKENS), F32)], 0
        )
        for level, chooser in enumerate((sel[head, 0:128], sel2[head], sel3[head])):
            tiles[level, 2 * head : 2 * head + 2] = select_rows_nt(rows, chooser)[0:2]
    for level in range(3):
        tiles[level, 4:8] = jnp.zeros((4, BLOCK), F32)

    for block in range(4):
        for head in range(HEADS):
            send(tiles.at[2], tiles3.at[me], send_stat.at[2 * block + head], recv_stat.at[2],
                 16 * block + worker3[head])
    for head in range(HEADS):
        send(tiles.at[1], tiles2.at[place], send_stat.at[8 + head], recv_stat.at[1],
             plane + worker2[head])
    for head in range(HEADS):
        send(tiles.at[0], tiles1.at[y], send_stat.at[10 + head], recv_stat.at[0],
             group + worker1[head])

    @pl.when(is1)
    def _():
        tiles1[y] = tiles[0]

    @pl.when(is2)
    def _():
        tiles2[place] = tiles[1]

    @pl.when(is3)
    def _():
        tiles3[me] = tiles[2]

    def backward0(unit, carry):
        head, segment, lanes = unit_refs(unit)
        rows = pl.ds(pl.multiple_of(KEYS * segment, KEYS), KEYS)
        key = keys[rows, lanes]
        grad_k = jnp.zeros((KEYS, DIM), F32)
        grad_v = jnp.zeros((KEYS, DIM), F32)
        for chunk in range(2):
            part = pl.ds(pl.multiple_of(KEYS * segment + 256 * chunk, 256), 256)
            rescale = jnp.exp(stat0[head, 0:1, part] - logs[head, 0:1, part])
            probs = powers0[unit, :, 256 * chunk : 256 * chunk + 256] * rescale
            grad_rows = dout[part, lanes]
            products = products0[unit, :, 256 * chunk : 256 * chunk + 256]
            low = (probs * (products - logs[head, 1:2, part])).astype(BF16)
            grad_k += nn(low, query[part, lanes])
            grad_v += nn(probs.astype(BF16), grad_rows)
            dq_out[part, lanes] = (FACTOR * tn(key, low)).T
        dk_out[rows, lanes] = FACTOR * grad_k
        dv_out[rows, lanes] = grad_v
        return carry

    lax.fori_loop(0, 3, backward0, 0)

    def row_blocks(blocks, head):
        first = head == 0
        return (
            [jnp.where(first, tile[0:1], tile[2:3]) for tile in blocks],
            [jnp.where(first, tile[1:2], tile[3:4]) for tile in blocks],
        )

    def pick(rows, block):
        chosen = rows[0]
        for i in range(1, len(rows)):
            chosen = jnp.where(block == i, rows[i], chosen)
        return chosen

    @pl.when(is2)
    def _():
        arrived(tiles2.at[pl.ds(0, 15)], recv_stat.at[1])
        for i in range(4):
            tiles1[i] = jnp.sum(tiles2[4 * i : 4 * i + 4], 0)

    @pl.when(is1)
    def _():
        arrived(tiles1.at[pl.ds(0, 3)], recv_stat.at[0])

    @pl.when(is1 | is2)
    def _():
        log_rows, delta_rows = row_blocks([tiles1[i] for i in range(4)], head12)
        whole_backward(jnp.concatenate(log_rows, 1), jnp.concatenate(delta_rows, 1))

        @pl.when(is2)
        def _():
            stack[head12, 128:160] = grad_work[mine2]

        @pl.when(is1)
        def _():
            stack[head12, 0:128] = grad_work[mine1]

    @pl.when(is3)
    def _():
        arrived(tiles3.at[pl.ds(0, 63)], recv_stat.at[2])
        blocks = [jnp.sum(tiles3[16 * i : 16 * i + 16], 0) for i in range(4)]
        log_rows, delta_rows = row_blocks(blocks, head3)
        grads = block_backward(
            jnp.concatenate(log_rows, 1), jnp.concatenate(delta_rows, 1),
            pick(log_rows, x), pick(delta_rows, x),
        )
        for i in range(16):
            tile = jnp.concatenate([grads[8 * i : 8 * i + 8], jnp.zeros((8, 3 * DIM), F32)], 0)
            grad_send3[i] = tile.astype(BF16)
        stack[head3, 160:176] = grad_send3[place]

    grads_back(False)

    lax.fori_loop(3, 4, backward0, 0)
    returned1(lambda h: back_rows1.at[h], recv_rows1)
    for head in range(HEADS):
        lane_shares = select_rows_nt(shares[head], sel[head])
        lane = iota((1, 256), 1)
        share = jnp.where(
            lane < 128, lane_shares[1:2], jnp.where(lane < 160, lane_shares[2:3], lane_shares[3:4])
        )
        stacked = jnp.concatenate(
            [back_rows1[head], back2[head, 0:32], back3[head, 0:8], jnp.zeros((88, DIM), F32)], 0
        ).T * share
        high = stacked.astype(BF16)
        low = (stacked - high.astype(F32)).astype(BF16)
        attended = shares[head, 0:1] * weighted0[head] + nn(high, sel[head]) + nn(low, sel[head])
        att_out[:, DIM * head : DIM * head + DIM] = attended.T

    stack_out[:, 176:256] = jnp.zeros((2, 80, 3 * DIM), BF16)
    returned1(lambda h: stack.at[h, pl.ds(0, 128)], recv_grad1)
    returned23(
        lambda h: stack.at[h, pl.ds(128, 32)], lambda h: stack.at[h, pl.ds(160, 16)], recv_grad
    )
    stack_out[:, 0:176] = stack[...]

    for device, copy in pending:
        @pl.when(device != me)
        def _(copy=copy):
            copy.wait_send()
    back(True)
    grads_back(True)


def finish(att, dq, dk, dv, spread, stack, att_out, dq_out, dk_out, dv_out, full, sems):
    first = pltpu.make_async_copy(att, att_out, sems.at[12])
    first.start()
    copies = [first]
    for part in range(4):
        rows = slice(256 * part, 256 * part + 256)
        for head in range(HEADS):
            lanes = slice(DIM * head, DIM * head + DIM)
            added = nn(spread[head, rows], stack[head])
            for i, ref in enumerate((dq, dk, dv)):
                full[i, rows, lanes] = ref[rows, lanes] + added[:, DIM * i : DIM * i + DIM]
        for i, out in enumerate((dq_out, dk_out, dv_out)):
            copies.append(
                pltpu.make_async_copy(full.at[i, rows], out.at[rows], sems.at[3 * part + i])
            )
            copies[-1].start()
    for copy in copies:
        copy.wait()


def body(query, keys, values, grad_out, offsets):
    vmem = pl.BlockSpec(memory_space=pltpu.VMEM)
    hbm = pl.BlockSpec(memory_space=pltpu.HBM)
    out = jax.ShapeDtypeStruct((TOKENS, HEADS * DIM), F32)
    dma = pltpu.SemaphoreType.DMA
    held = pltpu.VMEM((TOKENS, HEADS * DIM), BF16)
    pinned = [
        pltpu.with_memory_space_constraint(item, pltpu.HBM)
        for item in (offsets.T, query, keys, values, grad_out)
    ]
    parts = pl.pallas_call(
        kernel,
        out_shape=(
            out, out, out, out,
            jax.ShapeDtypeStruct((2, TOKENS, 256), BF16),
            jax.ShapeDtypeStruct((2, 256, 3 * DIM), BF16),
        ),
        in_specs=[hbm] * 5,
        out_specs=(vmem,) * 6,
        scratch_shapes=[
            pltpu.SMEM((HEADS, 3), jnp.int32),
            held, held, held, held,
            pltpu.VMEM((2, 256, TOKENS), BF16),
            pltpu.VMEM((2, 128, TOKENS), BF16),
            pltpu.VMEM((2, 128, TOKENS), BF16),
            pltpu.VMEM((4, KEYS, KEYS), F32),
            pltpu.VMEM((4, KEYS, KEYS), F32),
            pltpu.VMEM((2, 8, TOKENS), F32),
            pltpu.VMEM((2, DIM, TOKENS), F32),
            pltpu.VMEM((2, 8, TOKENS), F32),
            pltpu.VMEM((2, 8, TOKENS), F32),
            pltpu.VMEM((2, 128, 512), BF16),
            pltpu.VMEM((2, 32, 512), BF16),
            pltpu.VMEM((2, 16, 256), BF16),
            pltpu.VMEM((512, 512), BF16),
            pltpu.VMEM((64, 16, 256), BF16),
            pltpu.VMEM((512, 512), F32),
            pltpu.VMEM((512, 512), F32),
            pltpu.VMEM((8, 512), F32),
            pltpu.VMEM((512, 128), F32),
            pltpu.VMEM((4, 8, 128), F32),
            pltpu.VMEM((16, 40, 128), F32),
            pltpu.VMEM((16, 16, 128), F32),
            pltpu.VMEM((2, 8, 128), F32),
            pltpu.VMEM((2, 128, 128), F32),
            pltpu.VMEM((2, 40, 128), F32),
            pltpu.VMEM((2, 16, 128), F32),
            pltpu.VMEM((512, 384), BF16),
            pltpu.VMEM((16, 16, 384), BF16),
            pltpu.VMEM((2, 176, 384), BF16),
            pltpu.VMEM((3, 8, 128), F32),
            pltpu.VMEM((4, 8, 128), F32),
            pltpu.VMEM((16, 8, 128), F32),
            pltpu.VMEM((64, 8, 128), F32),
            dma((5,)),
            dma((12,)),
            dma((16,)),
            dma((4,)),
            dma((4,)),
            dma((12,)),
            dma((16,)),
            dma((4,)),
            dma((3,)),
            dma((4,)),
            dma((2,)),
            dma((2,)),
            dma((3,)),
            dma((4,)),
            dma((2,)),
        ],
        compiler_params=pltpu.CompilerParams(
            collective_id=0, has_side_effects=True, vmem_limit_bytes=32 * 2**20
        ),
    )(*pinned)
    return pl.pallas_call(
        finish,
        out_shape=(out, out, out, out),
        in_specs=[vmem] * 6,
        out_specs=(hbm,) * 4,
        scratch_shapes=[pltpu.VMEM((3, TOKENS, HEADS * DIM), F32), dma((13,))],
        compiler_params=pltpu.CompilerParams(vmem_limit_bytes=16 * 2**20),
    )(*parts)


def solution(mesh):
    spec = P("seq", "rep")
    return jax.shard_map(
        body,
        mesh=mesh,
        in_specs=(spec, spec, spec, spec, P(None, "rep")),
        out_specs=(spec, spec, spec, spec),
        check_vma=False,
    )
```

```python
import jax
import jax.numpy as jnp
from jax import lax
from jax.experimental import pallas as pl
from jax.experimental.pallas import tpu as pltpu
from jax.sharding import PartitionSpec as P

HEADS = 2
KEYS = 512
DIM = 128
TOKENS = 1024
BLOCK = 128
RATES = (8, 32, 128)
FACTOR = DIM**-0.5
MESH = pl.DeviceIdType.MESH
F32 = jnp.float32
BF16 = jnp.bfloat16


def dot(a, b, dims):
    return lax.dot_general(a, b, (dims, ((), ())), preferred_element_type=F32)


def nn(a, b):
    return dot(a, b, ((1,), (0,)))


def nt(a, b):
    return dot(a, b, ((1,), (1,)))


def tn(a, b):
    return dot(a, b, ((0,), (0,)))


def split3(a):
    high = a.astype(BF16)
    rest = a - high.astype(F32)
    middle = rest.astype(BF16)
    low = (rest - middle.astype(F32)).astype(BF16)
    return jnp.concatenate([high.astype(F32), middle.astype(F32), low.astype(F32)], 0).astype(BF16)


def join3(a):
    rows = a.shape[0] // 3
    return a[:rows] + a[rows : 2 * rows] + a[2 * rows :]


def select_rows(stats, chooser):
    return join3(nn(split3(stats), chooser))


def select_rows_nt(stats, chooser):
    return join3(nt(split3(stats), chooser))


def iota(shape, dim):
    return lax.broadcasted_iota(jnp.int32, shape, dim)


def kernel(
    offsets_hbm, query_hbm, keys_hbm, values_hbm, dout_hbm,
    att_out, dq_out, dk_out, dv_out, spread, stack_out,
    offsets, query, keys, values, dout,
    sel, sel2, sel3, powers0, products0, shares, weighted0, stat0, logs,
    pack1, pack2, pack3, work, in3, power_work, product_work, stat_work, weighted_work,
    stat_send, send2, send3, back_stat1, back_rows1, back2, back3, grad_work, grad_send3, stack,
    tiles, tiles1, tiles2, tiles3, shared, swap_send, swap1, swap2, swap3,
    load_sem, send_in, send_back, send_back1, send_rows1, send_stat, send_grad, send_grad1,
    recv_in, recv_back, recv_back1, recv_rows1, recv_stat, recv_grad, recv_grad1, send_swap, recv_swap,
):
    me = lax.axis_index("seq")
    y = lax.rem(me, 4)
    z = lax.rem(lax.div(me, 4), 4)
    x = lax.div(me, 16)
    place = lax.rem(me, 16)
    plane = me - place
    group = me - y
    core = lax.rem(lax.axis_index("rep"), 2)
    worker1 = (core, 2 + core)
    worker2 = (5 + core, 9 + core)
    worker3 = (7 - 3 * core, 11 - 3 * core)
    is1 = (y == worker1[0]) | (y == worker1[1])
    is2 = (place == worker2[0]) | (place == worker2[1])
    is3 = (place == worker3[0]) | (place == worker3[1])
    head12 = jnp.where((is1 & (y == worker1[0])) | (is2 & (place == worker2[0])), 0, 1)
    head3 = jnp.where(place == worker3[0], 0, 1)
    one2 = jnp.where(is2, 1, 0)
    one3 = jnp.where(is3, 1, 0)

    load_offsets = pltpu.make_async_copy(offsets_hbm, offsets, load_sem.at[4])
    load_offsets.start()
    loads = []
    for i, (source, held) in enumerate(
        ((query_hbm, query), (keys_hbm, keys), (values_hbm, values), (dout_hbm, dout))
    ):
        loads.append(pltpu.make_async_copy(source, held, load_sem.at[i]))
        loads[-1].start()

    barrier = pltpu.get_barrier_semaphore()

    def greet(device):
        pl.semaphore_signal(barrier, inc=1, device_id={"seq": device}, device_id_type=MESH)

    @pl.when(is3)
    def _():
        def step(i, carry):
            greet(lax.rem(me + i, 64))
            return carry

        lax.fori_loop(1, 64, step, 0)

    @pl.when(is2)
    def _():
        def step(i, carry):
            greet(plane + lax.rem(place + i, 16))
            return carry

        lax.fori_loop(1, 16, step, 0)

    for spot in worker2 + worker3:
        @pl.when(place != spot)
        def _(spot=spot):
            greet(plane + spot)

    for i in range(1, 4):
        greet(group + lax.rem(y + i, 4))

    bases = (0, 32 * y, 8 * place)
    load_offsets.wait()
    for head in range(HEADS):
        off = [offsets[head, level] for level in range(3)]

        def target(index, off=off):
            return jnp.where(
                index < 128,
                index * RATES[0] + off[0],
                jnp.where(
                    index < 160, (index - 128) * RATES[1] + off[1], (index - 160) * RATES[2] + off[2]
                ),
            )

        sel[head] = jnp.where(
            iota((256, TOKENS), 1) == target(iota((256, 1), 0)), 1.0, 0.0
        ).astype(BF16)
    for load in loads:
        load.wait()
    for head in range(HEADS):
        lanes = slice(DIM * head, DIM * head + DIM)
        chooser = sel[head, 0:176]
        first = nn(chooser, jnp.concatenate([keys[:, lanes], values[:, lanes]], 1))
        second = nn(chooser, jnp.concatenate([query[:, lanes], dout[:, lanes]], 1))
        pack1[head, :, 0:256] = first[:128].astype(BF16)
        pack1[head, :, 256:512] = second[:128].astype(BF16)
        pack2[head, :, 0:256] = first[128:160].astype(BF16)
        pack2[head, :, 256:512] = second[128:160].astype(BF16)
        pack3[head] = jnp.concatenate([first[160:168], second[160:168]], 0).astype(BF16)

    pl.semaphore_wait(barrier, 3 + (2 - one2) + (8 - one3) + 15 * one3 + 15 * one2)

    def remote(src, dst, send_sem, recv_sem, device):
        return pltpu.make_async_remote_copy(
            src_ref=src, dst_ref=dst, send_sem=send_sem, recv_sem=recv_sem,
            device_id={"seq": device}, device_id_type=MESH,
        )

    pending = []

    def send(src, dst, send_sem, recv_sem, device):
        copy = remote(src, dst, send_sem, recv_sem, device)
        pending.append((device, copy))

        @pl.when(device != me)
        def _():
            copy.start()

    def arrived(ref, sem):
        pltpu.make_async_copy(ref, ref, sem).wait()

    mine1 = pl.ds(pl.multiple_of(128 * y, 128), 128)
    mine2 = pl.ds(pl.multiple_of(32 * place, 32), 32)
    for block in range(4):
        for head in range(HEADS):
            send(pack3.at[head], in3.at[me], send_in.at[2 * block + head], recv_in.at[2],
                 16 * block + worker3[head])
    for head in range(HEADS):
        send(pack2.at[head], work.at[mine2], send_in.at[8 + head], recv_in.at[1],
             plane + worker2[head])
    for head in range(HEADS):
        send(pack1.at[head], work.at[mine1], send_in.at[10 + head], recv_in.at[0],
             group + worker1[head])

    @pl.when(is1)
    def _():
        work[mine1] = pack1[head12]

    @pl.when(is2)
    def _():
        work[mine2] = pack2[head12]

    @pl.when(is3)
    def _():
        in3[me] = pack3[head3]

    def unit_refs(unit):
        head = lax.div(unit, 2)
        segment = lax.rem(unit, 2)
        return head, segment, pl.ds(pl.multiple_of(DIM * head, DIM), DIM)

    def forward0(unit, carry):
        head, segment, lanes = unit_refs(unit)
        rows = pl.ds(pl.multiple_of(KEYS * segment, KEYS), KEYS)
        key, value = keys[rows, lanes], values[rows, lanes]
        for chunk in range(2):
            start = pl.multiple_of(KEYS * segment + 256 * chunk, 256)
            part = pl.ds(start, 256)
            scores = nt(key, query[part, lanes]) * FACTOR
            row_max = jnp.max(scores, 0, keepdims=True)
            powers = jnp.exp(scores - row_max)
            powers0[unit, :, 256 * chunk : 256 * chunk + 256] = powers
            weights = powers.astype(BF16)
            weighted0[head, :, part] = tn(value, weights)
            products = nt(value, dout[part, lanes])
            products0[unit, :, 256 * chunk : 256 * chunk + 256] = products
            stat0[head, 0:1, part] = row_max
            stat0[head, 1:2, part] = jnp.sum(powers, 0, keepdims=True)
            stat0[head, 2:3, part] = jnp.sum(weights.astype(F32) * products, 0, keepdims=True)
        return carry

    stat0[...] = jnp.zeros_like(stat0)
    lax.fori_loop(0, 4, forward0, 0)
    for head in range(HEADS):
        off = [offsets[head, level] for level in range(3)]
        column = iota((1, 256), 1)
        target = jnp.where(
            column < 128,
            column * RATES[0] + off[0],
            jnp.where(
                column < 160, (column - 128) * RATES[1] + off[1], (column - 160) * RATES[2] + off[2]
            ),
        )
        spread[head] = jnp.where(iota((TOKENS, 256), 0) == target, 1.0, 0.0).astype(BF16)
        row = iota((128, 1), 0)
        for ref, level in ((sel2, 1), (sel3, 2)):
            target = (row - bases[level]) * RATES[level] + off[level]
            ref[head] = jnp.where(iota((128, TOKENS), 1) == target, 1.0, 0.0).astype(BF16)

    for head in range(HEADS):
        for level, chooser in enumerate((sel[head, 0:128], sel2[head], sel3[head])):
            tiles[level, 3 * head : 3 * head + 3] = select_rows_nt(stat0[head], chooser)[0:3]
    for level in range(3):
        tiles[level, 6:8] = jnp.zeros((2, BLOCK), F32)
    for block in range(4):
        for head in range(HEADS):
            send(tiles.at[2], tiles3.at[me], send_stat.at[2 * block + head], recv_stat.at[2],
                 16 * block + worker3[head])
    for head in range(HEADS):
        send(tiles.at[1], tiles2.at[place], send_stat.at[8 + head], recv_stat.at[1],
             plane + worker2[head])
    for head in range(HEADS):
        send(tiles.at[0], tiles1.at[y], send_stat.at[10 + head], recv_stat.at[0],
             group + worker1[head])

    @pl.when(is1)
    def _():
        tiles1[y] = tiles[0]

    @pl.when(is2)
    def _():
        tiles2[place] = tiles[1]

    @pl.when(is3)
    def _():
        tiles3[me] = tiles[2]

    worker_head = jnp.where(is3, head3, head12)
    off1, off2, off3 = (
        jnp.where(worker_head == 0, offsets[0, level], offsets[1, level]) for level in range(3)
    )
    column = iota((1, KEYS), 1)
    row = iota((BLOCK, 1), 0)
    own_position = jnp.where(
        is1, column * RATES[0] + off1, jnp.where(is2, column * RATES[1] + off2, column * RATES[2] + off3)
    )
    shared[0] = jnp.where(
        column * RATES[0] + off1 == row * RATES[1] + off2, 1.0, 0.0
    ).astype(BF16)
    in_plane = own_position + jnp.where(is1, 4 * TOKENS * z, 0)
    shared[1] = jnp.where(in_plane == row * RATES[2] + off3, 1.0, 0.0).astype(BF16)
    members = [
        lax.rem(own_position, rate) == off for rate, off in zip(RATES, (off1, off2, off3))
    ]

    def merge(items):
        peak = items[0][0]
        for item in items[1:]:
            peak = jnp.maximum(peak, item[0])
        factors = [jnp.exp(item[0] - peak) for item in items]
        total = factors[0] * items[0][1]
        product = factors[0] * items[0][2]
        for factor, item in zip(factors[1:], items[1:]):
            total += factor * item[1]
            product += factor * item[2]
        return peak, total, product

    def of_level(rows, member):
        return jnp.where(member, rows[0:1], -jnp.inf), rows[1:2], rows[2:3]

    def whole_forward():
        for chunk in range(2):
            part = slice(256 * chunk, 256 * chunk + 256)
            scores = nt(work[:, 0:128], work[part, 256:384]) * FACTOR
            row_max = jnp.max(scores, 0, keepdims=True)
            powers = jnp.exp(scores - row_max)
            weights = powers.astype(BF16)
            products = nt(work[:, 128:256], work[part, 384:512])
            power_work[:, part] = powers
            product_work[:, part] = products
            stat_work[:, part] = jnp.concatenate(
                [
                    row_max,
                    jnp.sum(powers, 0, keepdims=True),
                    jnp.sum(weights.astype(F32) * products, 0, keepdims=True),
                    jnp.zeros((5, 256), F32),
                ],
                0,
            )
            weighted_work[part] = tn(weights, work[:, 128:256])

    def whole_backward(log_row, delta_row):
        grad_k = jnp.zeros((KEYS, DIM), F32)
        grad_v = jnp.zeros((KEYS, DIM), F32)
        for chunk in range(2):
            part = slice(256 * chunk, 256 * chunk + 256)
            log_part, delta_part = log_row[:, part], delta_row[:, part]
            probs = power_work[:, part] * jnp.exp(stat_work[0:1, part] - log_part)
            low = (probs * (product_work[:, part] - delta_part)).astype(BF16)
            grad_work[part, 0:128] = (FACTOR * tn(low, work[:, 0:128])).astype(BF16)
            grad_k += nn(low, work[part, 256:384])
            grad_v += nn(probs.astype(BF16), work[part, 384:512])
        grad_work[:, 128:256] = (FACTOR * grad_k).astype(BF16)
        grad_work[:, 256:384] = grad_v.astype(BF16)

    rows3 = pl.ds(pl.multiple_of(128 * x, 128), 128)

    def block_forward():
        scores = nt(work[:, 0:128], work[rows3, 256:384]) * FACTOR
        row_max = jnp.max(scores, 0, keepdims=True)
        powers = jnp.exp(scores - row_max)
        weights = powers.astype(BF16)
        products = nt(work[:, 128:256], work[rows3, 384:512])
        power_work[:, 0:128] = powers
        product_work[:, 0:128] = products
        stats = jnp.concatenate(
            [
                row_max,
                jnp.sum(powers, 0, keepdims=True),
                jnp.sum(weights.astype(F32) * products, 0, keepdims=True),
                jnp.zeros((5, BLOCK), F32),
            ],
            0,
        )
        stat_work[:, 0:128] = stats
        return tn(weights, work[:, 128:256]), stats

    def block_backward(log_all, delta_all, log_own, delta_own):
        k_all, q_all, d_all = work[:, 0:128], work[:, 256:384], work[:, 384:512]
        k_own, v_own = work[rows3, 0:128], work[rows3, 128:256]
        probs = power_work[:, 0:128] * jnp.exp(stat_work[0:1, 0:128] - log_own)
        low = (probs * (product_work[:, 0:128] - delta_own)).astype(BF16)
        grad_q = FACTOR * tn(low, k_all)
        probs = jnp.exp(nt(k_own, q_all) * FACTOR - log_all)
        low = (probs * (nt(v_own, d_all) - delta_all)).astype(BF16)
        grad_k = FACTOR * nn(low, q_all)
        grad_v = nn(probs.astype(BF16), d_all)
        return jnp.concatenate([grad_q, grad_k, grad_v], 1)

    def rows_of(ref, index, count):
        return ref.at[pl.ds(pl.multiple_of(count * index, count), count)]

    def returns(wait, src1, dst1, sem1, recv1, src2, dst2, src3, dst3, sems, recv):
        def each(src, dst, sem, recv_sem, device):
            copy = remote(src, dst, sem, recv_sem, device)
            if wait:
                copy.wait_send()
            else:
                copy.start()

        if src1 is not None:
            @pl.when(is1)
            def _():
                for i in range(1, 4):
                    other = lax.rem(y + i, 4)
                    each(src1(other), dst1(head12), sem1.at[i], recv1.at[head12], group + other)

        if src2 is not None:
            @pl.when(is2)
            def _():
                def step(i, carry):
                    other = lax.rem(place + i, 16)
                    each(src2(other), dst2(head12), sems.at[i], recv.at[head12], plane + other)
                    return carry

                lax.fori_loop(1, 16, step, 0)

            @pl.when(is3)
            def _():
                def step(i, carry):
                    other = lax.rem(place + i, 16)
                    each(src3(other), dst3(head3), sems.at[i], recv.at[2 + head3], plane + other)
                    return carry

                lax.fori_loop(1, 16, step, 0)

    def back(wait):
        returns(
            wait,
            lambda i: stat_send.at[i], lambda h: back_stat1.at[h], send_back1, recv_back1,
            lambda i: send2.at[i], lambda h: back2.at[h],
            lambda i: send3.at[i], lambda h: back3.at[h], send_back, recv_back,
        )
        returns(
            wait,
            lambda i: rows_of(weighted_work, i, 128), lambda h: back_rows1.at[h], send_rows1, recv_rows1,
            None, None, None, None, None, None,
        )

    def grads_back(wait):
        returns(
            wait,
            lambda i: rows_of(grad_work, i, 128), lambda h: stack.at[h, pl.ds(0, 128)], send_grad1, recv_grad1,
            lambda i: rows_of(grad_work, i, 32), lambda h: stack.at[h, pl.ds(128, 32)],
            lambda i: grad_send3.at[i], lambda h: stack.at[h, pl.ds(160, 16)], send_grad, recv_grad,
        )

    def returned1(dst, recv):
        for head in range(HEADS):
            @pl.when(y != worker1[head])
            def _(head=head):
                arrived(dst(head), recv.at[head])

    def returned23(dst2, dst3, recv):
        for head in range(HEADS):
            @pl.when(place != worker2[head])
            def _(head=head):
                arrived(dst2(head), recv.at[head])

            @pl.when(place != worker3[head])
            def _(head=head):
                arrived(dst3(head), recv.at[2 + head])

    @pl.when(is1)
    def _():
        arrived(work.at[pl.ds(0, 384)], recv_in.at[0])

    @pl.when(is2)
    def _():
        arrived(work.at[pl.ds(0, 480)], recv_in.at[1])

    @pl.when(is3)
    def _():
        arrived(in3.at[pl.ds(0, 63)], recv_in.at[2])
        both = in3[...].astype(F32)
        work[:, 0:256] = both[:, 0:8].reshape(KEYS, 256).astype(BF16)
        work[:, 256:512] = both[:, 8:16].reshape(KEYS, 256).astype(BF16)
        weighted, stats = block_forward()
        for i in range(16):
            send3[i] = jnp.concatenate([weighted[8 * i : 8 * i + 8], stats], 0)
        back3[head3] = send3[place]

    @pl.when(is1 | is2)
    def _():
        whole_forward()
        for i in range(4):
            stat_send[i] = stat_work[:, 128 * i : 128 * i + 128]

        @pl.when(is2)
        def _():
            for i in range(16):
                send2[i, 0:32] = weighted_work[32 * i : 32 * i + 32]
                send2[i, 32:40] = stat_send[i // 4]
            back2[head12] = send2[place]

        @pl.when(is1)
        def _():
            back_stat1[head12] = stat_send[y]
            back_rows1[head12] = weighted_work[mine1]

    def exchange(wait):
        def each(src, dst, slot, device):
            copy = remote(src, dst, send_swap.at[slot], recv_swap.at[0], device)
            if wait:
                copy.wait_send()
            else:
                copy.start()

        @pl.when(is1)
        def _():
            for block in range(4):
                device = 16 * block + jnp.where(head12 == 0, worker3[0], worker3[1])
                each(swap_send.at[1], swap3.at[4 * x + z], block, device)
            device = plane + jnp.where(head12 == 0, worker2[0], worker2[1])
            each(swap_send.at[0], swap2.at[z], 4, device)

        @pl.when(is2)
        def _():
            for block in range(4):
                device = 16 * block + jnp.where(head12 == 0, worker3[0], worker3[1])
                each(swap_send.at[1], swap3.at[16 + x], block, device)
            for block in range(4):
                device = plane + 4 * block + jnp.where(head12 == 0, worker1[0], worker1[1])
                each(stat_send.at[block], swap1.at[0], 4 + block, device)

        @pl.when(is3)
        def _():
            for i in range(1, 4):
                device = 16 * lax.rem(x + i, 4) + place
                each(swap_send.at[0], swap3.at[20 + x], i, device)
            for block in range(4):
                device = plane + 4 * block + jnp.where(head3 == 0, worker1[0], worker1[1])
                each(swap_send.at[0], swap1.at[1], 4 + block, device)
            device = plane + jnp.where(head3 == 0, worker2[0], worker2[1])
            each(swap_send.at[0], swap2.at[4], 0, device)

    @pl.when(is1)
    def _():
        swap_send[0] = select_rows_nt(stat_work[...], shared[0])

    @pl.when(is1 | is2)
    def _():
        swap_send[1] = select_rows_nt(stat_work[...], shared[1])

    @pl.when(is3)
    def _():
        swap_send[0] = stat_work[:, 0:128]
        swap3[20 + x] = stat_work[:, 0:128]

    exchange(False)
    back(False)

    def below_rows(blocks, head):
        rows = jnp.concatenate(blocks, 1)
        return [jnp.where(head == 0, rows[i : i + 1], rows[3 + i : 4 + i]) for i in range(3)]

    def final_rows(items):
        peak, total, product = merge(items)
        return peak + jnp.log(total), product / total

    def blocks_of(row):
        return [row[:, i : i + BLOCK] for i in range(0, KEYS, BLOCK)]

    def pick(rows, block):
        chosen = rows[0]
        for i in range(1, len(rows)):
            chosen = jnp.where(block == i, rows[i], chosen)
        return chosen

    @pl.when(is2)
    def _():
        arrived(tiles2.at[pl.ds(0, 15)], recv_stat.at[1])
        arrived(swap2, recv_swap.at[0])
        for i in range(4):
            tiles1[i] = jnp.sum(tiles2[4 * i : 4 * i + 4], 0)

    @pl.when(is1)
    def _():
        arrived(tiles1.at[pl.ds(0, 3)], recv_stat.at[0])
        arrived(swap1, recv_swap.at[0])

    @pl.when(is1 | is2)
    def _():
        below = below_rows([tiles1[i] for i in range(4)], head12)
        own = [stat_work[i : i + 1] for i in range(3)]
        lacking = jnp.where(
            is1, select_rows(swap1[0], shared[0]), jnp.concatenate([swap2[i] for i in range(4)], 1)
        )
        member = (is1 & members[1]) | (is2 & members[0])
        level3 = select_rows(jnp.where(is1, swap1[1], swap2[4]), shared[1])
        whole_backward(
            *final_rows([below, own, of_level(lacking, member), of_level(level3, members[2])])
        )

        @pl.when(is2)
        def _():
            stack[head12, 128:160] = grad_work[mine2]

        @pl.when(is1)
        def _():
            stack[head12, 0:128] = grad_work[mine1]

    @pl.when(is3)
    def _():
        arrived(tiles3.at[pl.ds(0, 63)], recv_stat.at[2])
        arrived(swap3.at[pl.ds(0, 23)], recv_swap.at[0])
        below = below_rows([jnp.sum(tiles3[16 * i : 16 * i + 16], 0) for i in range(4)], head3)
        own = jnp.concatenate([swap3[20 + i] for i in range(4)], 1)
        level1 = jnp.concatenate([jnp.sum(swap3[4 * i : 4 * i + 4], 0) for i in range(4)], 1)
        level2 = jnp.concatenate([swap3[16 + i] for i in range(4)], 1)
        log_row, delta_row = final_rows(
            [
                below,
                [own[i : i + 1] for i in range(3)],
                of_level(level1, members[0]),
                of_level(level2, members[1]),
            ]
        )
        grads = block_backward(
            log_row, delta_row, pick(blocks_of(log_row), x), pick(blocks_of(delta_row), x)
        )
        for i in range(16):
            tile = jnp.concatenate([grads[8 * i : 8 * i + 8], jnp.zeros((8, 3 * DIM), F32)], 0)
            grad_send3[i] = tile.astype(BF16)
        stack[head3, 160:176] = grad_send3[place]

    grads_back(False)

    returned1(lambda h: back_stat1.at[h], recv_back1)
    returned23(lambda h: back2.at[h], lambda h: back3.at[h], recv_back)
    position = iota((1, TOKENS), 1)
    for head in range(HEADS):
        found = (
            select_rows(back_stat1[head], sel[head, 0:128]),
            select_rows(back2[head, 32:40], sel2[head]),
            select_rows(back3[head, 8:16], sel3[head]),
        )
        items = [[stat0[head, i : i + 1] for i in range(3)]]
        for level in range(3):
            member = lax.rem(position, RATES[level]) == offsets[head, level]
            items.append(of_level(found[level], member))
        peak, total, product = merge(items)
        inverse = 1.0 / total
        logs[head] = jnp.concatenate(
            [peak + jnp.log(total), product * inverse, jnp.zeros((6, TOKENS), F32)], 0
        )
        shares[head] = jnp.concatenate(
            [jnp.exp(item[0] - peak) * inverse for item in items] + [jnp.zeros((4, TOKENS), F32)], 0
        )

    def backward0(unit, carry):
        head, segment, lanes = unit_refs(unit)
        rows = pl.ds(pl.multiple_of(KEYS * segment, KEYS), KEYS)
        key = keys[rows, lanes]
        grad_k = jnp.zeros((KEYS, DIM), F32)
        grad_v = jnp.zeros((KEYS, DIM), F32)
        for chunk in range(2):
            part = pl.ds(pl.multiple_of(KEYS * segment + 256 * chunk, 256), 256)
            rescale = jnp.exp(stat0[head, 0:1, part] - logs[head, 0:1, part])
            probs = powers0[unit, :, 256 * chunk : 256 * chunk + 256] * rescale
            grad_rows = dout[part, lanes]
            products = products0[unit, :, 256 * chunk : 256 * chunk + 256]
            low = (probs * (products - logs[head, 1:2, part])).astype(BF16)
            grad_k += nn(low, query[part, lanes])
            grad_v += nn(probs.astype(BF16), grad_rows)
            dq_out[part, lanes] = (FACTOR * tn(key, low)).T
        dk_out[rows, lanes] = FACTOR * grad_k
        dv_out[rows, lanes] = grad_v
        return carry

    lax.fori_loop(0, 4, backward0, 0)

    returned1(lambda h: back_rows1.at[h], recv_rows1)
    for head in range(HEADS):
        lane_shares = select_rows_nt(shares[head], sel[head])
        lane = iota((1, 256), 1)
        share = jnp.where(
            lane < 128, lane_shares[1:2], jnp.where(lane < 160, lane_shares[2:3], lane_shares[3:4])
        )
        stacked = jnp.concatenate(
            [back_rows1[head], back2[head, 0:32], back3[head, 0:8], jnp.zeros((88, DIM), F32)], 0
        ).T * share
        high = stacked.astype(BF16)
        low = (stacked - high.astype(F32)).astype(BF16)
        attended = shares[head, 0:1] * weighted0[head] + nn(high, sel[head]) + nn(low, sel[head])
        att_out[:, DIM * head : DIM * head + DIM] = attended.T

    stack_out[:, 176:256] = jnp.zeros((2, 80, 3 * DIM), BF16)
    returned1(lambda h: stack.at[h, pl.ds(0, 128)], recv_grad1)
    returned23(
        lambda h: stack.at[h, pl.ds(128, 32)], lambda h: stack.at[h, pl.ds(160, 16)], recv_grad
    )
    stack_out[:, 0:176] = stack[...]

    for device, copy in pending:
        @pl.when(device != me)
        def _(copy=copy):
            copy.wait_send()
    exchange(True)
    back(True)
    grads_back(True)


def finish(att, dq, dk, dv, spread, stack, att_out, dq_out, dk_out, dv_out, full, sems):
    first = pltpu.make_async_copy(att, att_out, sems.at[12])
    first.start()
    copies = [first]
    for part in range(4):
        rows = slice(256 * part, 256 * part + 256)
        for head in range(HEADS):
            lanes = slice(DIM * head, DIM * head + DIM)
            added = nn(spread[head, rows], stack[head])
            for i, ref in enumerate((dq, dk, dv)):
                full[i, rows, lanes] = ref[rows, lanes] + added[:, DIM * i : DIM * i + DIM]
        for i, out in enumerate((dq_out, dk_out, dv_out)):
            copies.append(
                pltpu.make_async_copy(full.at[i, rows], out.at[rows], sems.at[3 * part + i])
            )
            copies[-1].start()
    for copy in copies:
        copy.wait()


def body(query, keys, values, grad_out, offsets):
    vmem = pl.BlockSpec(memory_space=pltpu.VMEM)
    hbm = pl.BlockSpec(memory_space=pltpu.HBM)
    out = jax.ShapeDtypeStruct((TOKENS, HEADS * DIM), F32)
    dma = pltpu.SemaphoreType.DMA
    held = pltpu.VMEM((TOKENS, HEADS * DIM), BF16)
    pinned = [
        pltpu.with_memory_space_constraint(item, pltpu.HBM)
        for item in (offsets.T, query, keys, values, grad_out)
    ]
    parts = pl.pallas_call(
        kernel,
        out_shape=(
            out, out, out, out,
            jax.ShapeDtypeStruct((2, TOKENS, 256), BF16),
            jax.ShapeDtypeStruct((2, 256, 3 * DIM), BF16),
        ),
        in_specs=[hbm] * 5,
        out_specs=(vmem,) * 6,
        scratch_shapes=[
            pltpu.SMEM((HEADS, 3), jnp.int32),
            held, held, held, held,
            pltpu.VMEM((2, 256, TOKENS), BF16),
            pltpu.VMEM((2, 128, TOKENS), BF16),
            pltpu.VMEM((2, 128, TOKENS), BF16),
            pltpu.VMEM((4, KEYS, KEYS), F32),
            pltpu.VMEM((4, KEYS, KEYS), F32),
            pltpu.VMEM((2, 8, TOKENS), F32),
            pltpu.VMEM((2, DIM, TOKENS), F32),
            pltpu.VMEM((2, 8, TOKENS), F32),
            pltpu.VMEM((2, 8, TOKENS), F32),
            pltpu.VMEM((2, 128, 512), BF16),
            pltpu.VMEM((2, 32, 512), BF16),
            pltpu.VMEM((2, 16, 256), BF16),
            pltpu.VMEM((512, 512), BF16),
            pltpu.VMEM((64, 16, 256), BF16),
            pltpu.VMEM((512, 512), F32),
            pltpu.VMEM((512, 512), F32),
            pltpu.VMEM((8, 512), F32),
            pltpu.VMEM((512, 128), F32),
            pltpu.VMEM((4, 8, 128), F32),
            pltpu.VMEM((16, 40, 128), F32),
            pltpu.VMEM((16, 16, 128), F32),
            pltpu.VMEM((2, 8, 128), F32),
            pltpu.VMEM((2, 128, 128), F32),
            pltpu.VMEM((2, 40, 128), F32),
            pltpu.VMEM((2, 16, 128), F32),
            pltpu.VMEM((512, 384), BF16),
            pltpu.VMEM((16, 16, 384), BF16),
            pltpu.VMEM((2, 176, 384), BF16),
            pltpu.VMEM((3, 8, 128), F32),
            pltpu.VMEM((4, 8, 128), F32),
            pltpu.VMEM((16, 8, 128), F32),
            pltpu.VMEM((64, 8, 128), F32),
            pltpu.VMEM((2, 128, KEYS), BF16),
            pltpu.VMEM((2, 8, 128), F32),
            pltpu.VMEM((2, 8, 128), F32),
            pltpu.VMEM((5, 8, 128), F32),
            pltpu.VMEM((24, 8, 128), F32),
            dma((5,)),
            dma((12,)),
            dma((16,)),
            dma((4,)),
            dma((4,)),
            dma((12,)),
            dma((16,)),
            dma((4,)),
            dma((3,)),
            dma((4,)),
            dma((2,)),
            dma((2,)),
            dma((3,)),
            dma((4,)),
            dma((2,)),
            dma((8,)),
            dma((1,)),
        ],
        compiler_params=pltpu.CompilerParams(
            collective_id=0, has_side_effects=True, vmem_limit_bytes=32 * 2**20
        ),
    )(*pinned)
    return pl.pallas_call(
        finish,
        out_shape=(out, out, out, out),
        in_specs=[vmem] * 6,
        out_specs=(hbm,) * 4,
        scratch_shapes=[pltpu.VMEM((3, TOKENS, HEADS * DIM), F32), dma((13,))],
        compiler_params=pltpu.CompilerParams(vmem_limit_bytes=16 * 2**20),
    )(*parts)


def solution(mesh):
    spec = P("seq", "rep")
    return jax.shard_map(
        body,
        mesh=mesh,
        in_specs=(spec, spec, spec, spec, P(None, "rep")),
        out_specs=(spec, spec, spec, spec),
        check_vma=False,
    )
```

```python
import jax
import jax.numpy as jnp
from jax import lax
from jax.experimental import pallas as pl
from jax.experimental.pallas import tpu as pltpu
from jax.sharding import PartitionSpec as P

HEADS = 2
KEYS = 512
DIM = 128
TOKENS = 1024
BLOCK = 128
RATES = (8, 32, 128)
FACTOR = DIM**-0.5
MESH = pl.DeviceIdType.MESH
F32 = jnp.float32
BF16 = jnp.bfloat16


def dot(a, b, dims):
    return lax.dot_general(a, b, (dims, ((), ())), preferred_element_type=F32)


def nn(a, b):
    return dot(a, b, ((1,), (0,)))


def nt(a, b):
    return dot(a, b, ((1,), (1,)))


def tn(a, b):
    return dot(a, b, ((0,), (0,)))


def split3(a):
    high = a.astype(BF16)
    rest = a - high.astype(F32)
    middle = rest.astype(BF16)
    low = (rest - middle.astype(F32)).astype(BF16)
    return jnp.concatenate([high.astype(F32), middle.astype(F32), low.astype(F32)], 0).astype(BF16)


def join3(a):
    rows = a.shape[0] // 3
    return a[:rows] + a[rows : 2 * rows] + a[2 * rows :]


def select_rows(stats, chooser):
    return join3(nn(split3(stats), chooser))


def select_rows_nt(stats, chooser):
    return join3(nt(split3(stats), chooser))


def iota(shape, dim):
    return lax.broadcasted_iota(jnp.int32, shape, dim)


def kernel(
    offsets_hbm, query_hbm, keys_hbm, values_hbm, dout_hbm,
    att_out, dq_out, dk_out, dv_out, spread, stack_out,
    offsets, query, keys, values, dout,
    small, wide3, sel, sel2, sel3, powers0, products0, shares, weighted0, stat0, logs,
    pack1, pack2, pack3, work, in3, power_work, product_work, stat_work, weighted_work,
    stat_send, send2, send3, back_stat1, back_rows1, back2, back3, grad_work, grad_send3, stack,
    tiles, tiles1, tiles2, tiles3, shared, swap_send, swap1, swap2, swap3,
    load_sem, send_in, send_back, send_back1, send_rows1, send_stat, send_grad, send_grad1,
    recv_in, recv_back, recv_back1, recv_rows1, recv_stat, recv_grad, recv_grad1, send_swap, recv_swap,
):
    me = lax.axis_index("seq")
    y = lax.rem(me, 4)
    z = lax.rem(lax.div(me, 4), 4)
    x = lax.div(me, 16)
    place = lax.rem(me, 16)
    plane = me - place
    group = me - y
    core = lax.rem(lax.axis_index("rep"), 2)
    worker1 = (core, 2 + core)
    worker2 = (5 + core, 9 + core)
    worker3 = (7 - 3 * core, 11 - 3 * core)
    is1 = (y == worker1[0]) | (y == worker1[1])
    is2 = (place == worker2[0]) | (place == worker2[1])
    is3 = (place == worker3[0]) | (place == worker3[1])
    head12 = jnp.where((is1 & (y == worker1[0])) | (is2 & (place == worker2[0])), 0, 1)
    head3 = jnp.where(place == worker3[0], 0, 1)
    one2 = jnp.where(is2, 1, 0)
    one3 = jnp.where(is3, 1, 0)

    load_offsets = pltpu.make_async_copy(offsets_hbm, offsets, load_sem.at[4])
    load_offsets.start()
    loads = []
    for i, (source, held) in enumerate(
        ((keys_hbm, keys), (values_hbm, values), (query_hbm, query), (dout_hbm, dout))
    ):
        loads.append(pltpu.make_async_copy(source, held, load_sem.at[i]))
        loads[-1].start()

    barrier = pltpu.get_barrier_semaphore()

    def greet(device):
        pl.semaphore_signal(barrier, inc=1, device_id={"seq": device}, device_id_type=MESH)

    @pl.when(is3)
    def _():
        def step(i, carry):
            greet(lax.rem(me + i, 64))
            return carry

        lax.fori_loop(1, 64, step, 0)

    @pl.when(is2)
    def _():
        def step(i, carry):
            greet(plane + lax.rem(place + i, 16))
            return carry

        lax.fori_loop(1, 16, step, 0)

    for spot in worker2 + worker3:
        @pl.when(place != spot)
        def _(spot=spot):
            greet(plane + spot)

    for i in range(1, 4):
        greet(group + lax.rem(y + i, 4))

    load_offsets.wait()
    row = iota((48, 1), 0)
    for head in range(HEADS):
        off = [offsets[head, level] for level in range(3)]
        for part in range(4):
            target = jnp.where(
                row < 32,
                row * RATES[0] + off[0],
                jnp.where(
                    row < 40, (row - 32) * RATES[1] + off[1], (row - 40 - 2 * part) * RATES[2] + off[2]
                ),
            )
            small[head, part] = jnp.where(iota((48, 256), 1) == target, 1.0, 0.0).astype(BF16)
    for pair, sources in enumerate(((keys, values), (query, dout))):
        for load in loads[2 * pair : 2 * pair + 2]:
            load.wait()
        wide = slice(256 * pair, 256 * pair + 256)
        for head in range(HEADS):
            lanes = slice(DIM * head, DIM * head + DIM)
            pieces = []
            for part in range(4):
                rows = slice(256 * part, 256 * part + 256)
                both = jnp.concatenate([source[rows, lanes] for source in sources], 1)
                pieces.append(nn(small[head, part], both))
                pack1[head, 32 * part : 32 * part + 32, wide] = pieces[part][0:32].astype(BF16)
            pack2[head, :, wide] = jnp.concatenate([piece[32:40] for piece in pieces], 0).astype(BF16)
            wide3[head, 8 * pair : 8 * pair + 8] = (
                (pieces[0][40:48] + pieces[1][40:48]) + (pieces[2][40:48] + pieces[3][40:48])
            )
    for head in range(HEADS):
        pack3[head] = wide3[head].astype(BF16)

    pl.semaphore_wait(barrier, 3 + (2 - one2) + (8 - one3) + 15 * one3 + 15 * one2)

    def remote(src, dst, send_sem, recv_sem, device):
        return pltpu.make_async_remote_copy(
            src_ref=src, dst_ref=dst, send_sem=send_sem, recv_sem=recv_sem,
            device_id={"seq": device}, device_id_type=MESH,
        )

    def send(src, dst, send_sem, recv_sem, device):
        copy = remote(src, dst, send_sem, recv_sem, device)

        @pl.when(device != me)
        def _():
            copy.start()

    def arrived(ref, sem):
        pltpu.make_async_copy(ref, ref, sem).wait()

    mine1 = pl.ds(pl.multiple_of(128 * y, 128), 128)
    mine2 = pl.ds(pl.multiple_of(32 * place, 32), 32)
    for head in range(HEADS):
        send(pack1.at[head], work.at[mine1], send_in.at[0], recv_in.at[0],
             group + worker1[head])
    for block in range(4):
        for head in range(HEADS):
            send(pack3.at[head], in3.at[me], send_in.at[2], recv_in.at[2],
                 16 * block + worker3[head])
    for head in range(HEADS):
        send(pack2.at[head], work.at[mine2], send_in.at[1], recv_in.at[1],
             plane + worker2[head])

    @pl.when(is1)
    def _():
        work[mine1] = pack1[head12]

    @pl.when(is2)
    def _():
        work[mine2] = pack2[head12]

    @pl.when(is3)
    def _():
        in3[me] = pack3[head3]

    def unit_refs(unit):
        head = lax.div(unit, 2)
        segment = lax.rem(unit, 2)
        return head, segment, pl.ds(pl.multiple_of(DIM * head, DIM), DIM)

    def forward0(unit, carry):
        head, segment, lanes = unit_refs(unit)
        rows = pl.ds(pl.multiple_of(KEYS * segment, KEYS), KEYS)
        key, value = keys[rows, lanes], values[rows, lanes]
        for chunk in range(2):
            start = pl.multiple_of(KEYS * segment + 256 * chunk, 256)
            part = pl.ds(start, 256)
            scores = nt(key, query[part, lanes]) * FACTOR
            row_max = jnp.max(scores, 0, keepdims=True)
            powers = jnp.exp(scores - row_max)
            powers0[unit, :, 256 * chunk : 256 * chunk + 256] = powers
            weights = powers.astype(BF16)
            weighted0[head, :, part] = tn(value, weights)
            products = nt(value, dout[part, lanes])
            products0[unit, :, 256 * chunk : 256 * chunk + 256] = products
            stat0[head, 0:1, part] = row_max
            stat0[head, 1:2, part] = jnp.sum(powers, 0, keepdims=True)
            stat0[head, 2:3, part] = jnp.sum(weights.astype(F32) * products, 0, keepdims=True)
        return carry

    stat0[...] = jnp.zeros_like(stat0)
    lax.fori_loop(0, 4, forward0, 0)
    bases = (0, 32 * y, 8 * place)

    def target(index, off):
        return jnp.where(
            index < 128,
            index * RATES[0] + off[0],
            jnp.where(
                index < 160, (index - 128) * RATES[1] + off[1], (index - 160) * RATES[2] + off[2]
            ),
        )

    for head in range(HEADS):
        off = [offsets[head, level] for level in range(3)]
        sel[head] = jnp.where(
            iota((256, TOKENS), 1) == target(iota((256, 1), 0), off), 1.0, 0.0
        ).astype(BF16)
        row = iota((128, 1), 0)
        for ref, level in ((sel2, 1), (sel3, 2)):
            wanted = (row - bases[level]) * RATES[level] + off[level]
            ref[head] = jnp.where(iota((128, TOKENS), 1) == wanted, 1.0, 0.0).astype(BF16)

    for head in range(HEADS):
        for level, chooser in enumerate((sel[head, 0:128], sel2[head], sel3[head])):
            tiles[level, 3 * head : 3 * head + 3] = select_rows_nt(stat0[head], chooser)[0:3]
    for level in range(3):
        tiles[level, 6:8] = jnp.zeros((2, BLOCK), F32)
    for block in range(4):
        for head in range(HEADS):
            send(tiles.at[2], tiles3.at[me], send_stat.at[2], recv_stat.at[2],
                 16 * block + worker3[head])
    for head in range(HEADS):
        send(tiles.at[1], tiles2.at[place], send_stat.at[1], recv_stat.at[1],
             plane + worker2[head])
    for head in range(HEADS):
        send(tiles.at[0], tiles1.at[y], send_stat.at[0], recv_stat.at[0],
             group + worker1[head])

    @pl.when(is1)
    def _():
        tiles1[y] = tiles[0]

    @pl.when(is2)
    def _():
        tiles2[place] = tiles[1]

    @pl.when(is3)
    def _():
        tiles3[me] = tiles[2]

    worker_head = jnp.where(is3, head3, head12)
    off1, off2, off3 = (
        jnp.where(worker_head == 0, offsets[0, level], offsets[1, level]) for level in range(3)
    )
    column = iota((1, KEYS), 1)
    row = iota((BLOCK, 1), 0)
    own_position = jnp.where(
        is1, column * RATES[0] + off1, jnp.where(is2, column * RATES[1] + off2, column * RATES[2] + off3)
    )
    shared[0] = jnp.where(
        column * RATES[0] + off1 == row * RATES[1] + off2, 1.0, 0.0
    ).astype(BF16)
    in_plane = own_position + jnp.where(is1, 4 * TOKENS * z, 0)
    shared[1] = jnp.where(in_plane == row * RATES[2] + off3, 1.0, 0.0).astype(BF16)
    members = [
        lax.rem(own_position, rate) == off for rate, off in zip(RATES, (off1, off2, off3))
    ]

    def merge(items):
        peak = items[0][0]
        for item in items[1:]:
            peak = jnp.maximum(peak, item[0])
        factors = [jnp.exp(item[0] - peak) for item in items]
        total = factors[0] * items[0][1]
        product = factors[0] * items[0][2]
        for factor, item in zip(factors[1:], items[1:]):
            total += factor * item[1]
            product += factor * item[2]
        return peak, total, product

    def of_level(rows, member):
        return jnp.where(member, rows[0:1], -jnp.inf), rows[1:2], rows[2:3]

    def whole_forward():
        for chunk in range(2):
            part = slice(256 * chunk, 256 * chunk + 256)
            scores = nt(work[:, 0:128], work[part, 256:384]) * FACTOR
            row_max = jnp.max(scores, 0, keepdims=True)
            powers = jnp.exp(scores - row_max)
            weights = powers.astype(BF16)
            products = nt(work[:, 128:256], work[part, 384:512])
            power_work[:, part] = powers
            product_work[:, part] = products
            stat_work[:, part] = jnp.concatenate(
                [
                    row_max,
                    jnp.sum(powers, 0, keepdims=True),
                    jnp.sum(weights.astype(F32) * products, 0, keepdims=True),
                    jnp.zeros((5, 256), F32),
                ],
                0,
            )
            weighted_work[part] = tn(weights, work[:, 128:256])

    def whole_backward(log_row, delta_row):
        grad_k = jnp.zeros((KEYS, DIM), F32)
        grad_v = jnp.zeros((KEYS, DIM), F32)
        for chunk in range(2):
            part = slice(256 * chunk, 256 * chunk + 256)
            log_part, delta_part = log_row[:, part], delta_row[:, part]
            probs = power_work[:, part] * jnp.exp(stat_work[0:1, part] - log_part)
            low = (probs * (product_work[:, part] - delta_part)).astype(BF16)
            grad_work[part, 0:128] = (FACTOR * tn(low, work[:, 0:128])).astype(BF16)
            grad_k += nn(low, work[part, 256:384])
            grad_v += nn(probs.astype(BF16), work[part, 384:512])
        grad_work[:, 128:256] = (FACTOR * grad_k).astype(BF16)
        grad_work[:, 256:384] = grad_v.astype(BF16)

    rows3 = pl.ds(pl.multiple_of(128 * x, 128), 128)

    def block_forward():
        scores = nt(work[:, 0:128], work[rows3, 256:384]) * FACTOR
        row_max = jnp.max(scores, 0, keepdims=True)
        powers = jnp.exp(scores - row_max)
        weights = powers.astype(BF16)
        products = nt(work[:, 128:256], work[rows3, 384:512])
        power_work[:, 0:128] = powers
        product_work[:, 0:128] = products
        stats = jnp.concatenate(
            [
                row_max,
                jnp.sum(powers, 0, keepdims=True),
                jnp.sum(weights.astype(F32) * products, 0, keepdims=True),
                jnp.zeros((5, BLOCK), F32),
            ],
            0,
        )
        stat_work[:, 0:128] = stats
        return tn(weights, work[:, 128:256]), stats

    def block_backward(log_all, delta_all, log_own, delta_own):
        k_all, q_all, d_all = work[:, 0:128], work[:, 256:384], work[:, 384:512]
        k_own, v_own = work[rows3, 0:128], work[rows3, 128:256]
        probs = power_work[:, 0:128] * jnp.exp(stat_work[0:1, 0:128] - log_own)
        low = (probs * (product_work[:, 0:128] - delta_own)).astype(BF16)
        grad_q = FACTOR * tn(low, k_all)
        probs = jnp.exp(nt(k_own, q_all) * FACTOR - log_all)
        low = (probs * (nt(v_own, d_all) - delta_all)).astype(BF16)
        grad_k = FACTOR * nn(low, q_all)
        grad_v = nn(probs.astype(BF16), d_all)
        return jnp.concatenate([grad_q, grad_k, grad_v], 1)

    def rows_of(ref, index, count):
        return ref.at[pl.ds(pl.multiple_of(count * index, count), count)]

    def returns(src1, dst1, sem1, recv1, src2, dst2, src3, dst3, sems, recv):
        def each(src, dst, sem, recv_sem, device):
            remote(src, dst, sem.at[0], recv_sem, device).start()

        if src1 is not None:
            @pl.when(is1)
            def _():
                for i in range(1, 4):
                    other = lax.rem(y + i, 4)
                    each(src1(other), dst1(head12), sem1, recv1.at[head12], group + other)

        if src2 is not None:
            @pl.when(is2)
            def _():
                def step(i, carry):
                    other = lax.rem(place + i, 16)
                    each(src2(other), dst2(head12), sems, recv.at[head12], plane + other)
                    return carry

                lax.fori_loop(1, 16, step, 0)

            @pl.when(is3)
            def _():
                def step(i, carry):
                    other = lax.rem(place + i, 16)
                    each(src3(other), dst3(head3), sems, recv.at[2 + head3], plane + other)
                    return carry

                lax.fori_loop(1, 16, step, 0)

    def back():
        returns(
            lambda i: stat_send.at[i], lambda h: back_stat1.at[h], send_back1, recv_back1,
            lambda i: send2.at[i], lambda h: back2.at[h],
            lambda i: send3.at[i], lambda h: back3.at[h], send_back, recv_back,
        )
        returns(
            lambda i: rows_of(weighted_work, i, 128), lambda h: back_rows1.at[h], send_rows1, recv_rows1,
            None, None, None, None, None, None,
        )

    def grads_back():
        returns(
            lambda i: rows_of(grad_work, i, 128), lambda h: stack.at[h, pl.ds(0, 128)], send_grad1, recv_grad1,
            lambda i: rows_of(grad_work, i, 32), lambda h: stack.at[h, pl.ds(128, 32)],
            lambda i: grad_send3.at[i], lambda h: stack.at[h, pl.ds(160, 16)], send_grad, recv_grad,
        )

    def returned1(dst, recv):
        for head in range(HEADS):
            @pl.when(y != worker1[head])
            def _(head=head):
                arrived(dst(head), recv.at[head])

    def returned23(dst2, dst3, recv):
        for head in range(HEADS):
            @pl.when(place != worker2[head])
            def _(head=head):
                arrived(dst2(head), recv.at[head])

            @pl.when(place != worker3[head])
            def _(head=head):
                arrived(dst3(head), recv.at[2 + head])

    @pl.when(is1)
    def _():
        arrived(work.at[pl.ds(0, 384)], recv_in.at[0])

    @pl.when(is2)
    def _():
        arrived(work.at[pl.ds(0, 480)], recv_in.at[1])

    @pl.when(is3)
    def _():
        arrived(in3.at[pl.ds(0, 63)], recv_in.at[2])
        both = in3[...].astype(F32)
        work[:, 0:256] = both[:, 0:8].reshape(KEYS, 256).astype(BF16)
        work[:, 256:512] = both[:, 8:16].reshape(KEYS, 256).astype(BF16)
        weighted, stats = block_forward()
        for i in range(16):
            send3[i] = jnp.concatenate([weighted[8 * i : 8 * i + 8], stats], 0)
        back3[head3] = send3[place]

    @pl.when(is1 | is2)
    def _():
        whole_forward()
        for i in range(4):
            stat_send[i] = stat_work[:, 128 * i : 128 * i + 128]

        @pl.when(is2)
        def _():
            for i in range(16):
                send2[i, 0:32] = weighted_work[32 * i : 32 * i + 32]
                send2[i, 32:40] = stat_send[i // 4]
            back2[head12] = send2[place]

        @pl.when(is1)
        def _():
            back_stat1[head12] = stat_send[y]
            back_rows1[head12] = weighted_work[mine1]

    def exchange():
        def each(src, dst, device):
            remote(src, dst, send_swap.at[0], recv_swap.at[0], device).start()

        @pl.when(is1)
        def _():
            for block in range(4):
                device = 16 * block + jnp.where(head12 == 0, worker3[0], worker3[1])
                each(swap_send.at[1], swap3.at[4 * x + z], device)
            device = plane + jnp.where(head12 == 0, worker2[0], worker2[1])
            each(swap_send.at[0], swap2.at[z], device)

        @pl.when(is2)
        def _():
            for block in range(4):
                device = 16 * block + jnp.where(head12 == 0, worker3[0], worker3[1])
                each(swap_send.at[1], swap3.at[16 + x], device)
            for block in range(4):
                device = plane + 4 * block + jnp.where(head12 == 0, worker1[0], worker1[1])
                each(stat_send.at[block], swap1.at[0], device)

        @pl.when(is3)
        def _():
            for i in range(1, 4):
                device = 16 * lax.rem(x + i, 4) + place
                each(swap_send.at[0], swap3.at[20 + x], device)
            for block in range(4):
                device = plane + 4 * block + jnp.where(head3 == 0, worker1[0], worker1[1])
                each(swap_send.at[0], swap1.at[1], device)
            device = plane + jnp.where(head3 == 0, worker2[0], worker2[1])
            each(swap_send.at[0], swap2.at[4], device)

    @pl.when(is1)
    def _():
        swap_send[0] = select_rows_nt(stat_work[...], shared[0])

    @pl.when(is1 | is2)
    def _():
        swap_send[1] = select_rows_nt(stat_work[...], shared[1])

    @pl.when(is3)
    def _():
        swap_send[0] = stat_work[:, 0:128]
        swap3[20 + x] = stat_work[:, 0:128]

    exchange()
    back()
    for head in range(HEADS):
        att_out[:, DIM * head : DIM * head + DIM] = weighted0[head].T
    for head in range(HEADS):
        off = [offsets[head, level] for level in range(3)]
        spread[head] = jnp.where(
            iota((TOKENS, 256), 0) == target(iota((1, 256), 1), off), 1.0, 0.0
        ).astype(BF16)

    def below_rows(blocks, head):
        rows = jnp.concatenate(blocks, 1)
        return [jnp.where(head == 0, rows[i : i + 1], rows[3 + i : 4 + i]) for i in range(3)]

    def final_rows(items):
        peak, total, product = merge(items)
        return peak + jnp.log(total), product / total

    def blocks_of(row):
        return [row[:, i : i + BLOCK] for i in range(0, KEYS, BLOCK)]

    def pick(rows, block):
        chosen = rows[0]
        for i in range(1, len(rows)):
            chosen = jnp.where(block == i, rows[i], chosen)
        return chosen

    @pl.when(is2)
    def _():
        arrived(tiles2.at[pl.ds(0, 15)], recv_stat.at[1])
        arrived(swap2, recv_swap.at[0])
        for i in range(4):
            tiles1[i] = jnp.sum(tiles2[4 * i : 4 * i + 4], 0)

    @pl.when(is1)
    def _():
        arrived(tiles1.at[pl.ds(0, 3)], recv_stat.at[0])
        arrived(swap1, recv_swap.at[0])

    @pl.when(is1 | is2)
    def _():
        below = below_rows([tiles1[i] for i in range(4)], head12)
        own = [stat_work[i : i + 1] for i in range(3)]
        lacking = jnp.where(
            is1, select_rows(swap1[0], shared[0]), jnp.concatenate([swap2[i] for i in range(4)], 1)
        )
        member = (is1 & members[1]) | (is2 & members[0])
        level3 = select_rows(jnp.where(is1, swap1[1], swap2[4]), shared[1])
        whole_backward(
            *final_rows([below, own, of_level(lacking, member), of_level(level3, members[2])])
        )

        @pl.when(is2)
        def _():
            stack[head12, 128:160] = grad_work[mine2]

        @pl.when(is1)
        def _():
            stack[head12, 0:128] = grad_work[mine1]

    @pl.when(is3)
    def _():
        arrived(tiles3.at[pl.ds(0, 63)], recv_stat.at[2])
        arrived(swap3.at[pl.ds(0, 23)], recv_swap.at[0])
        below = below_rows([jnp.sum(tiles3[16 * i : 16 * i + 16], 0) for i in range(4)], head3)
        own = jnp.concatenate([swap3[20 + i] for i in range(4)], 1)
        level1 = jnp.concatenate([jnp.sum(swap3[4 * i : 4 * i + 4], 0) for i in range(4)], 1)
        level2 = jnp.concatenate([swap3[16 + i] for i in range(4)], 1)
        log_row, delta_row = final_rows(
            [
                below,
                [own[i : i + 1] for i in range(3)],
                of_level(level1, members[0]),
                of_level(level2, members[1]),
            ]
        )
        grads = block_backward(
            log_row, delta_row, pick(blocks_of(log_row), x), pick(blocks_of(delta_row), x)
        )
        for i in range(16):
            tile = jnp.concatenate([grads[8 * i : 8 * i + 8], jnp.zeros((8, 3 * DIM), F32)], 0)
            grad_send3[i] = tile.astype(BF16)
        stack[head3, 160:176] = grad_send3[place]

    grads_back()

    returned1(lambda h: back_stat1.at[h], recv_back1)
    returned23(lambda h: back2.at[h], lambda h: back3.at[h], recv_back)
    position = iota((1, TOKENS), 1)
    for head in range(HEADS):
        found = (
            select_rows(back_stat1[head], sel[head, 0:128]),
            select_rows(back2[head, 32:40], sel2[head]),
            select_rows(back3[head, 8:16], sel3[head]),
        )
        items = [[stat0[head, i : i + 1] for i in range(3)]]
        for level in range(3):
            member = lax.rem(position, RATES[level]) == offsets[head, level]
            items.append(of_level(found[level], member))
        peak, total, product = merge(items)
        inverse = 1.0 / total
        logs[head] = jnp.concatenate(
            [peak + jnp.log(total), product * inverse, jnp.zeros((6, TOKENS), F32)], 0
        )
        shares[head] = jnp.concatenate(
            [jnp.exp(item[0] - peak) * inverse for item in items] + [jnp.zeros((4, TOKENS), F32)], 0
        )

    def backward0(unit, carry):
        head, segment, lanes = unit_refs(unit)
        rows = pl.ds(pl.multiple_of(KEYS * segment, KEYS), KEYS)
        key = keys[rows, lanes]
        grad_k = jnp.zeros((KEYS, DIM), F32)
        grad_v = jnp.zeros((KEYS, DIM), F32)
        for chunk in range(2):
            part = pl.ds(pl.multiple_of(KEYS * segment + 256 * chunk, 256), 256)
            rescale = jnp.exp(stat0[head, 0:1, part] - logs[head, 0:1, part])
            probs = powers0[unit, :, 256 * chunk : 256 * chunk + 256] * rescale
            grad_rows = dout[part, lanes]
            products = products0[unit, :, 256 * chunk : 256 * chunk + 256]
            low = (probs * (products - logs[head, 1:2, part])).astype(BF16)
            grad_k += nn(low, query[part, lanes])
            grad_v += nn(probs.astype(BF16), grad_rows)
            dq_out[part, lanes] = (FACTOR * tn(key, low)).T
        dk_out[rows, lanes] = FACTOR * grad_k
        dv_out[rows, lanes] = grad_v
        return carry

    lax.fori_loop(0, 4, backward0, 0)

    returned1(lambda h: back_rows1.at[h], recv_rows1)
    for head in range(HEADS):
        lane_shares = select_rows_nt(shares[head], sel[head])
        lane = iota((1, 256), 1)
        share = jnp.where(
            lane < 128, lane_shares[1:2], jnp.where(lane < 160, lane_shares[2:3], lane_shares[3:4])
        )
        stacked = jnp.concatenate(
            [back_rows1[head], back2[head, 0:32], back3[head, 0:8], jnp.zeros((88, DIM), F32)], 0
        ) * jnp.concatenate([share, jnp.zeros((7, 256), F32)], 0).T[:, 0:1]
        high = stacked.astype(BF16)
        low = (stacked - high.astype(F32)).astype(BF16)
        added = nn(spread[head], jnp.concatenate([high, low], 1))
        lanes = slice(DIM * head, DIM * head + DIM)
        att_out[:, lanes] = (
            att_out[:, lanes] * shares[head].T[:, 0:1] + added[:, 0:DIM] + added[:, DIM : 2 * DIM]
        )

    for sems, refs in ((send_in, (pack1, pack2, in3)), (send_stat, (tiles1, tiles2, tiles3))):
        for level, (here, count) in enumerate(((is1, 2), (is2, 2), (is3, 8))):
            @pl.when(here)
            def _(ref=refs[level], sem=sems.at[level], count=count):
                arrived(ref.at[pl.ds(0, count - 1)], sem)

            @pl.when(jnp.logical_not(here))
            def _(ref=refs[level], sem=sems.at[level], count=count):
                arrived(ref.at[pl.ds(0, count)], sem)

    @pl.when(is1)
    def _():
        arrived(swap3.at[pl.ds(0, 5)], send_swap.at[0])
        arrived(stat_send.at[pl.ds(0, 3)], send_back1.at[0])
        arrived(weighted_work.at[pl.ds(0, 384)], send_rows1.at[0])
        arrived(grad_work.at[pl.ds(0, 384)], send_grad1.at[0])

    @pl.when(is2)
    def _():
        arrived(swap3.at[pl.ds(0, 8)], send_swap.at[0])
        arrived(send2.at[pl.ds(0, 15)], send_back.at[0])
        arrived(grad_work.at[pl.ds(0, 480)], send_grad.at[0])

    @pl.when(is3)
    def _():
        arrived(swap3.at[pl.ds(0, 8)], send_swap.at[0])
        arrived(send3.at[pl.ds(0, 15)], send_back.at[0])
        arrived(grad_send3.at[pl.ds(0, 15)], send_grad.at[0])

    stack_out[:, 176:256] = jnp.zeros((2, 80, 3 * DIM), BF16)
    returned1(lambda h: stack.at[h, pl.ds(0, 128)], recv_grad1)
    returned23(
        lambda h: stack.at[h, pl.ds(128, 32)], lambda h: stack.at[h, pl.ds(160, 16)], recv_grad
    )
    stack_out[:, 0:176] = stack[...]


def finish(att, dq, dk, dv, spread, stack, att_out, dq_out, dk_out, dv_out, full, sems):
    first = pltpu.make_async_copy(att, att_out, sems.at[12])
    first.start()
    copies = [first]
    for part in range(4):
        rows = slice(256 * part, 256 * part + 256)
        for head in range(HEADS):
            lanes = slice(DIM * head, DIM * head + DIM)
            added = nn(spread[head, rows], stack[head])
            for i, ref in enumerate((dq, dk, dv)):
                full[i, rows, lanes] = ref[rows, lanes] + added[:, DIM * i : DIM * i + DIM]
        for i, out in enumerate((dq_out, dk_out, dv_out)):
            copies.append(
                pltpu.make_async_copy(full.at[i, rows], out.at[rows], sems.at[3 * part + i])
            )
            copies[-1].start()
    for copy in copies:
        copy.wait()


def body(query, keys, values, grad_out, offsets):
    vmem = pl.BlockSpec(memory_space=pltpu.VMEM)
    hbm = pl.BlockSpec(memory_space=pltpu.HBM)
    out = jax.ShapeDtypeStruct((TOKENS, HEADS * DIM), F32)
    dma = pltpu.SemaphoreType.DMA
    held = pltpu.VMEM((TOKENS, HEADS * DIM), BF16)
    pinned = [
        pltpu.with_memory_space_constraint(item, pltpu.HBM)
        for item in (offsets.T, query, keys, values, grad_out)
    ]
    parts = pl.pallas_call(
        kernel,
        out_shape=(
            out, out, out, out,
            jax.ShapeDtypeStruct((2, TOKENS, 256), BF16),
            jax.ShapeDtypeStruct((2, 256, 3 * DIM), BF16),
        ),
        in_specs=[hbm] * 5,
        out_specs=(vmem,) * 6,
        scratch_shapes=[
            pltpu.SMEM((HEADS, 3), jnp.int32),
            held, held, held, held,
            pltpu.VMEM((2, 4, 48, 256), BF16),
            pltpu.VMEM((2, 16, 256), F32),
            pltpu.VMEM((2, 256, TOKENS), BF16),
            pltpu.VMEM((2, 128, TOKENS), BF16),
            pltpu.VMEM((2, 128, TOKENS), BF16),
            pltpu.VMEM((4, KEYS, KEYS), F32),
            pltpu.VMEM((4, KEYS, KEYS), F32),
            pltpu.VMEM((2, 8, TOKENS), F32),
            pltpu.VMEM((2, DIM, TOKENS), F32),
            pltpu.VMEM((2, 8, TOKENS), F32),
            pltpu.VMEM((2, 8, TOKENS), F32),
            pltpu.VMEM((2, 128, 512), BF16),
            pltpu.VMEM((2, 32, 512), BF16),
            pltpu.VMEM((2, 16, 256), BF16),
            pltpu.VMEM((512, 512), BF16),
            pltpu.VMEM((64, 16, 256), BF16),
            pltpu.VMEM((512, 512), F32),
            pltpu.VMEM((512, 512), F32),
            pltpu.VMEM((8, 512), F32),
            pltpu.VMEM((512, 128), F32),
            pltpu.VMEM((4, 8, 128), F32),
            pltpu.VMEM((16, 40, 128), F32),
            pltpu.VMEM((16, 16, 128), F32),
            pltpu.VMEM((2, 8, 128), F32),
            pltpu.VMEM((2, 128, 128), F32),
            pltpu.VMEM((2, 40, 128), F32),
            pltpu.VMEM((2, 16, 128), F32),
            pltpu.VMEM((512, 384), BF16),
            pltpu.VMEM((16, 16, 384), BF16),
            pltpu.VMEM((2, 176, 384), BF16),
            pltpu.VMEM((3, 8, 128), F32),
            pltpu.VMEM((4, 8, 128), F32),
            pltpu.VMEM((16, 8, 128), F32),
            pltpu.VMEM((64, 8, 128), F32),
            pltpu.VMEM((2, 128, KEYS), BF16),
            pltpu.VMEM((2, 8, 128), F32),
            pltpu.VMEM((2, 8, 128), F32),
            pltpu.VMEM((5, 8, 128), F32),
            pltpu.VMEM((24, 8, 128), F32),
            dma((5,)),
            dma((3,)),
            dma((1,)),
            dma((1,)),
            dma((1,)),
            dma((3,)),
            dma((1,)),
            dma((1,)),
            dma((3,)),
            dma((4,)),
            dma((2,)),
            dma((2,)),
            dma((3,)),
            dma((4,)),
            dma((2,)),
            dma((1,)),
            dma((1,)),
        ],
        compiler_params=pltpu.CompilerParams(
            collective_id=0, has_side_effects=True, vmem_limit_bytes=32 * 2**20
        ),
    )(*pinned)
    return pl.pallas_call(
        finish,
        out_shape=(out, out, out, out),
        in_specs=[vmem] * 6,
        out_specs=(hbm,) * 4,
        scratch_shapes=[pltpu.VMEM((3, TOKENS, HEADS * DIM), F32), dma((13,))],
        compiler_params=pltpu.CompilerParams(vmem_limit_bytes=16 * 2**20),
    )(*parts)


def solution(mesh):
    spec = P("seq", "rep")
    return jax.shard_map(
        body,
        mesh=mesh,
        in_specs=(spec, spec, spec, spec, P(None, "rep")),
        out_specs=(spec, spec, spec, spec),
        check_vma=False,
    )
```

```python
import jax
import jax.numpy as jnp
from jax import lax
from jax.experimental import pallas as pl
from jax.experimental.pallas import tpu as pltpu
from jax.sharding import PartitionSpec as P

HEADS = 2
KEYS = 512
DIM = 128
TOKENS = 1024
BLOCK = 128
RATES = (8, 32, 128)
FACTOR = DIM**-0.5
MESH = pl.DeviceIdType.MESH
F32 = jnp.float32
BF16 = jnp.bfloat16


def dot(a, b, dims):
    return lax.dot_general(a, b, (dims, ((), ())), preferred_element_type=F32)


def nn(a, b):
    return dot(a, b, ((1,), (0,)))


def nt(a, b):
    return dot(a, b, ((1,), (1,)))


def tn(a, b):
    return dot(a, b, ((0,), (0,)))


def split3(a):
    high = a.astype(BF16)
    rest = a - high.astype(F32)
    middle = rest.astype(BF16)
    low = (rest - middle.astype(F32)).astype(BF16)
    return jnp.concatenate([high.astype(F32), middle.astype(F32), low.astype(F32)], 0).astype(BF16)


def join3(a):
    rows = a.shape[0] // 3
    return a[:rows] + a[rows : 2 * rows] + a[2 * rows :]


def select_rows(stats, chooser):
    return join3(nn(split3(stats), chooser))


def select_rows_nt(stats, chooser):
    return join3(nt(split3(stats), chooser))


def iota(shape, dim):
    return lax.broadcasted_iota(jnp.int32, shape, dim)


def kernel(
    offsets_hbm, query_hbm, keys_hbm, values_hbm, dout_hbm,
    att_out, dq_out, dk_out, dv_out, spread, stack_out,
    offsets, query, keys, values, dout,
    small, wide3, sel, sel2, sel3, powers0, products0, shares, weighted0, stat0, logs,
    pack1, pack2, pack3, work, in3, power_work, product_work, stat_work, weighted_work,
    stat_send, send2, send3, back_stat1, back_rows1, back2, back3, grad_work, grad_send3, stack,
    tiles, tiles1, tiles2, tiles3, shared, swap_send, swap1, swap2, swap3,
    load_sem, send_in, send_back, send_back1, send_rows1, send_stat, send_grad, send_grad1,
    recv_in, recv_back, recv_back1, recv_rows1, recv_stat, recv_grad, recv_grad1, send_swap, recv_swap,
):
    me = lax.axis_index("seq")
    y = lax.rem(me, 4)
    z = lax.rem(lax.div(me, 4), 4)
    x = lax.div(me, 16)
    place = lax.rem(me, 16)
    plane = me - place
    group = me - y
    core = lax.rem(lax.axis_index("rep"), 2)
    worker1 = (core, 2 + core)
    worker2 = (5 + core, 9 + core)
    worker3 = (7 - 3 * core, 11 - 3 * core)
    is1 = (y == worker1[0]) | (y == worker1[1])
    is2 = (place == worker2[0]) | (place == worker2[1])
    is3 = (place == worker3[0]) | (place == worker3[1])
    head12 = jnp.where((is1 & (y == worker1[0])) | (is2 & (place == worker2[0])), 0, 1)
    head3 = jnp.where(place == worker3[0], 0, 1)
    one2 = jnp.where(is2, 1, 0)
    one3 = jnp.where(is3, 1, 0)

    load_offsets = pltpu.make_async_copy(offsets_hbm, offsets, load_sem.at[4])
    load_offsets.start()
    loads = []
    for i, (source, held) in enumerate(
        ((keys_hbm, keys), (values_hbm, values), (query_hbm, query), (dout_hbm, dout))
    ):
        loads.append(pltpu.make_async_copy(source, held, load_sem.at[i]))
        loads[-1].start()

    barrier = pltpu.get_barrier_semaphore()

    def greet(device):
        pl.semaphore_signal(barrier, inc=1, device_id={"seq": device}, device_id_type=MESH)

    @pl.when(is3)
    def _():
        def step(i, carry):
            greet(lax.rem(me + i, 64))
            return carry

        lax.fori_loop(1, 64, step, 0)

    @pl.when(is2)
    def _():
        def step(i, carry):
            greet(plane + lax.rem(place + i, 16))
            return carry

        lax.fori_loop(1, 16, step, 0)

    for spot in worker2 + worker3:
        @pl.when(place != spot)
        def _(spot=spot):
            greet(plane + spot)

    for i in range(1, 4):
        greet(group + lax.rem(y + i, 4))

    load_offsets.wait()
    row = iota((48, 1), 0)
    for head in range(HEADS):
        off = [offsets[head, level] for level in range(3)]
        for part in range(4):
            target = jnp.where(
                row < 32,
                row * RATES[0] + off[0],
                jnp.where(
                    row < 40, (row - 32) * RATES[1] + off[1], (row - 40 - 2 * part) * RATES[2] + off[2]
                ),
            )
            small[head, part] = jnp.where(iota((48, 256), 1) == target, 1.0, 0.0).astype(BF16)
    for pair, sources in enumerate(((keys, values), (query, dout))):
        for load in loads[2 * pair : 2 * pair + 2]:
            load.wait()
        wide = slice(256 * pair, 256 * pair + 256)
        for head in range(HEADS):
            lanes = slice(DIM * head, DIM * head + DIM)
            pieces = []
            for part in range(4):
                rows = slice(256 * part, 256 * part + 256)
                both = jnp.concatenate([source[rows, lanes] for source in sources], 1)
                pieces.append(nn(small[head, part], both))
                pack1[head, 32 * part : 32 * part + 32, wide] = pieces[part][0:32].astype(BF16)
            pack2[head, :, wide] = jnp.concatenate([piece[32:40] for piece in pieces], 0).astype(BF16)
            wide3[head, 8 * pair : 8 * pair + 8] = (
                (pieces[0][40:48] + pieces[1][40:48]) + (pieces[2][40:48] + pieces[3][40:48])
            )
    for head in range(HEADS):
        pack3[head] = wide3[head].astype(BF16)

    pl.semaphore_wait(barrier, 3 + (2 - one2) + (8 - one3) + 15 * one3 + 15 * one2)

    def remote(src, dst, send_sem, recv_sem, device):
        return pltpu.make_async_remote_copy(
            src_ref=src, dst_ref=dst, send_sem=send_sem, recv_sem=recv_sem,
            device_id={"seq": device}, device_id_type=MESH,
        )

    def send(src, dst, send_sem, recv_sem, device):
        copy = remote(src, dst, send_sem, recv_sem, device)

        @pl.when(device != me)
        def _():
            copy.start()

    def arrived(ref, sem):
        pltpu.make_async_copy(ref, ref, sem).wait()

    mine1 = pl.ds(pl.multiple_of(128 * y, 128), 128)
    mine2 = pl.ds(pl.multiple_of(32 * place, 32), 32)
    for head in range(HEADS):
        send(pack1.at[head, :, 0:384], work.at[mine1, 0:384], send_in.at[0], recv_in.at[0],
             group + worker1[head])
    for block in range(4):
        for head in range(HEADS):
            send(pack3.at[head], in3.at[me], send_in.at[2], recv_in.at[2],
                 16 * block + worker3[head])
    for head in range(HEADS):
        send(pack2.at[head], work.at[mine2], send_in.at[1], recv_in.at[1],
             plane + worker2[head])

    for head in range(HEADS):
        send(pack1.at[head, :, 384:512], work.at[mine1, 384:512], send_in.at[3], recv_in.at[3],
             group + worker1[head])

    @pl.when(is1)
    def _():
        work[mine1] = pack1[head12]

    @pl.when(is2)
    def _():
        work[mine2] = pack2[head12]

    @pl.when(is3)
    def _():
        in3[me] = pack3[head3]

    def unit_refs(unit):
        head, segment = unit // 2, unit % 2
        return head, segment, pl.ds(DIM * head, DIM)

    def forward0(unit):
        head, segment, lanes = unit_refs(unit)
        rows = pl.ds(KEYS * segment, KEYS)
        key, value = keys[rows, lanes], values[rows, lanes]
        for chunk in range(2):
            part = pl.ds(KEYS * segment + 256 * chunk, 256)
            scores = nt(key, query[part, lanes]) * FACTOR
            row_max = jnp.max(scores, 0, keepdims=True)
            powers = jnp.exp(scores - row_max)
            powers0[unit, :, 256 * chunk : 256 * chunk + 256] = powers
            weights = powers.astype(BF16)
            weighted0[head, :, part] = tn(value, weights)
            products = nt(value, dout[part, lanes])
            products0[unit, :, 256 * chunk : 256 * chunk + 256] = products
            stat0[head, 0:1, part] = row_max
            stat0[head, 1:2, part] = jnp.sum(powers, 0, keepdims=True)
            stat0[head, 2:3, part] = jnp.sum(weights.astype(F32) * products, 0, keepdims=True)

    stat0[...] = jnp.zeros_like(stat0)
    for unit in range(4):
        forward0(unit)
    bases = (0, 32 * y, 8 * place)

    def target(index, off):
        return jnp.where(
            index < 128,
            index * RATES[0] + off[0],
            jnp.where(
                index < 160, (index - 128) * RATES[1] + off[1], (index - 160) * RATES[2] + off[2]
            ),
        )

    for head in range(HEADS):
        off = [offsets[head, level] for level in range(3)]
        sel[head] = jnp.where(
            iota((256, TOKENS), 1) == target(iota((256, 1), 0), off), 1.0, 0.0
        ).astype(BF16)
        row = iota((128, 1), 0)
        for ref, level in ((sel2, 1), (sel3, 2)):
            wanted = (row - bases[level]) * RATES[level] + off[level]
            ref[head] = jnp.where(iota((128, TOKENS), 1) == wanted, 1.0, 0.0).astype(BF16)

    for head in range(HEADS):
        for level, chooser in enumerate((sel[head, 0:128], sel2[head], sel3[head])):
            tiles[level, 3 * head : 3 * head + 3] = select_rows_nt(stat0[head], chooser)[0:3]
    for level in range(3):
        tiles[level, 6:8] = jnp.zeros((2, BLOCK), F32)
    for block in range(4):
        for head in range(HEADS):
            send(tiles.at[2], tiles3.at[me], send_stat.at[2], recv_stat.at[2],
                 16 * block + worker3[head])
    for head in range(HEADS):
        send(tiles.at[1], tiles2.at[place], send_stat.at[1], recv_stat.at[1],
             plane + worker2[head])
    for head in range(HEADS):
        send(tiles.at[0], tiles1.at[y], send_stat.at[0], recv_stat.at[0],
             group + worker1[head])

    @pl.when(is1)
    def _():
        tiles1[y] = tiles[0]

    @pl.when(is2)
    def _():
        tiles2[place] = tiles[1]

    @pl.when(is3)
    def _():
        tiles3[me] = tiles[2]

    worker_head = jnp.where(is3, head3, head12)
    off1, off2, off3 = (
        jnp.where(worker_head == 0, offsets[0, level], offsets[1, level]) for level in range(3)
    )
    column = iota((1, KEYS), 1)
    row = iota((BLOCK, 1), 0)
    own_position = jnp.where(
        is1, column * RATES[0] + off1, jnp.where(is2, column * RATES[1] + off2, column * RATES[2] + off3)
    )
    shared[0] = jnp.where(
        column * RATES[0] + off1 == row * RATES[1] + off2, 1.0, 0.0
    ).astype(BF16)
    in_plane = own_position + jnp.where(is1, 4 * TOKENS * z, 0)
    shared[1] = jnp.where(in_plane == row * RATES[2] + off3, 1.0, 0.0).astype(BF16)
    members = [
        lax.rem(own_position, rate) == off for rate, off in zip(RATES, (off1, off2, off3))
    ]

    def merge(items):
        peak = items[0][0]
        for item in items[1:]:
            peak = jnp.maximum(peak, item[0])
        factors = [jnp.exp(item[0] - peak) for item in items]
        total = factors[0] * items[0][1]
        product = factors[0] * items[0][2]
        for factor, item in zip(factors[1:], items[1:]):
            total += factor * item[1]
            product += factor * item[2]
        return peak, total, product

    def of_level(rows, member):
        return jnp.where(member, rows[0:1], -jnp.inf), rows[1:2], rows[2:3]

    def whole_powers():
        for chunk in range(2):
            part = slice(256 * chunk, 256 * chunk + 256)
            scores = nt(work[:, 0:128], work[part, 256:384]) * FACTOR
            row_max = jnp.max(scores, 0, keepdims=True)
            powers = jnp.exp(scores - row_max)
            power_work[:, part] = powers
            stat_work[0:1, part] = row_max
            stat_work[1:2, part] = jnp.sum(powers, 0, keepdims=True)

    def whole_products():
        for chunk in range(2):
            part = slice(256 * chunk, 256 * chunk + 256)
            products = nt(work[:, 128:256], work[part, 384:512])
            product_work[:, part] = products
            weights = power_work[:, part].astype(BF16)
            stat_work[2:3, part] = jnp.sum(weights.astype(F32) * products, 0, keepdims=True)

    def whole_weighted():
        for chunk in range(2):
            part = slice(256 * chunk, 256 * chunk + 256)
            weighted_work[part] = tn(power_work[:, part].astype(BF16), work[:, 128:256])

    def whole_backward(log_row, delta_row):
        grad_k = jnp.zeros((KEYS, DIM), F32)
        grad_v = jnp.zeros((KEYS, DIM), F32)
        for chunk in range(2):
            part = slice(256 * chunk, 256 * chunk + 256)
            log_part, delta_part = log_row[:, part], delta_row[:, part]
            probs = power_work[:, part] * jnp.exp(stat_work[0:1, part] - log_part)
            low = (probs * (product_work[:, part] - delta_part)).astype(BF16)
            grad_work[part, 0:128] = (FACTOR * tn(low, work[:, 0:128])).astype(BF16)
            grad_k += nn(low, work[part, 256:384])
            grad_v += nn(probs.astype(BF16), work[part, 384:512])
        grad_work[:, 128:256] = (FACTOR * grad_k).astype(BF16)
        grad_work[:, 256:384] = grad_v.astype(BF16)

    rows3 = pl.ds(pl.multiple_of(128 * x, 128), 128)

    def block_forward():
        scores = nt(work[:, 0:128], work[rows3, 256:384]) * FACTOR
        row_max = jnp.max(scores, 0, keepdims=True)
        powers = jnp.exp(scores - row_max)
        weights = powers.astype(BF16)
        products = nt(work[:, 128:256], work[rows3, 384:512])
        power_work[:, 0:128] = powers
        product_work[:, 0:128] = products
        stats = jnp.concatenate(
            [
                row_max,
                jnp.sum(powers, 0, keepdims=True),
                jnp.sum(weights.astype(F32) * products, 0, keepdims=True),
                jnp.zeros((5, BLOCK), F32),
            ],
            0,
        )
        stat_work[:, 0:128] = stats

    def block_backward(log_all, delta_all, log_own, delta_own):
        k_all, q_all, d_all = work[:, 0:128], work[:, 256:384], work[:, 384:512]
        k_own, v_own = work[rows3, 0:128], work[rows3, 128:256]
        probs = power_work[:, 0:128] * jnp.exp(stat_work[0:1, 0:128] - log_own)
        low = (probs * (product_work[:, 0:128] - delta_own)).astype(BF16)
        grad_q = FACTOR * tn(low, k_all)
        probs = jnp.exp(nt(k_own, q_all) * FACTOR - log_all)
        low = (probs * (nt(v_own, d_all) - delta_all)).astype(BF16)
        grad_k = FACTOR * nn(low, q_all)
        grad_v = nn(probs.astype(BF16), d_all)
        return jnp.concatenate([grad_q, grad_k, grad_v], 1)

    def rows_of(ref, index, count):
        return ref.at[pl.ds(pl.multiple_of(count * index, count), count)]

    def returns(src1, dst1, sem1, recv1, src2, dst2, src3, dst3, sems, recv):
        def each(src, dst, sem, recv_sem, device):
            remote(src, dst, sem.at[0], recv_sem, device).start()

        if src1 is not None:
            @pl.when(is1)
            def _():
                for i in range(1, 4):
                    other = lax.rem(y + i, 4)
                    each(src1(other), dst1(head12), sem1, recv1.at[head12], group + other)

        if src2 is not None:
            @pl.when(is2)
            def _():
                def step(i, carry):
                    other = lax.rem(place + i, 16)
                    each(src2(other), dst2(head12), sems, recv.at[head12], plane + other)
                    return carry

                lax.fori_loop(1, 16, step, 0)

            @pl.when(is3)
            def _():
                def step(i, carry):
                    other = lax.rem(place + i, 16)
                    each(src3(other), dst3(head3), sems, recv.at[2 + head3], plane + other)
                    return carry

                lax.fori_loop(1, 16, step, 0)

    def back():
        returns(
            lambda i: stat_send.at[i], lambda h: back_stat1.at[h], send_back1, recv_back1,
            lambda i: send2.at[i], lambda h: back2.at[h],
            lambda i: send3.at[i], lambda h: back3.at[h], send_back, recv_back,
        )
        returns(
            lambda i: rows_of(weighted_work, i, 128), lambda h: back_rows1.at[h], send_rows1, recv_rows1,
            None, None, None, None, None, None,
        )

    def grads_back():
        returns(
            lambda i: rows_of(grad_work, i, 128), lambda h: stack.at[h, pl.ds(0, 128)], send_grad1, recv_grad1,
            lambda i: rows_of(grad_work, i, 32), lambda h: stack.at[h, pl.ds(128, 32)],
            lambda i: grad_send3.at[i], lambda h: stack.at[h, pl.ds(160, 16)], send_grad, recv_grad,
        )

    def returned1(dst, recv):
        for head in range(HEADS):
            @pl.when(y != worker1[head])
            def _(head=head):
                arrived(dst(head), recv.at[head])

    def returned23(dst2, dst3, recv):
        for head in range(HEADS):
            @pl.when(place != worker2[head])
            def _(head=head):
                arrived(dst2(head), recv.at[head])

            @pl.when(place != worker3[head])
            def _(head=head):
                arrived(dst3(head), recv.at[2 + head])

    @pl.when(is1)
    def _():
        arrived(work.at[pl.ds(0, 384), pl.ds(0, 384)], recv_in.at[0])

    @pl.when(is2)
    def _():
        arrived(work.at[pl.ds(0, 480)], recv_in.at[1])

    @pl.when(is3)
    def _():
        arrived(in3.at[pl.ds(0, 63)], recv_in.at[2])
        both = in3[...].astype(F32)
        work[:, 0:256] = both[:, 0:8].reshape(KEYS, 256).astype(BF16)
        work[:, 256:512] = both[:, 8:16].reshape(KEYS, 256).astype(BF16)
        block_forward()

    @pl.when(is1 | is2)
    def _():
        stat_work[...] = jnp.zeros_like(stat_work)
        whole_powers()

        @pl.when(is1)
        def _():
            arrived(work.at[pl.ds(0, 384), pl.ds(384, 128)], recv_in.at[3])

        whole_products()
        for i in range(4):
            stat_send[i] = stat_work[:, 128 * i : 128 * i + 128]

    def exchange():
        def each(src, dst, device):
            remote(src, dst, send_swap.at[0], recv_swap.at[0], device).start()

        @pl.when(is1)
        def _():
            for block in range(4):
                device = 16 * block + jnp.where(head12 == 0, worker3[0], worker3[1])
                each(swap_send.at[1], swap3.at[4 * x + z], device)
            device = plane + jnp.where(head12 == 0, worker2[0], worker2[1])
            each(swap_send.at[0], swap2.at[z], device)

        @pl.when(is2)
        def _():
            for block in range(4):
                device = 16 * block + jnp.where(head12 == 0, worker3[0], worker3[1])
                each(swap_send.at[1], swap3.at[16 + x], device)
            for block in range(4):
                device = plane + 4 * block + jnp.where(head12 == 0, worker1[0], worker1[1])
                each(stat_send.at[block], swap1.at[0], device)

        @pl.when(is3)
        def _():
            for i in range(1, 4):
                device = 16 * lax.rem(x + i, 4) + place
                each(swap_send.at[0], swap3.at[20 + x], device)
            for block in range(4):
                device = plane + 4 * block + jnp.where(head3 == 0, worker1[0], worker1[1])
                each(swap_send.at[0], swap1.at[1], device)
            device = plane + jnp.where(head3 == 0, worker2[0], worker2[1])
            each(swap_send.at[0], swap2.at[4], device)

    @pl.when(is1)
    def _():
        swap_send[0] = select_rows_nt(stat_work[...], shared[0])

    @pl.when(is1 | is2)
    def _():
        swap_send[1] = select_rows_nt(stat_work[...], shared[1])

    @pl.when(is3)
    def _():
        swap_send[0] = stat_work[:, 0:128]
        swap3[20 + x] = stat_work[:, 0:128]

    exchange()

    @pl.when(is1 | is2)
    def _():
        whole_weighted()

        @pl.when(is2)
        def _():
            for i in range(16):
                send2[i, 0:32] = weighted_work[32 * i : 32 * i + 32]
                send2[i, 32:40] = stat_send[i // 4]
            back2[head12] = send2[place]

        @pl.when(is1)
        def _():
            back_stat1[head12] = stat_send[y]
            back_rows1[head12] = weighted_work[mine1]

    @pl.when(is3)
    def _():
        weighted = tn(power_work[:, 0:128].astype(BF16), work[:, 128:256])
        for i in range(16):
            send3[i] = jnp.concatenate([weighted[8 * i : 8 * i + 8], stat_work[:, 0:128]], 0)
        back3[head3] = send3[place]

    back()
    for head in range(HEADS):
        att_out[:, DIM * head : DIM * head + DIM] = weighted0[head].T
    for head in range(HEADS):
        off = [offsets[head, level] for level in range(3)]
        spread[head] = jnp.where(
            iota((TOKENS, 256), 0) == target(iota((1, 256), 1), off), 1.0, 0.0
        ).astype(BF16)

    def below_rows(blocks, head):
        rows = jnp.concatenate(blocks, 1)
        return [jnp.where(head == 0, rows[i : i + 1], rows[3 + i : 4 + i]) for i in range(3)]

    def final_rows(items):
        peak, total, product = merge(items)
        return peak + jnp.log(total), product / total

    def blocks_of(row):
        return [row[:, i : i + BLOCK] for i in range(0, KEYS, BLOCK)]

    def pick(rows, block):
        chosen = rows[0]
        for i in range(1, len(rows)):
            chosen = jnp.where(block == i, rows[i], chosen)
        return chosen

    @pl.when(is2)
    def _():
        arrived(tiles2.at[pl.ds(0, 15)], recv_stat.at[1])
        arrived(swap2, recv_swap.at[0])
        for i in range(4):
            tiles1[i] = jnp.sum(tiles2[4 * i : 4 * i + 4], 0)

    @pl.when(is1)
    def _():
        arrived(tiles1.at[pl.ds(0, 3)], recv_stat.at[0])
        arrived(swap1, recv_swap.at[0])

    @pl.when(is1 | is2)
    def _():
        below = below_rows([tiles1[i] for i in range(4)], head12)
        own = [stat_work[i : i + 1] for i in range(3)]
        lacking = jnp.where(
            is1, select_rows(swap1[0], shared[0]), jnp.concatenate([swap2[i] for i in range(4)], 1)
        )
        member = (is1 & members[1]) | (is2 & members[0])
        level3 = select_rows(jnp.where(is1, swap1[1], swap2[4]), shared[1])
        whole_backward(
            *final_rows([below, own, of_level(lacking, member), of_level(level3, members[2])])
        )

        @pl.when(is2)
        def _():
            stack[head12, 128:160] = grad_work[mine2]

        @pl.when(is1)
        def _():
            stack[head12, 0:128] = grad_work[mine1]

    @pl.when(is3)
    def _():
        arrived(tiles3.at[pl.ds(0, 63)], recv_stat.at[2])
        arrived(swap3.at[pl.ds(0, 23)], recv_swap.at[0])
        below = below_rows([jnp.sum(tiles3[16 * i : 16 * i + 16], 0) for i in range(4)], head3)
        own = jnp.concatenate([swap3[20 + i] for i in range(4)], 1)
        level1 = jnp.concatenate([jnp.sum(swap3[4 * i : 4 * i + 4], 0) for i in range(4)], 1)
        level2 = jnp.concatenate([swap3[16 + i] for i in range(4)], 1)
        log_row, delta_row = final_rows(
            [
                below,
                [own[i : i + 1] for i in range(3)],
                of_level(level1, members[0]),
                of_level(level2, members[1]),
            ]
        )
        grads = block_backward(
            log_row, delta_row, pick(blocks_of(log_row), x), pick(blocks_of(delta_row), x)
        )
        for i in range(16):
            tile = jnp.concatenate([grads[8 * i : 8 * i + 8], jnp.zeros((8, 3 * DIM), F32)], 0)
            grad_send3[i] = tile.astype(BF16)
        stack[head3, 160:176] = grad_send3[place]

    grads_back()

    returned1(lambda h: back_stat1.at[h], recv_back1)
    returned23(lambda h: back2.at[h], lambda h: back3.at[h], recv_back)
    position = iota((1, TOKENS), 1)
    for head in range(HEADS):
        found = (
            select_rows(back_stat1[head], sel[head, 0:128]),
            select_rows(back2[head, 32:40], sel2[head]),
            select_rows(back3[head, 8:16], sel3[head]),
        )
        items = [[stat0[head, i : i + 1] for i in range(3)]]
        for level in range(3):
            member = lax.rem(position, RATES[level]) == offsets[head, level]
            items.append(of_level(found[level], member))
        peak, total, product = merge(items)
        inverse = 1.0 / total
        logs[head] = jnp.concatenate(
            [peak + jnp.log(total), product * inverse, jnp.zeros((6, TOKENS), F32)], 0
        )
        shares[head] = jnp.concatenate(
            [jnp.exp(item[0] - peak) * inverse for item in items] + [jnp.zeros((4, TOKENS), F32)], 0
        )

    def backward0(unit):
        head, segment, lanes = unit_refs(unit)
        rows = pl.ds(KEYS * segment, KEYS)
        key = keys[rows, lanes]
        grad_k = jnp.zeros((KEYS, DIM), F32)
        grad_v = jnp.zeros((KEYS, DIM), F32)
        for chunk in range(2):
            part = pl.ds(KEYS * segment + 256 * chunk, 256)
            rescale = jnp.exp(stat0[head, 0:1, part] - logs[head, 0:1, part])
            probs = powers0[unit, :, 256 * chunk : 256 * chunk + 256] * rescale
            grad_rows = dout[part, lanes]
            products = products0[unit, :, 256 * chunk : 256 * chunk + 256]
            low = (probs * (products - logs[head, 1:2, part])).astype(BF16)
            grad_k += nn(low, query[part, lanes])
            grad_v += nn(probs.astype(BF16), grad_rows)
            dq_out[part, lanes] = (FACTOR * tn(key, low)).T
        dk_out[rows, lanes] = FACTOR * grad_k
        dv_out[rows, lanes] = grad_v

    for unit in range(4):
        backward0(unit)

    returned1(lambda h: back_rows1.at[h], recv_rows1)
    for head in range(HEADS):
        lane_shares = select_rows_nt(shares[head], sel[head])
        lane = iota((1, 256), 1)
        share = jnp.where(
            lane < 128, lane_shares[1:2], jnp.where(lane < 160, lane_shares[2:3], lane_shares[3:4])
        )
        stacked = jnp.concatenate(
            [back_rows1[head], back2[head, 0:32], back3[head, 0:8], jnp.zeros((88, DIM), F32)], 0
        ) * jnp.concatenate([share, jnp.zeros((7, 256), F32)], 0).T[:, 0:1]
        high = stacked.astype(BF16)
        low = (stacked - high.astype(F32)).astype(BF16)
        added = nn(spread[head], jnp.concatenate([high, low], 1))
        lanes = slice(DIM * head, DIM * head + DIM)
        att_out[:, lanes] = (
            att_out[:, lanes] * shares[head].T[:, 0:1] + added[:, 0:DIM] + added[:, DIM : 2 * DIM]
        )

    keys_part, dout_part = pack1.at[:, :, pl.ds(0, 384)], pack1.at[:, :, pl.ds(384, 128)]
    for sems, refs in (
        (send_in, (keys_part, pack2, in3, dout_part)),
        (send_stat, (tiles1, tiles2, tiles3)),
    ):
        for level, (here, count) in enumerate(((is1, 2), (is2, 2), (is3, 8), (is1, 2))[: len(refs)]):
            @pl.when(here)
            def _(ref=refs[level], sem=sems.at[level], count=count):
                arrived(ref.at[pl.ds(0, count - 1)], sem)

            @pl.when(jnp.logical_not(here))
            def _(ref=refs[level], sem=sems.at[level], count=count):
                arrived(ref.at[pl.ds(0, count)], sem)

    @pl.when(is1)
    def _():
        arrived(swap3.at[pl.ds(0, 5)], send_swap.at[0])
        arrived(stat_send.at[pl.ds(0, 3)], send_back1.at[0])
        arrived(weighted_work.at[pl.ds(0, 384)], send_rows1.at[0])
        arrived(grad_work.at[pl.ds(0, 384)], send_grad1.at[0])

    @pl.when(is2)
    def _():
        arrived(swap3.at[pl.ds(0, 8)], send_swap.at[0])
        arrived(send2.at[pl.ds(0, 15)], send_back.at[0])
        arrived(grad_work.at[pl.ds(0, 480)], send_grad.at[0])

    @pl.when(is3)
    def _():
        arrived(swap3.at[pl.ds(0, 8)], send_swap.at[0])
        arrived(send3.at[pl.ds(0, 15)], send_back.at[0])
        arrived(grad_send3.at[pl.ds(0, 15)], send_grad.at[0])

    stack_out[:, 176:256] = jnp.zeros((2, 80, 3 * DIM), BF16)
    returned1(lambda h: stack.at[h, pl.ds(0, 128)], recv_grad1)
    returned23(
        lambda h: stack.at[h, pl.ds(128, 32)], lambda h: stack.at[h, pl.ds(160, 16)], recv_grad
    )
    stack_out[:, 0:176] = stack[...]


def finish(att, dq, dk, dv, spread, stack, att_out, dq_out, dk_out, dv_out, full, sems):
    first = pltpu.make_async_copy(att, att_out, sems.at[12])
    first.start()
    copies = [first]
    for part in range(4):
        rows = slice(256 * part, 256 * part + 256)
        for head in range(HEADS):
            lanes = slice(DIM * head, DIM * head + DIM)
            added = nn(spread[head, rows], stack[head])
            for i, ref in enumerate((dq, dk, dv)):
                full[i, rows, lanes] = ref[rows, lanes] + added[:, DIM * i : DIM * i + DIM]
        for i, out in enumerate((dq_out, dk_out, dv_out)):
            copies.append(
                pltpu.make_async_copy(full.at[i, rows], out.at[rows], sems.at[3 * part + i])
            )
            copies[-1].start()
    for copy in copies:
        copy.wait()


def body(query, keys, values, grad_out, offsets):
    vmem = pl.BlockSpec(memory_space=pltpu.VMEM)
    hbm = pl.BlockSpec(memory_space=pltpu.HBM)
    out = jax.ShapeDtypeStruct((TOKENS, HEADS * DIM), F32)
    dma = pltpu.SemaphoreType.DMA
    held = pltpu.VMEM((TOKENS, HEADS * DIM), BF16)
    pinned = [
        pltpu.with_memory_space_constraint(item, pltpu.HBM)
        for item in (offsets.T, query, keys, values, grad_out)
    ]
    parts = pl.pallas_call(
        kernel,
        out_shape=(
            out, out, out, out,
            jax.ShapeDtypeStruct((2, TOKENS, 256), BF16),
            jax.ShapeDtypeStruct((2, 256, 3 * DIM), BF16),
        ),
        in_specs=[hbm] * 5,
        out_specs=(vmem,) * 6,
        scratch_shapes=[
            pltpu.SMEM((HEADS, 3), jnp.int32),
            held, held, held, held,
            pltpu.VMEM((2, 4, 48, 256), BF16),
            pltpu.VMEM((2, 16, 256), F32),
            pltpu.VMEM((2, 256, TOKENS), BF16),
            pltpu.VMEM((2, 128, TOKENS), BF16),
            pltpu.VMEM((2, 128, TOKENS), BF16),
            pltpu.VMEM((4, KEYS, KEYS), F32),
            pltpu.VMEM((4, KEYS, KEYS), F32),
            pltpu.VMEM((2, 8, TOKENS), F32),
            pltpu.VMEM((2, DIM, TOKENS), F32),
            pltpu.VMEM((2, 8, TOKENS), F32),
            pltpu.VMEM((2, 8, TOKENS), F32),
            pltpu.VMEM((2, 128, 512), BF16),
            pltpu.VMEM((2, 32, 512), BF16),
            pltpu.VMEM((2, 16, 256), BF16),
            pltpu.VMEM((512, 512), BF16),
            pltpu.VMEM((64, 16, 256), BF16),
            pltpu.VMEM((512, 512), F32),
            pltpu.VMEM((512, 512), F32),
            pltpu.VMEM((8, 512), F32),
            pltpu.VMEM((512, 128), F32),
            pltpu.VMEM((4, 8, 128), F32),
            pltpu.VMEM((16, 40, 128), F32),
            pltpu.VMEM((16, 16, 128), F32),
            pltpu.VMEM((2, 8, 128), F32),
            pltpu.VMEM((2, 128, 128), F32),
            pltpu.VMEM((2, 40, 128), F32),
            pltpu.VMEM((2, 16, 128), F32),
            pltpu.VMEM((512, 384), BF16),
            pltpu.VMEM((16, 16, 384), BF16),
            pltpu.VMEM((2, 176, 384), BF16),
            pltpu.VMEM((3, 8, 128), F32),
            pltpu.VMEM((4, 8, 128), F32),
            pltpu.VMEM((16, 8, 128), F32),
            pltpu.VMEM((64, 8, 128), F32),
            pltpu.VMEM((2, 128, KEYS), BF16),
            pltpu.VMEM((2, 8, 128), F32),
            pltpu.VMEM((2, 8, 128), F32),
            pltpu.VMEM((5, 8, 128), F32),
            pltpu.VMEM((24, 8, 128), F32),
            dma((5,)),
            dma((4,)),
            dma((1,)),
            dma((1,)),
            dma((1,)),
            dma((3,)),
            dma((1,)),
            dma((1,)),
            dma((4,)),
            dma((4,)),
            dma((2,)),
            dma((2,)),
            dma((3,)),
            dma((4,)),
            dma((2,)),
            dma((1,)),
            dma((1,)),
        ],
        compiler_params=pltpu.CompilerParams(
            collective_id=0, has_side_effects=True, vmem_limit_bytes=32 * 2**20
        ),
    )(*pinned)
    return pl.pallas_call(
        finish,
        out_shape=(out, out, out, out),
        in_specs=[vmem] * 6,
        out_specs=(hbm,) * 4,
        scratch_shapes=[pltpu.VMEM((3, TOKENS, HEADS * DIM), F32), dma((13,))],
        compiler_params=pltpu.CompilerParams(vmem_limit_bytes=16 * 2**20),
    )(*parts)


def solution(mesh):
    spec = P("seq", "rep")
    return jax.shard_map(
        body,
        mesh=mesh,
        in_specs=(spec, spec, spec, spec, P(None, "rep")),
        out_specs=(spec, spec, spec, spec),
        check_vma=False,
    )
```
